128 devices in a mesh: gz: 16 (over y, x), gy: 8 (over z, core).
Axes of the slice: x: 4, y: 4, z: 4, core: 2. Of those that a mesh axis runs over, the one named last changes fastest.
Arguments:
- density: float32 [256, 128, 1024], P('gz', 'gy'), may hold values from 0.1 to 10
Outputs:
- coefficients: float32 [256, 128, 1024], P('gz', 'gy')
The draws below stay inside these ranges and needn't reach their ends.
All inputs are finite; a program needn't handle non-finite values.
Results may differ from the reference program's by a relative error of at most 0.00002.
Values sent between devices are 32-bit elements; how exact they have to be, the bound alone decides.
No kernel may reach another device: no remote copies, remote signals or barrier semaphores. Data moves between devices by JAX's collectives and lax.ppermute only.
A program may use at most 192 MiB of HBM per device.

```python
import math
import jax
import jax.numpy as jnp
from jax import lax

NX = 1024
LEVELS = 4
NZ = 256
NY = 128


def block_levels(stream_key, shape, shards, smallest, high):
    gain = 1.0
    for position, shards_of in shards:
        heights = jax.random.uniform(jax.random.fold_in(jax.random.fold_in(stream_key, 6), position), (shards_of,), jnp.float32, smallest / len(shards), high / len(shards))
        gain = gain * jnp.repeat(jnp.exp(heights), shape[position] // shards_of).reshape((-1,) + (1,) * (len(shape) - 1 - position))
    return gain


def setup_inputs(seed: int = 0) -> dict:
    keys = jax.random.split(jax.random.key(seed), 2)
    density = jnp.clip(jnp.exp(math.log(10.0) - 4.6051702 * jax.random.uniform(keys[0], (NZ, NY, NX), jnp.float32) ** block_levels(keys[0], (NZ, NY, NX), ((0, 16), (1, 8)), -0.2, 0.2)), 0.1, 10.0)
    return dict(density=density)


predict_one = -1.586134342059924
update_one = -0.052980118572961
predict_two = 0.882911075530934
update_two = 0.443506852043971
norm_gain = 1.230174104914001


def cut(array, along, start, length):
    return lax.slice_in_dim(array, start, start + length, 1, along)


def split_pairs(array, along):
    total = array.shape[along]
    return lax.slice_in_dim(array, 0, total, 2, along), lax.slice_in_dim(array, 1, total, 2, along)


def join_pairs(smooth, detail, along):
    shape = list(smooth.shape)
    shape[along] = 2 * shape[along]
    return jnp.stack([smooth, detail], axis=along + 1).reshape(shape)


def lift_local(array, along):
    smooth, detail = split_pairs(array, along)
    pairs = smooth.shape[along]

    def ahead(values):
        return jnp.concatenate([cut(values, along, 1, pairs - 1), cut(values, along, pairs - 1, 1)], axis=along)

    def behind(values):
        return jnp.concatenate([cut(values, along, 0, 1), cut(values, along, 0, pairs - 1)], axis=along)

    detail = detail + predict_one * (smooth + ahead(smooth))
    smooth = smooth + update_one * (behind(detail) + detail)
    detail = detail + predict_two * (smooth + ahead(smooth))
    smooth = smooth + update_two * (behind(detail) + detail)
    return join_pairs(smooth / norm_gain, detail * (norm_gain / 2.0), along)


def decompose(cube, depth):
    for along in (2, 1, 0):
        cube = lift_local(cube, along)
    if depth > 1:
        coarse = decompose(cube[::2, ::2, ::2], depth - 1)
        cube = cube.at[::2, ::2, ::2].set(coarse)
    return cube


def reference(density):
    return decompose(density, LEVELS)
```

```python
import functools

import jax
import jax.numpy as jnp
import numpy as np
from jax import lax
from jax.experimental import pallas as pl
from jax.experimental.pallas import tpu as pltpu
from jax.sharding import PartitionSpec as P

A1 = -1.586134342059924
B1 = -0.052980118572961
A2 = 0.882911075530934
B2 = 0.443506852043971
GAIN = 1.230174104914001

WIDE = 1024
LANES = 128
TILES = WIDE // LANES
HIGH = lax.Precision.HIGHEST


def lift(rows, left, right, first, last, choose):
    p, q = left
    s_next, r = right
    smooth, detail = rows[0::2], rows[1::2]
    m = len(smooth)
    s_next = choose(last, smooth[-1], s_next)
    d1 = [detail[i] + A1 * (smooth[i] + (smooth[i + 1] if i + 1 < m else s_next)) for i in range(m)]
    d1_before = choose(first, d1[0], p + A1 * smooth[0])
    s1 = [smooth[i] + B1 * ((d1[i - 1] if i else d1_before) + d1[i]) for i in range(m)]
    s1_after = choose(last, s1[-1], r + B1 * d1[-1])
    d2 = [d1[i] + A2 * (s1[i] + (s1[i + 1] if i + 1 < m else s1_after)) for i in range(m)]
    d2_before = choose(first, d2[0], d1_before + A2 * (q + B1 * d1_before + s1[0]))
    s2 = [s1[i] + B2 * ((d2[i - 1] if i else d2_before) + d2[i]) for i in range(m)]
    return [v * (1.0 / GAIN) for v in s2], [v * (GAIN / 2.0) for v in d2]


def lift_alone(rows):
    zero = jnp.zeros_like(rows[0])
    return lift(rows, (zero, zero), (zero, zero), False, False, lambda c, a, b: a if c else b)[0]


def edges(rows):
    s, d = rows[0::2], rows[1::2]
    to_right = (d[-1] + A1 * s[-1], s[-1] + B1 * (d[-2] + A1 * (s[-2] + s[-1])))
    to_left = (s[0], s[0] + B1 * (d[0] + A1 * (s[0] + s[1])))
    return to_right, to_left


def own_left(to_left):
    s, r = to_left
    c2 = (B2 * A2 * B1 * A1 / GAIN) * s
    c1 = ((B1 * A1 + B2 * A1 + 3 * B2 * A2 * B1 * A1) / GAIN) * s + (B2 * A2 / GAIN) * r
    return c1 + A1 * c2, (1 + B1 * A1) * c2


def own_right(to_right):
    p, q = to_right
    c0 = ((B1 + B2 + 3 * B2 * A2 * B1) / GAIN) * p + (B2 * A2 / GAIN) * q
    c1 = (B2 * A2 * B1 / GAIN) * p
    return c0, c0 + B1 * (c1 + A1 * c0)


def add_pairs(a, b):
    return a[0] + b[0], a[1] + b[1]


def mix(flag, a, b):
    return jnp.where(flag, a, b)


def interleave(smooth, detail):
    return [v for pair in zip(smooth, detail) for v in pair]


def lane_factors(stride):
    lane = np.arange(WIDE)
    odd = (lane % (2 * stride)) == stride
    even = (lane % (2 * stride)) == 0
    table = np.zeros((16, WIDE), np.float64)
    for k, a in enumerate((A1, B1, A2, B2)):
        at = even if k % 2 else odd
        table[k] = np.where(at, a, 0.0)
        table[4 + k] = np.where(at, a, 0.0)
        if k % 2:
            table[k, 0] = 0.0
            table[4 + k, 0] = 2 * a
        else:
            table[k, WIDE - stride] = 2 * a
            table[4 + k, WIDE - stride] = 0.0
    table[8] = np.where(even, 1.0 / GAIN, np.where(odd, GAIN / 2.0, 1.0))
    return table.astype(np.float32)


def lift_lanes(v, table, stride):
    for k in range(4):
        before = pltpu.roll(v, stride, 1)
        after = pltpu.roll(v, WIDE - stride, 1)
        v = v + table[k : k + 1, :] * before + table[4 + k : 5 + k, :] * after
    return v * table[8:9, :]


def lane_id(shape):
    return lax.broadcasted_iota(jnp.int32, shape, len(shape) - 1)


def pack_two(a, b, even):
    return jnp.where(even, a, pltpu.roll(b, 1, 1))


def unpack_two(w):
    return w, pltpu.roll(w, LANES - 1, 1)


def gather_tiles(ref, at):
    return jnp.concatenate([ref[t, at, :] for t in range(TILES)], axis=1)


def tile(t):
    return slice(t * LANES, (t + 1) * LANES)


def along_x(table, x, out, pay_e, pay_o):
    def plane(z, carry):
        at = pl.ds(pl.multiple_of(z * 16, 16), 16)
        v = lift_lanes(x[at, :], table, 1)
        for t in range(TILES):
            out[t, at, :] = v[:, tile(t)]
        return carry

    lax.fori_loop(0, 16, plane, 0)
    flip = lax.axis_index("gy") % 2 == 1
    even = lane_id((8, LANES)) % 2 == 0
    for half in range(2):
        for t in range(TILES):
            lanes = pl.ds(t * LANES, LANES)
            rows = [out[t, pl.ds(half * 128 + y, 8, stride=16), :] for y in range(16)]
            to_right, to_left = edges(rows)
            next_right, next_left = edges(lift_alone(rows))
            going_right = to_right + (pack_two(*next_right, even),)
            going_left = to_left + (pack_two(*next_left, even),)
            for c in range(3):
                pay_e[c, pl.ds(half * 8, 8), lanes] = mix(flip, going_left[c], going_right[c])
                pay_o[c, pl.ds(half * 8, 8), lanes] = mix(flip, going_right[c], going_left[c])


def along_y(x, got_e, got_o, one, two, pay_e, pay_o):
    me = lax.axis_index("gy")
    first, last, flip = me == 0, me == lax.axis_size("gy") - 1, me % 2 == 1
    even = lane_id((8, LANES)) % 2 == 0
    for half in range(2):
        for t in range(TILES):
            lanes = pl.ds(t * LANES, LANES)
            rows = [x[t, pl.ds(half * 128 + y, 8, stride=16), :] for y in range(16)]
            e = [got_e[c, pl.ds(half * 8, 8), lanes] for c in range(3)]
            o = [got_o[c, pl.ds(half * 8, 8), lanes] for c in range(3)]
            left = [mix(flip, e[c], o[c]) for c in range(3)]
            right = [mix(flip, o[c], e[c]) for c in range(3)]
            to_right, to_left = edges(rows)
            smooth, detail = lift(rows, left[:2], right[:2], first, last, mix)
            for y, v in enumerate(interleave(smooth, detail)):
                one[t, pl.ds(half * 128 + y, 8, stride=16), :] = v
            left2 = add_pairs(unpack_two(left[2]), own_left(to_left))
            right2 = add_pairs(unpack_two(right[2]), own_right(to_right))
            smooth, detail = lift(smooth, left2, right2, first, last, mix)
            for y, v in enumerate(interleave(smooth, detail)):
                two[t, pl.ds(half * 64 + y, 8, stride=8), :] = v
    flip = lax.axis_index("gz") % 2 == 1
    for t in range(TILES):
        lanes = pl.ds(t * LANES, LANES)
        going_right, going_left = [None] * 6, [None] * 6
        for half in range(2):
            rows = [one[t, pl.ds(z * 16 + half * 8, 8), :] for z in range(16)]
            to_right, to_left = edges(rows)
            for c in range(2):
                going_right[2 * c + half] = to_right[c]
                going_left[2 * c + half] = to_left[c]
        rows = [two[t, pl.ds(z * 8, 8), :] for z in range(16)]
        to_right, to_left = edges(rows)
        next_right, next_left = edges(lift_alone(rows))
        going_right[4:] = pack_two(*to_right, even), pack_two(*next_right, even)
        going_left[4:] = pack_two(*to_left, even), pack_two(*next_left, even)
        for c in range(6):
            pay_e[c, :, lanes] = mix(flip, going_left[c], going_right[c])
            pay_o[c, :, lanes] = mix(flip, going_right[c], going_left[c])


def along_z(table2, table3, one, two, got_e, got_o, out, pay, fine, spread):
    me = lax.axis_index("gz")
    first, last, flip = me == 0, me == lax.axis_size("gz") - 1, me % 2 == 1
    for t in range(TILES):
        lanes = pl.ds(t * LANES, LANES)
        e = [got_e[c, :, lanes] for c in range(6)]
        o = [got_o[c, :, lanes] for c in range(6)]
        left = [mix(flip, e[c], o[c]) for c in range(6)]
        right = [mix(flip, o[c], e[c]) for c in range(6)]
        for half in range(2):
            rows = [one[t, pl.ds(z * 16 + half * 8, 8), :] for z in range(16)]
            smooth, detail = lift(rows, left[half:4:2], right[half:4:2], first, last, mix)
            for z, v in enumerate(interleave(smooth, detail)):
                out[pl.ds(z * 16 + half * 8, 8), lanes] = v
        rows = [two[t, pl.ds(z * 8, 8), :] for z in range(16)]
        to_right, to_left = edges(rows)
        smooth, _ = lift(rows, unpack_two(left[4]), unpack_two(right[4]), first, last, mix)
        left2 = add_pairs(unpack_two(left[5]), own_left(to_left))
        right2 = add_pairs(unpack_two(right[5]), own_right(to_right))
        smooth, detail = lift(smooth, left2, right2, first, last, mix)
        for z, v in enumerate(interleave(smooth, detail)):
            fine[t, pl.ds(z * 8, 8), :] = v
    row = lax.broadcasted_iota(jnp.int32, (16, LANES), 0)
    here = (row % 2 == 0) & (lane_id((16, LANES)) % 2 == 0)
    for z in range(8):
        v = lift_lanes(gather_tiles(fine, pl.ds(z * 8, 8)), table2, 2)
        for t in range(TILES):
            part = v[:, tile(t)]
            if z % 2 == 0:
                fine[t, pl.ds(z * 8, 8), :] = part
            spread[t, pl.ds(z * 16, 8, stride=2), :] = part
            at, lanes = pl.ds(z * 32, 16), pl.ds(t * LANES, LANES)
            out[at, lanes] = jnp.where(here, spread[t, pl.ds(z * 16, 16), :], out[at, lanes])
    lane = lane_id((4, WIDE))
    packed = None
    for z in range(4):
        v = lift_lanes(gather_tiles(fine, pl.ds(z * 16, 4, stride=2)), table3, 4)
        packed = jnp.where(lane % 4 == z, pltpu.roll(v, z, 1), packed) if z else v
    for to in range(pay.shape[0]):
        pay[to, pl.ds(0, 4), :] = packed[:, : WIDE // 2]
        pay[to, pl.ds(4, 4), :] = packed[:, WIDE // 2 :]


def coarse_y(weights, got, pay, held):
    me = lax.axis_index("gy")
    rows = got[...].reshape(64, WIDE // 2)
    held[...] = jnp.dot(weights[me], rows, precision=HIGH, preferred_element_type=jnp.float32)
    lane = lane_id((2, WIDE // 2))
    four = jnp.where(lane % 8 < 4, held[pl.ds(8, 2), :], pltpu.roll(held[pl.ds(10, 2), :], 4, 1))
    three = held[pl.ds(0, 8), :]
    for to in range(pay.shape[0]):
        pay[to, :, pl.ds(0, WIDE // 2)] = three
        for part in range(4):
            pay[to, pl.ds(2 * part, 2), pl.ds(WIDE // 2, LANES)] = four[:, tile(part)]


def coarse_z(table4, weights3, weights4, got, base, out, planes, three, four, spread, sem):
    loads = [pltpu.make_async_copy(base.at[4 * i], planes.at[i], sem.at[i]) for i in range(4)]
    for load in loads:
        load.start()
    me = lax.axis_index("gz")
    half = WIDE // 2
    g3 = jnp.dot(
        weights3[me], got[:, :, pl.ds(0, half)].reshape(128, half), precision=HIGH, preferred_element_type=jnp.float32
    )
    g4 = jnp.dot(
        weights4[me], got[:, :, pl.ds(half, LANES)].reshape(128, LANES), precision=HIGH, preferred_element_type=jnp.float32
    )
    sum3 = g3[0:32]
    for j in range(1, 4):
        sum3 = sum3 + pltpu.roll(g3[j * 32 : j * 32 + 32], half - j, 1)
    for o in range(4):
        for h in range(2):
            part = sum3[o * 8 + h * 4 : o * 8 + h * 4 + 4]
            for t in range(TILES // 2):
                three[h * (TILES // 2) + t, pl.ds(o * 4, 4), :] = part[:, tile(t)]
    for h in range(2):
        sum4 = g4[0:16] if h == 0 else pltpu.roll(g4[0:16], LANES - 4, 1)
        for j in range(1, 4):
            sum4 = sum4 + pltpu.roll(g4[j * 16 : j * 16 + 16], LANES - 4 * h - j, 1)
        for o in range(2):
            for part in range(4):
                at = o * 8 + part * 2
                four[pl.ds(o * 2, 2), pl.ds(h * half + part * LANES, LANES)] = sum4[at : at + 2]
    last = lift_lanes(four[...], table4, 8)
    lane = lane_id((2, LANES))
    for o in range(2):
        at = pl.ds(o * 8, 2, stride=2)
        for t in range(TILES):
            three[t, at, :] = jnp.where(lane % 8 == 0, last[o * 2 : o * 2 + 2, tile(t)], three[t, at, :])
    for load in loads:
        load.wait()
    row = lax.broadcasted_iota(jnp.int32, (16, LANES), 0)
    here = (row % 4 == 0) & (lane_id((16, LANES)) % 4 == 0)
    stores = []
    for i in range(4):
        for t in range(TILES):
            spread[t, pl.ds(i * 16, 4, stride=4), :] = three[t, pl.ds(i * 4, 4), :]
            lanes = pl.ds(t * LANES, LANES)
            planes[i, :, lanes] = jnp.where(here, spread[t, pl.ds(i * 16, 16), :], planes[i, :, lanes])
        stores.append(pltpu.make_async_copy(planes.at[i], out.at[4 * i], sem.at[i]))
        stores[-1].start()
    for store in stores:
        store.wait()


def two_levels(n):
    fixed = lambda c, a, b: a if c else b
    none = (0.0, 0.0)
    cells = list(np.eye(n))
    smooth, detail = lift(cells, none, none, True, True, fixed)
    upper = np.stack(interleave(smooth, detail))
    smooth, detail = lift(smooth, none, none, True, True, fixed)
    return upper, np.stack(interleave(smooth, detail))


def weights_y(devices):
    upper, lower = two_levels(4 * devices)
    out = np.zeros((devices, 16, devices, 2, 4), np.float64)
    for b in range(devices):
        for h in range(2):
            out[b, 4 * h : 4 * h + 4, :, h, :] = upper[4 * b : 4 * b + 4].reshape(4, devices, 4)
            out[b, 8 + 2 * h : 10 + 2 * h, :, h, :] = lower[2 * b : 2 * b + 2].reshape(2, devices, 4)
    return out.reshape(devices, 16, devices * 8).astype(np.float32)


def weights_z(devices):
    upper, lower = two_levels(4 * devices)
    w3 = np.zeros((devices, 4, 4, 8, devices, 8), np.float64)
    w4 = np.zeros((devices, 4, 2, 8, devices, 8), np.float64)
    for a in range(devices):
        u = upper[4 * a : 4 * a + 4].reshape(4, devices, 4)
        v = lower[2 * a : 2 * a + 2].reshape(2, devices, 4)
        for j in range(4):
            for r in range(8):
                w3[a, j, :, r, :, r] = u[:, :, j]
                w4[a, j, :, r, :, r] = v[:, :, j]
    return (
        w3.reshape(devices, 128, devices * 8).astype(np.float32),
        w4.reshape(devices, 64, devices * 8).astype(np.float32),
    )


def swap(values, axis, start):
    devices = lax.axis_size(axis)
    pairs = []
    for i in range(start, devices - 1, 2):
        pairs += [(i, i + 1), (i + 1, i)]
    return lax.ppermute(values, axis, pairs)


def f32(*shape):
    return jax.ShapeDtypeStruct(shape, jnp.float32)


def call(body, out, scratch=(), **more):
    return pl.pallas_call(
        body,
        out_shape=out,
        scratch_shapes=list(scratch),
        compiler_params=pltpu.CompilerParams(vmem_limit_bytes=24 * 1024 * 1024),
        **more,
    )


def per_device(density):
    planes, rows, cells = density.shape
    ny, nz = lax.axis_size("gy"), lax.axis_size("gz")
    tables = [jnp.asarray(lane_factors(s)) for s in (1, 2, 4, 8)]
    flat = density.reshape(planes * rows, cells)
    tiled = f32(TILES, planes * rows, LANES)
    payload = f32(3, 16, cells)
    x, pay_e, pay_o = call(along_x, [tiled, payload, payload])(tables[0], flat)
    got_e, got_o = swap(pay_e, "gy", 0), swap(pay_o, "gy", 1)
    payload = f32(6, 8, cells)
    one, two, pay_e, pay_o = call(along_y, [tiled, f32(TILES, planes * rows // 2, LANES), payload, payload])(
        x, got_e, got_o
    )
    got_e, got_o = swap(pay_e, "gz", 0), swap(pay_o, "gz", 1)
    base, pay = call(
        along_z,
        [f32(planes * rows, cells), f32(ny, 8, cells // 2)],
        [pltpu.VMEM((TILES, 64, LANES), jnp.float32), pltpu.VMEM((TILES, 128, LANES), jnp.float32)],
    )(tables[1], tables[2], one, two, got_e, got_o)
    got = lax.all_to_all(pay, "gy", 0, 0, tiled=True)
    pay = call(coarse_y, f32(nz, 8, cells // 2 + LANES), [pltpu.VMEM((16, cells // 2), jnp.float32)])(
        jnp.asarray(weights_y(ny)), got
    )
    got = lax.all_to_all(pay, "gz", 0, 0, tiled=True)
    w3, w4 = weights_z(nz)
    whole = pl.BlockSpec(memory_space=pltpu.VMEM)
    return call(
        coarse_z,
        f32(planes, rows, cells),
        [
            pltpu.VMEM((4, rows, cells), jnp.float32),
            pltpu.VMEM((TILES, 16, LANES), jnp.float32),
            pltpu.VMEM((4, cells), jnp.float32),
            pltpu.VMEM((TILES, 64, LANES), jnp.float32),
            pltpu.SemaphoreType.DMA((4,)),
        ],
        in_specs=[whole] * 4 + [pl.BlockSpec(memory_space=pl.ANY)],
        out_specs=pl.BlockSpec(memory_space=pl.ANY),
        input_output_aliases={4: 0},
    )(tables[3], jnp.asarray(w3), jnp.asarray(w4), got, base.reshape(planes, rows, cells))


def solution(mesh):
    return jax.shard_map(
        per_device, mesh=mesh, in_specs=(P("gz", "gy", None),), out_specs=P("gz", "gy", None), check_vma=False
    )
```

```python
import functools

import jax
import jax.numpy as jnp
import numpy as np
from jax import lax
from jax.experimental import pallas as pl
from jax.experimental.pallas import tpu as pltpu
from jax.sharding import PartitionSpec as P

A1 = -1.586134342059924
B1 = -0.052980118572961
A2 = 0.882911075530934
B2 = 0.443506852043971
GAIN = 1.230174104914001

WIDE = 1024
LANES = 128
TILES = WIDE // LANES
HIGH = lax.Precision.HIGHEST


def lift(rows, left, right, first, last, choose):
    p, q = left
    s_next, r = right
    smooth, detail = rows[0::2], rows[1::2]
    m = len(smooth)
    s_next = choose(last, smooth[-1], s_next)
    d1 = [detail[i] + A1 * (smooth[i] + (smooth[i + 1] if i + 1 < m else s_next)) for i in range(m)]
    d1_before = choose(first, d1[0], p + A1 * smooth[0])
    s1 = [smooth[i] + B1 * ((d1[i - 1] if i else d1_before) + d1[i]) for i in range(m)]
    s1_after = choose(last, s1[-1], r + B1 * d1[-1])
    d2 = [d1[i] + A2 * (s1[i] + (s1[i + 1] if i + 1 < m else s1_after)) for i in range(m)]
    d2_before = choose(first, d2[0], d1_before + A2 * (q + B1 * d1_before + s1[0]))
    s2 = [s1[i] + B2 * ((d2[i - 1] if i else d2_before) + d2[i]) for i in range(m)]
    return [v * (1.0 / GAIN) for v in s2], [v * (GAIN / 2.0) for v in d2]


def lift_alone(rows):
    zero = jnp.zeros_like(rows[0])
    return lift(rows, (zero, zero), (zero, zero), False, False, lambda c, a, b: a if c else b)[0]


def edges(rows):
    s, d = rows[0::2], rows[1::2]
    to_right = (d[-1] + A1 * s[-1], s[-1] + B1 * (d[-2] + A1 * (s[-2] + s[-1])))
    to_left = (s[0], s[0] + B1 * (d[0] + A1 * (s[0] + s[1])))
    return to_right, to_left


def own_left(to_left):
    s, r = to_left
    c2 = (B2 * A2 * B1 * A1 / GAIN) * s
    c1 = ((B1 * A1 + B2 * A1 + 3 * B2 * A2 * B1 * A1) / GAIN) * s + (B2 * A2 / GAIN) * r
    return c1 + A1 * c2, (1 + B1 * A1) * c2


def own_right(to_right):
    p, q = to_right
    c0 = ((B1 + B2 + 3 * B2 * A2 * B1) / GAIN) * p + (B2 * A2 / GAIN) * q
    c1 = (B2 * A2 * B1 / GAIN) * p
    return c0, c0 + B1 * (c1 + A1 * c0)


def add_pairs(a, b):
    return a[0] + b[0], a[1] + b[1]


def mix(flag, a, b):
    return jnp.where(flag, a, b)


def interleave(smooth, detail):
    return [v for pair in zip(smooth, detail) for v in pair]


def lane_factors(stride):
    run = np.arange(WIDE) // stride
    ends = run[-1]
    odd, even = run % 2 == 1, run % 2 == 0
    table = np.zeros((16, WIDE), np.float64)
    for k, a in enumerate((A1, B1, A2, B2)):
        at = even if k % 2 else odd
        closed = run == (0 if k % 2 else ends)
        before, after = (4 + k, k) if k % 2 else (k, 4 + k)
        table[before] = np.where(at, np.where(closed, 2 * a, a), 0.0)
        table[after] = np.where(at & ~closed, a, 0.0)
    table[8] = np.where(even, 1.0 / GAIN, GAIN / 2.0)
    return table.astype(np.float32)


def lift_lanes(v, table, stride):
    for k in range(4):
        before = pltpu.roll(v, stride, 1)
        after = pltpu.roll(v, WIDE - stride, 1)
        v = v + table[k : k + 1, :] * before + table[4 + k : 5 + k, :] * after
    return v * table[8:9, :]


def lane_id(shape):
    return lax.broadcasted_iota(jnp.int32, shape, len(shape) - 1)


def pack_two(a, b, even):
    return jnp.where(even, a, pltpu.roll(b, 1, 1))


def unpack_two(w):
    return w, pltpu.roll(w, LANES - 1, 1)


def gather_tiles(ref, at):
    return jnp.concatenate([ref[t, at, :] for t in range(TILES)], axis=1)


def tile(t):
    return slice(t * LANES, (t + 1) * LANES)


def times(count, body, unroll=1):
    def step(i, carry):
        body(i)
        return carry

    lax.fori_loop(0, count, step, 0, unroll=unroll)


def tile_lanes(t):
    return pl.ds(pl.multiple_of(t * LANES, LANES), LANES)


def lift_two(a, b, phase):
    lane = lane_id((a[0].shape[0], LANES))
    here = lane % (2 * phase) < phase
    count, reach = len(a), 2 * phase
    s = [jnp.where(here, x, pltpu.roll(y, phase, 1)) for x, y in zip(a, b)]
    d = [jnp.where(here, pltpu.roll(x, LANES - phase, 1), y) for x, y in zip(a, b)]

    def ahead(x):
        r = [pltpu.roll(w, LANES - reach, 1) for w in x]
        return [jnp.where(lane < LANES - reach, r[t], r[t + 1] if t + 1 < count else x[t]) for t in range(count)]

    def behind(x):
        r = [pltpu.roll(w, reach, 1) for w in x]
        return [jnp.where(lane >= reach, r[t], r[t - 1] if t else x[t]) for t in range(count)]

    d = [x + A1 * (y + z) for x, y, z in zip(d, s, ahead(s))]
    s = [x + B1 * (y + z) for x, y, z in zip(s, d, behind(d))]
    d = [x + A2 * (y + z) for x, y, z in zip(d, s, ahead(s))]
    s = [(x + B2 * (y + z)) * (1.0 / GAIN) for x, y, z in zip(s, d, behind(d))]
    return s, [x * (GAIN / 2.0) for x in d]


def separate(s, d, phase):
    here = lane_id(s[0].shape) % (2 * phase) < phase
    a = [jnp.where(here, x, pltpu.roll(y, phase, 1)) for x, y in zip(s, d)]
    b = [jnp.where(here, pltpu.roll(x, LANES - phase, 1), y) for x, y in zip(s, d)]
    return a, b


def tiles_of(ref, at):
    v = ref[at, :]
    return [v[:, tile(t)] for t in range(TILES)]


def put_tiles(ref, at, parts):
    for t, v in enumerate(parts):
        ref[at, tile(t)] = v


def along_x(weights3, weights4, density, out, pay_e, pay_o, own, pay, x, w3, w4, e1, e2, e3, sem):
    me = lax.axis_index("gy")
    part = x.shape[0] // 4
    loads = [
        pltpu.make_async_copy(density.at[pl.ds(k * part, part)], x.at[pl.ds(k * part, part)], sem.at[k])
        for k in (0, 2, 1, 3)
    ]
    loads.append(pltpu.make_async_copy(weights3.at[me], w3, sem.at[4]))
    loads.append(pltpu.make_async_copy(weights4.at[me], w4, sem.at[5]))
    for load in loads:
        load.start()

    def plane(i):
        z, y = i // 2, i % 2
        at = pl.multiple_of(z * 16 + y * 8, 8)
        far = pl.multiple_of(z * 16 + y * 8 + 128, 8)
        s, d = lift_two(tiles_of(x, pl.ds(at, 8)), tiles_of(x, pl.ds(far, 8)), 1)
        put_tiles(e1, pl.ds(at, 8), s)
        a, b = separate(s, d, 1)
        for t in range(TILES):
            out[t, pl.ds(at, 8), :] = a[t]
            out[t, pl.ds(far, 8), :] = b[t]

    loads[0].wait()
    loads[1].wait()
    times(8, plane, 4)
    loads[2].wait()
    loads[3].wait()
    times(8, lambda i: plane(i + 8), 4)

    def second(i):
        at = pl.multiple_of(i * 8, 8)
        s, _ = lift_two(tiles_of(e1, pl.ds(at, 8)), tiles_of(e1, pl.ds(at + 64, 8)), 2)
        put_tiles(e2, pl.ds(at, 8), s)

    times(8, second, 4)

    def third(i):
        at = pl.multiple_of(i * 8, 8)
        s, _ = lift_two(tiles_of(e2, pl.ds(at, 8)), tiles_of(e2, pl.ds(at + 32, 8)), 4)
        put_tiles(e3, pl.ds(at, 8), s)

    times(4, third, 4)
    loads[4].wait()
    loads[5].wait()
    flip = me % 2 == 1
    even = lane_id((8, LANES)) % 2 == 0
    three = jnp.dot(w3[...], e2[...], precision=HIGH, preferred_element_type=jnp.float32)
    own[...] = three[0:16]
    pay_e[3] = mix(flip, three[32:48], three[16:32])
    pay_o[3] = mix(flip, three[16:32], three[32:48])
    four = jnp.dot(w4[...], e3[...], precision=HIGH, preferred_element_type=jnp.float32)
    for to in range(pay.shape[0]):
        pay[to, :, 0:WIDE] = mix(to > me, three[48:56], three[56:64])
        pay[to, 0:4, WIDE:] = four[to * 4 : to * 4 + 4, : WIDE // 2]
        pay[to, 4:8, WIDE:] = four[to * 4 : to * 4 + 4, WIDE // 2 :]

    def column(t):
        lanes = tile_lanes(t)
        for half in range(2):
            rows = [out[t, pl.ds(half * 128 + y, 8, stride=16), :] for y in range(16)]
            to_right, to_left = edges(rows)
            next_right, next_left = edges(lift_alone(rows))
            going_right = to_right + (pack_two(*next_right, even),)
            going_left = to_left + (pack_two(*next_left, even),)
            for c in range(3):
                pay_e[c, pl.ds(half * 8, 8), lanes] = mix(flip, going_left[c], going_right[c])
                pay_o[c, pl.ds(half * 8, 8), lanes] = mix(flip, going_right[c], going_left[c])

    times(TILES, column, 2)


def along_y(near3, weights3, weights4, x, got_e, got_o, own, got, one, two, pay_e, pay_o, pay, n3, w3, w4, held3, held4, turned3, turned4, sem):
    mz = lax.axis_index("gz")
    loads = [
        pltpu.make_async_copy(near3, n3, sem.at[0]),
        pltpu.make_async_copy(weights3.at[mz], w3, sem.at[1]),
        pltpu.make_async_copy(weights4.at[mz], w4, sem.at[2]),
    ]
    for load in loads:
        load.start()
    me = lax.axis_index("gy")
    first, last, flip = me == 0, me == lax.axis_size("gy") - 1, me % 2 == 1
    even = lane_id((8, LANES)) % 2 == 0

    def column(t):
        lanes = tile_lanes(t)
        for half in range(2):
            rows = [x[t, pl.ds(half * 128 + y, 8, stride=16), :] for y in range(16)]
            e = [got_e[c, pl.ds(half * 8, 8), lanes] for c in range(3)]
            o = [got_o[c, pl.ds(half * 8, 8), lanes] for c in range(3)]
            left = [mix(flip, e[c], o[c]) for c in range(3)]
            right = [mix(flip, o[c], e[c]) for c in range(3)]
            to_right, to_left = edges(rows)
            smooth, detail = lift(rows, left[:2], right[:2], first, last, mix)
            for y, v in enumerate(interleave(smooth, detail)):
                one[t, pl.ds(half * 128 + y, 8, stride=16), :] = v
            left2 = add_pairs(unpack_two(left[2]), own_left(to_left))
            right2 = add_pairs(unpack_two(right[2]), own_right(to_right))
            smooth, detail = lift(smooth, left2, right2, first, last, mix)
            for y, v in enumerate(interleave(smooth, detail)):
                two[t, pl.ds(half * 64 + y, 8, stride=8), :] = v

    times(TILES, column, TILES)
    for load in loads:
        load.wait()
    far = jnp.concatenate(
        [
            mix(me >= 2, got[jnp.maximum(me - 2, 0), :, 0:WIDE], 0.0),
            mix(me + 2 < got.shape[0], got[jnp.minimum(me + 2, got.shape[0] - 1), :, 0:WIDE], 0.0),
        ],
        axis=0,
    )
    held3[...] = (own[...] + (got_e[3] + got_o[3])) + jnp.dot(
        n3[...], far, precision=HIGH, preferred_element_type=jnp.float32
    )
    four = got[0, :, WIDE:]
    for k in range(1, got.shape[0]):
        four = four + got[k, :, WIDE:]
    held4[:, 0 : WIDE // 2] = four[0:4]
    held4[:, WIDE // 2 :] = four[4:8]
    lane = lane_id((4, LANES))
    for t in range(TILES):
        rows = [held3[pl.ds(4 * r, 4), tile(t)] for r in range(4)]
        for f in range(4):
            v = None
            for r in range(4):
                moved = pltpu.roll(rows[r], (r - f) % LANES, 1) if r != f else rows[r]
                v = jnp.where(lane % 4 == r, moved, v) if r else moved
            turned3[pl.ds(4 * f, 4), tile(t)] = v
        v = held4[:, tile(t)]
        for f in range(8):
            turned4[pl.ds(4 * f, 4), tile(t)] = pltpu.roll(v, LANES - f, 1) if f else v
    three = jnp.dot(w3[...], turned3[...], precision=HIGH, preferred_element_type=jnp.float32)
    four = jnp.dot(w4[...], turned4[...], precision=HIGH, preferred_element_type=jnp.float32)
    count = pay.shape[0]
    lane = lane_id((count, LANES))
    for t in range(TILES):
        v = four[0:count, tile(t)]
        for k in range(1, 4):
            v = jnp.where(lane % 8 == k, pltpu.roll(four[k * count : (k + 1) * count, tile(t)], k, 1), v)
        pay[:, t, WIDE // 2 :] = v
    for to in range(count):
        pay[to, 0:4, 0 : WIDE // 2] = three[to * 4 : to * 4 + 4, : WIDE // 2]
        pay[to, 4:8, 0 : WIDE // 2] = three[to * 4 : to * 4 + 4, WIDE // 2 :]
    flip = lax.axis_index("gz") % 2 == 1

    def stack(t):
        lanes = tile_lanes(t)
        going_right, going_left = [None] * 6, [None] * 6
        for half in range(2):
            rows = [one[t, pl.ds(z * 16 + half * 8, 8), :] for z in range(16)]
            to_right, to_left = edges(rows)
            for c in range(2):
                going_right[2 * c + half] = to_right[c]
                going_left[2 * c + half] = to_left[c]
        rows = [two[t, pl.ds(z * 8, 8), :] for z in range(16)]
        to_right, to_left = edges(rows)
        next_right, next_left = edges(lift_alone(rows))
        going_right[4:] = pack_two(*to_right, even), pack_two(*next_right, even)
        going_left[4:] = pack_two(*to_left, even), pack_two(*next_left, even)
        for c in range(6):
            pay_e[c, :, lanes] = mix(flip, going_left[c], going_right[c])
            pay_o[c, :, lanes] = mix(flip, going_right[c], going_left[c])

    times(TILES, stack, TILES)


def along_z(tables, one, two, got_e, got_o, got, result, out, fine, spread, coarse, table, sem):
    load = pltpu.make_async_copy(tables, table, sem.at[16])
    load.start()
    me = lax.axis_index("gz")
    first, last, flip = me == 0, me == lax.axis_size("gz") - 1, me % 2 == 1

    def stack(t):
        lanes = tile_lanes(t)
        e = [got_e[c, :, lanes] for c in range(6)]
        o = [got_o[c, :, lanes] for c in range(6)]
        left = [mix(flip, e[c], o[c]) for c in range(6)]
        right = [mix(flip, o[c], e[c]) for c in range(6)]
        for half in range(2):
            rows = [one[t, pl.ds(z * 16 + half * 8, 8), :] for z in range(16)]
            smooth, detail = lift(rows, left[half:4:2], right[half:4:2], first, last, mix)
            for z, v in enumerate(interleave(smooth, detail)):
                out[z, pl.ds(half * 8, 8), lanes] = v
        rows = [two[t, pl.ds(z * 8, 8), :] for z in range(16)]
        to_right, to_left = edges(rows)
        smooth, _ = lift(rows, unpack_two(left[4]), unpack_two(right[4]), first, last, mix)
        left2 = add_pairs(unpack_two(left[5]), own_left(to_left))
        right2 = add_pairs(unpack_two(right[5]), own_right(to_right))
        smooth, detail = lift(smooth, left2, right2, first, last, mix)
        for z, v in enumerate(interleave(smooth, detail)):
            fine[pl.ds(z * 8, 8), lanes] = v

    times(TILES, stack, TILES)
    sends = [pltpu.make_async_copy(out.at[z], result.at[z], sem.at[z]) for z in range(16)]
    for z in range(1, 16, 2):
        sends[z].start()
    half = WIDE // 2
    load.wait()
    total = got[0]
    for k in range(1, got.shape[0]):
        total = total + got[k]
    three = jnp.concatenate([total[0:4, :half], total[4:8, :half]], axis=1)
    three = lift_lanes(three, table.at[1], 4)
    four = jnp.concatenate([total[t : t + 1, half:] for t in range(TILES)], axis=1)
    four = lift_lanes(four, table.at[2], 8)
    for t in range(TILES):
        v = three[:, tile(t)]
        for r in range(4):
            coarse[t, pl.ds(r, 4, stride=4), :] = pltpu.roll(v, LANES - r, 1) if r else v
        v = four[:, tile(t)]
        here = lane_id((1, LANES)) % 8 == 0
        for k in range(4):
            at = pl.ds((k // 2) * 8 + (k % 2) * 2, 1)
            moved = pltpu.roll(v, LANES - k, 1) if k else v
            coarse[t, at, :] = jnp.where(here, moved, coarse[t, at, :])
    row = lax.broadcasted_iota(jnp.int32, (16, LANES), 0)
    lane = lane_id((16, LANES))
    at_two = (row % 2 == 0) & (lane % 2 == 0)
    at_three = (row % 4 == 0) & (lane % 4 == 0)
    for z in range(8):
        v = lift_lanes(fine[pl.ds(z * 8, 8), :], table.at[0], 2)
        for t in range(TILES):
            spread[t, pl.ds(z * 16, 8, stride=2), :] = v[:, tile(t)]
            w = jnp.where(at_two, spread[t, pl.ds(z * 16, 16), :], out[2 * z, :, tile(t)])
            if z % 2 == 0:
                spread[t, pl.ds(z * 16, 4, stride=4), :] = coarse[t, pl.ds(z * 2, 4), :]
                w = jnp.where(at_three, spread[t, pl.ds(z * 16, 16), :], w)
            out[2 * z, :, tile(t)] = w
        sends[2 * z].start()
    for send in sends:
        send.wait()


def deep_levels(n):
    fixed = lambda c, a, b: a if c else b
    level = lambda rows: lift(rows, (0.0, 0.0), (0.0, 0.0), True, True, fixed)
    cells = level(level(list(np.eye(n)))[0])[0]
    smooth, detail = level(cells)
    return cells, np.stack(interleave(smooth, detail)), np.stack(interleave(*level(smooth)))


def weights_y(devices):
    cells, three, four = deep_levels(16 * devices)
    w3 = np.zeros((devices, 64, 4, 16), np.float64)
    w4 = np.zeros((devices, devices, 2, 2, 2, 16), np.float64)
    for a in range(devices):
        mine = slice(16 * a, 16 * a + 16)
        for k, b in enumerate((a, a + 1, a - 1)):
            for r in range(4):
                for z in range(4):
                    if 0 <= b < devices:
                        w3[a, 16 * k + 4 * r + z, z] = three[4 * b + r, mine]
        for z in range(4):
            for c in range(2):
                if a + 2 < devices:
                    w3[a, 48 + 4 * c + z, z] = edges(cells[4 * a + 4 : 4 * a + 8])[0][c][mine]
                if a - 2 >= 0:
                    w3[a, 56 + 4 * c + z, z] = edges(cells[4 * a - 4 : 4 * a])[1][c][mine]
        for z in range(2):
            w4[a, :, :, z, z] = four[:, mine].reshape(devices, 2, 16)
    near = np.zeros((4, 4, 4, 4), np.float64)
    fixed = lambda c, x, y: y
    for c in range(4):
        unit = [1.0 if c == k else 0.0 for k in range(4)]
        rows = interleave(*lift([0.0] * 4, unit[:2], unit[2:], False, False, fixed))
        for r in range(4):
            for z in range(4):
                near[r, z, c, z] = rows[r]
    return (
        near.reshape(16, 16).astype(np.float32),
        w3.reshape(devices, 64, 64).astype(np.float32),
        w4.reshape(devices, 4 * devices, 32).astype(np.float32),
    )


def weights_z(devices):
    _, three, four = deep_levels(16 * devices)
    w3 = np.zeros((devices, devices, 4, 4, 4), np.float64)
    w4 = np.zeros((devices, 2, 2, devices, 8, 2, 2), np.float64)
    for a in range(devices):
        for f in range(8):
            for zz in range(4):
                if f < 4:
                    z = 16 * a + zz + 4 * (f // 2) + 8 * (f % 2)
                    w3[a, :, :, f, zz] = three[:, z].reshape(devices, 4)
                if zz < 2:
                    z = 16 * a + zz + 2 * (f // 4) + 4 * (f // 2 % 2) + 8 * (f % 2)
                    for o in range(2):
                        w4[a, :, o, :, f, o, zz] = four[:, z].reshape(devices, 2).T
    return (
        w3.reshape(devices, 4 * devices, 16).astype(np.float32),
        w4.reshape(devices, 4 * devices, 32).astype(np.float32),
    )


def swap(values, axis, start):
    devices = lax.axis_size(axis)
    pairs = []
    for i in range(start, devices - 1, 2):
        pairs += [(i, i + 1), (i + 1, i)]
    return lax.ppermute(values, axis, pairs)


def f32(*shape):
    return jax.ShapeDtypeStruct(shape, jnp.float32)


def call(body, out, scratch=(), **more):
    return pl.pallas_call(
        body,
        out_shape=out,
        scratch_shapes=list(scratch),
        compiler_params=pltpu.CompilerParams(vmem_limit_bytes=24 * 1024 * 1024),
        **more,
    )


def per_device(density):
    planes, rows, cells = density.shape
    ny, nz = lax.axis_size("gy"), lax.axis_size("gz")
    near, y3, y4 = [jnp.asarray(w) for w in weights_y(ny)]
    z3, z4 = [jnp.asarray(w) for w in weights_z(nz)]
    tables = jnp.asarray(np.stack([lane_factors(s) for s in (2, 4, 8)]))
    vmem = lambda *shape: pltpu.VMEM(shape, jnp.float32)
    sems = lambda count: pltpu.SemaphoreType.DMA((count,))
    far, here = pl.BlockSpec(memory_space=pltpu.HBM), pl.BlockSpec(memory_space=pltpu.VMEM)
    stay = lambda v: pltpu.with_memory_space_constraint(v, pltpu.HBM)
    near, y3, y4, z3, z4, tables = [stay(v) for v in (near, y3, y4, z3, z4, tables)]
    flat = stay(density.reshape(planes * rows, cells))
    tiled = f32(TILES, planes * rows, LANES)
    payload = f32(4, 16, cells)
    x, pay_e, pay_o, own, pay = call(
        along_x,
        [tiled, payload, payload, f32(16, cells), f32(ny, 8, cells * 3 // 2)],
        [
            vmem(planes * rows, cells),
            vmem(64, 64),
            vmem(4 * ny, 32),
            vmem(128, cells),
            vmem(64, cells),
            vmem(32, cells),
            sems(6),
        ],
        in_specs=[far, far, far],
    )(y3, y4, flat)
    got_e, got_o = swap(pay_e, "gy", 0), swap(pay_o, "gy", 1)
    got = lax.all_to_all(pay, "gy", 0, 0, tiled=True)
    payload = f32(6, 8, cells)
    one, two, pay_e, pay_o, pay = call(
        along_y,
        [
            tiled,
            f32(TILES, planes * rows // 2, LANES),
            payload,
            payload,
            f32(nz, 8, cells // 2 + LANES),
        ],
        [
            vmem(16, 16),
            vmem(4 * nz, 16),
            vmem(4 * nz, 32),
            vmem(16, cells),
            vmem(4, cells),
            vmem(16, cells),
            vmem(32, cells),
            sems(3),
        ],
        in_specs=[far, far, far] + [here] * 5,
    )(near, z3, z4, x, got_e, got_o, own, got)
    got_e, got_o = swap(pay_e, "gz", 0), swap(pay_o, "gz", 1)
    got = lax.all_to_all(pay, "gz", 0, 0, tiled=True)
    return call(
        along_z,
        f32(planes, rows, cells),
        [
            vmem(planes, rows, cells),
            vmem(64, cells),
            vmem(TILES, 128, LANES),
            vmem(TILES, 16, LANES),
            vmem(3, 16, cells),
            sems(planes + 1),
        ],
        in_specs=[far] + [here] * 5,
        out_specs=far,
    )(tables, one, two, got_e, got_o, got)


def solution(mesh):
    return jax.shard_map(
        per_device, mesh=mesh, in_specs=(P("gz", "gy", None),), out_specs=P("gz", "gy", None), check_vma=False
    )
```

```python
import functools

import jax
import jax.numpy as jnp
import numpy as np
from jax import lax
from jax.experimental import pallas as pl
from jax.experimental.pallas import tpu as pltpu
from jax.sharding import PartitionSpec as P

A1 = -1.586134342059924
B1 = -0.052980118572961
A2 = 0.882911075530934
B2 = 0.443506852043971
GAIN = 1.230174104914001

WIDE = 1024
LANES = 128
TILES = WIDE // LANES
HIGH = lax.Precision.HIGHEST


def lift(rows, left, right, first, last, choose):
    p, q = left
    s_next, r = right
    smooth, detail = rows[0::2], rows[1::2]
    m = len(smooth)
    s_next = choose(last, smooth[-1], s_next)
    d1 = [detail[i] + A1 * (smooth[i] + (smooth[i + 1] if i + 1 < m else s_next)) for i in range(m)]
    d1_before = choose(first, d1[0], p + A1 * smooth[0])
    s1 = [smooth[i] + B1 * ((d1[i - 1] if i else d1_before) + d1[i]) for i in range(m)]
    s1_after = choose(last, s1[-1], r + B1 * d1[-1])
    d2 = [d1[i] + A2 * (s1[i] + (s1[i + 1] if i + 1 < m else s1_after)) for i in range(m)]
    d2_before = choose(first, d2[0], d1_before + A2 * (q + B1 * d1_before + s1[0]))
    s2 = [s1[i] + B2 * ((d2[i - 1] if i else d2_before) + d2[i]) for i in range(m)]
    return [v * (1.0 / GAIN) for v in s2], [v * (GAIN / 2.0) for v in d2]


def lift_alone(rows):
    zero = jnp.zeros_like(rows[0])
    return lift(rows, (zero, zero), (zero, zero), False, False, lambda c, a, b: a if c else b)[0]


def edges(rows):
    s, d = rows[0::2], rows[1::2]
    to_right = (d[-1] + A1 * s[-1], s[-1] + B1 * (d[-2] + A1 * (s[-2] + s[-1])))
    to_left = (s[0], s[0] + B1 * (d[0] + A1 * (s[0] + s[1])))
    return to_right, to_left


def own_left(to_left):
    s, r = to_left
    c2 = (B2 * A2 * B1 * A1 / GAIN) * s
    c1 = ((B1 * A1 + B2 * A1 + 3 * B2 * A2 * B1 * A1) / GAIN) * s + (B2 * A2 / GAIN) * r
    return c1 + A1 * c2, (1 + B1 * A1) * c2


def own_right(to_right):
    p, q = to_right
    c0 = ((B1 + B2 + 3 * B2 * A2 * B1) / GAIN) * p + (B2 * A2 / GAIN) * q
    c1 = (B2 * A2 * B1 / GAIN) * p
    return c0, c0 + B1 * (c1 + A1 * c0)


def add_pairs(a, b):
    return a[0] + b[0], a[1] + b[1]


def mix(flag, a, b):
    return jnp.where(flag, a, b)


def interleave(smooth, detail):
    return [v for pair in zip(smooth, detail) for v in pair]


def lane_factors(stride):
    run = np.arange(WIDE) // stride
    ends = run[-1]
    odd, even = run % 2 == 1, run % 2 == 0
    table = np.zeros((16, WIDE), np.float64)
    for k, a in enumerate((A1, B1, A2, B2)):
        at = even if k % 2 else odd
        closed = run == (0 if k % 2 else ends)
        before, after = (4 + k, k) if k % 2 else (k, 4 + k)
        table[before] = np.where(at, np.where(closed, 2 * a, a), 0.0)
        table[after] = np.where(at & ~closed, a, 0.0)
    table[8] = np.where(even, 1.0 / GAIN, GAIN / 2.0)
    return table.astype(np.float32)


def lift_lanes(v, table, stride):
    for k in range(4):
        before = pltpu.roll(v, stride, 1)
        after = pltpu.roll(v, WIDE - stride, 1)
        v = v + table[k : k + 1, :] * before + table[4 + k : 5 + k, :] * after
    return v * table[8:9, :]


def lane_id(shape):
    return lax.broadcasted_iota(jnp.int32, shape, len(shape) - 1)


def pack_two(a, b, even):
    return jnp.where(even, a, pltpu.roll(b, 1, 1))


def unpack_two(w):
    return w, pltpu.roll(w, LANES - 1, 1)


def tile(t):
    return slice(t * LANES, (t + 1) * LANES)


def times(count, body, unroll=1):
    if unroll == count:
        for i in range(count):
            body(i)
        return

    def step(i, carry):
        body(i)
        return carry

    lax.fori_loop(0, count, step, 0, unroll=unroll)


def tile_lanes(t):
    return pl.ds(t * LANES if isinstance(t, int) else pl.multiple_of(t * LANES, LANES), LANES)


def lift_two(a, b, phase):
    lane = lane_id((a[0].shape[0], LANES))
    here = lane % (2 * phase) < phase
    count, reach = len(a), 2 * phase
    s = [jnp.where(here, x, pltpu.roll(y, phase, 1)) for x, y in zip(a, b)]
    d = [jnp.where(here, pltpu.roll(x, LANES - phase, 1), y) for x, y in zip(a, b)]

    def ahead(x):
        r = [pltpu.roll(w, LANES - reach, 1) for w in x]
        return [jnp.where(lane < LANES - reach, r[t], r[t + 1] if t + 1 < count else x[t]) for t in range(count)]

    def behind(x):
        r = [pltpu.roll(w, reach, 1) for w in x]
        return [jnp.where(lane >= reach, r[t], r[t - 1] if t else x[t]) for t in range(count)]

    d = [x + A1 * (y + z) for x, y, z in zip(d, s, ahead(s))]
    s = [x + B1 * (y + z) for x, y, z in zip(s, d, behind(d))]
    d = [x + A2 * (y + z) for x, y, z in zip(d, s, ahead(s))]
    s = [(x + B2 * (y + z)) * (1.0 / GAIN) for x, y, z in zip(s, d, behind(d))]
    return s, [x * (GAIN / 2.0) for x in d]


def separate(s, d, phase):
    here = lane_id(s[0].shape) % (2 * phase) < phase
    a = [jnp.where(here, x, pltpu.roll(y, phase, 1)) for x, y in zip(s, d)]
    b = [jnp.where(here, pltpu.roll(x, LANES - phase, 1), y) for x, y in zip(s, d)]
    return a, b


def tiles_of(ref, at):
    v = ref[at, :]
    return [v[:, tile(t)] for t in range(TILES)]


def put_tiles(ref, at, parts):
    for t, v in enumerate(parts):
        ref[at, tile(t)] = v


def along_x(density, out, pay_e, pay_o, e1, x, sem):
    part = x.shape[0] // 4
    loads = [
        pltpu.make_async_copy(density.at[pl.ds(k * part, part)], x.at[pl.ds(k * part, part)], sem.at[k])
        for k in (0, 2, 1, 3)
    ]
    for load in loads:
        load.start()

    def plane(i):
        z, y = i // 2, i % 2
        at = pl.multiple_of(z * 16 + y * 8, 8)
        far = pl.multiple_of(z * 16 + y * 8 + 128, 8)
        s, d = lift_two(tiles_of(x, pl.ds(at, 8)), tiles_of(x, pl.ds(far, 8)), 1)
        put_tiles(e1, pl.ds(at, 8), s)
        a, b = separate(s, d, 1)
        for t in range(TILES):
            out[t, pl.ds(at, 8), :] = a[t]
            out[t, pl.ds(far, 8), :] = b[t]

    loads[0].wait()
    loads[1].wait()
    times(8, plane, 4)
    loads[2].wait()
    loads[3].wait()
    times(8, lambda i: plane(i + 8), 4)
    flip = lax.axis_index("gy") % 2 == 1
    even = lane_id((8, LANES)) % 2 == 0

    def column(t):
        lanes = tile_lanes(t)
        for half in range(2):
            rows = [out[t, pl.ds(half * 128 + y, 8, stride=16), :] for y in range(16)]
            to_right, to_left = edges(rows)
            next_right, next_left = edges(lift_alone(rows))
            going_right = to_right + (pack_two(*next_right, even),)
            going_left = to_left + (pack_two(*next_left, even),)
            for c in range(3):
                pay_e[c, pl.ds(half * 8, 8), lanes] = mix(flip, going_left[c], going_right[c])
                pay_o[c, pl.ds(half * 8, 8), lanes] = mix(flip, going_right[c], going_left[c])

    times(TILES, column, 2)


def thin_y(weights3, weights4, e1, own, pay, w3, w4, e2, e3, sem):
    me = lax.axis_index("gy")
    loads = [
        pltpu.make_async_copy(weights3.at[me], w3, sem.at[0]),
        pltpu.make_async_copy(weights4.at[me], w4, sem.at[1]),
    ]
    for load in loads:
        load.start()

    def second(i):
        at = pl.multiple_of(i * 8, 8)
        s, _ = lift_two(tiles_of(e1, pl.ds(at, 8)), tiles_of(e1, pl.ds(at + 64, 8)), 2)
        put_tiles(e2, pl.ds(at, 8), s)

    times(8, second, 4)

    def third(i):
        at = pl.multiple_of(i * 8, 8)
        s, _ = lift_two(tiles_of(e2, pl.ds(at, 8)), tiles_of(e2, pl.ds(at + 32, 8)), 4)
        put_tiles(e3, pl.ds(at, 8), s)

    times(4, third, 4)
    for load in loads:
        load.wait()
    three = jnp.dot(w3[...], e2[...], precision=HIGH, preferred_element_type=jnp.float32)
    own[...] = three[0:16]
    four = jnp.dot(w4[...], e3[...], precision=HIGH, preferred_element_type=jnp.float32)
    for to in range(pay.shape[0]):
        right = mix(to == me + 1, three[16:24], three[24:32])
        left = mix(to == me - 1, three[32:40], three[40:48])
        pay[to, :, 0:WIDE] = mix(to > me, right, left)
        pay[to, 0:4, WIDE:] = four[to * 4 : to * 4 + 4, : WIDE // 2]
        pay[to, 4:8, WIDE:] = four[to * 4 : to * 4 + 4, WIDE // 2 :]


def along_y(x, got_e, got_o, one, two, pay_e, pay_o):
    me = lax.axis_index("gy")
    first, last, flip = me == 0, me == lax.axis_size("gy") - 1, me % 2 == 1
    even = lane_id((8, LANES)) % 2 == 0

    def column(t):
        lanes = tile_lanes(t)
        for half in range(2):
            rows = [x[t, pl.ds(half * 128 + y, 8, stride=16), :] for y in range(16)]
            e = [got_e[c, pl.ds(half * 8, 8), lanes] for c in range(3)]
            o = [got_o[c, pl.ds(half * 8, 8), lanes] for c in range(3)]
            left = [mix(flip, e[c], o[c]) for c in range(3)]
            right = [mix(flip, o[c], e[c]) for c in range(3)]
            to_right, to_left = edges(rows)
            smooth, detail = lift(rows, left[:2], right[:2], first, last, mix)
            for y, v in enumerate(interleave(smooth, detail)):
                one[t, pl.ds(half * 128 + y, 8, stride=16), :] = v
            left2 = add_pairs(unpack_two(left[2]), own_left(to_left))
            right2 = add_pairs(unpack_two(right[2]), own_right(to_right))
            smooth, detail = lift(smooth, left2, right2, first, last, mix)
            for y, v in enumerate(interleave(smooth, detail)):
                two[t, pl.ds(half * 64 + y, 8, stride=8), :] = v

    times(TILES, column, TILES)
    flip = lax.axis_index("gz") % 2 == 1

    def stack(t):
        lanes = tile_lanes(t)
        going_right, going_left = [None] * 6, [None] * 6
        for half in range(2):
            rows = [one[t, pl.ds(z * 16 + half * 8, 8), :] for z in range(16)]
            to_right, to_left = edges(rows)
            for c in range(2):
                going_right[2 * c + half] = to_right[c]
                going_left[2 * c + half] = to_left[c]
        rows = [two[t, pl.ds(z * 8, 8), :] for z in range(16)]
        to_right, to_left = edges(rows)
        next_right, next_left = edges(lift_alone(rows))
        going_right[4:] = pack_two(*to_right, even), pack_two(*next_right, even)
        going_left[4:] = pack_two(*to_left, even), pack_two(*next_left, even)
        for c in range(6):
            pay_e[c, :, lanes] = mix(flip, going_left[c], going_right[c])
            pay_o[c, :, lanes] = mix(flip, going_right[c], going_left[c])

    times(TILES, stack, TILES)


def thin_z(weights3, weights4, two, own, got, pay, w3, w4, thick, cells, beyond, held4, turned3, turned4, sem):
    mz = lax.axis_index("gz")
    loads = [
        pltpu.make_async_copy(weights3.at[mz], w3, sem.at[0]),
        pltpu.make_async_copy(weights4.at[mz], w4, sem.at[1]),
    ]
    for load in loads:
        load.start()
    me, count = lax.axis_index("gy"), got.shape[0]
    first, last = me == 0, me == count - 1
    even = lane_id((8, LANES)) % 2 == 0
    for t in range(TILES):
        for r in range(4):
            low, high = [two[t, pl.ds(64 * half + 2 * r, 8, stride=8), :] for half in range(2)]
            v = pack_two(low, high, even)
            thick[pl.ds(4 * r, 4), tile(t)] = v[0:4]
            thick[pl.ds(16 + 4 * r, 4), tile(t)] = v[4:8]
    for i in range(2):
        s, _ = lift_two(tiles_of(thick, pl.ds(8 * i, 8)), tiles_of(thick, pl.ds(16 + 8 * i, 8)), 2)
        put_tiles(cells, pl.ds(8 * i, 8), s)
    near = lambda k: got[jnp.clip(me + k, 0, count - 1), :, 0:WIDE]
    beyond[0:8] = own[0:8] + (mix(me >= 1, near(-1), 0.0) + mix(me >= 2, near(-2), 0.0))
    beyond[8:16] = own[8:16] + (mix(me < count - 1, near(1), 0.0) + mix(me < count - 2, near(2), 0.0))
    four = got[0, :, WIDE:]
    for k in range(1, count):
        four = four + got[k, :, WIDE:]
    held4[:, 0 : WIDE // 2] = four[0:4]
    held4[:, WIDE // 2 :] = four[4:8]
    lane = lane_id((4, LANES))
    for t in range(TILES):
        at = lambda r: pl.ds(4 * r, 4)
        p, q, s, r = [beyond[at(c), tile(t)] for c in range(4)]
        rows = [cells[at(c), tile(t)] for c in range(4)]
        rows = interleave(*lift(rows, (p, q), (s, r), first, last, mix))
        for f in range(4):
            v = None
            for r in range(4):
                moved = pltpu.roll(rows[r], (r - f) % LANES, 1) if r != f else rows[r]
                v = jnp.where(lane % 4 == r, moved, v) if r else moved
            turned3[at(f), tile(t)] = v
        v = held4[:, tile(t)]
        for f in range(8):
            turned4[at(f), tile(t)] = pltpu.roll(v, LANES - f, 1) if f else v
    for load in loads:
        load.wait()
    three = jnp.dot(w3[...], turned3[...], precision=HIGH, preferred_element_type=jnp.float32)
    four = jnp.dot(w4[...], turned4[...], precision=HIGH, preferred_element_type=jnp.float32)
    count = pay.shape[0]
    lane = lane_id((count, LANES))
    for t in range(TILES):
        v = four[0:count, tile(t)]
        for k in range(1, 4):
            v = jnp.where(lane % 8 == k, pltpu.roll(four[k * count : (k + 1) * count, tile(t)], k, 1), v)
        pay[:, t, WIDE // 2 :] = v
    for to in range(count):
        pay[to, 0:4, 0 : WIDE // 2] = three[to * 4 : to * 4 + 4, : WIDE // 2]
        pay[to, 4:8, 0 : WIDE // 2] = three[to * 4 : to * 4 + 4, WIDE // 2 :]


def along_z(tables, one, two, got_e, got_o, result, fourth, out, fine, spread, table, sem):
    load = pltpu.make_async_copy(tables.at[0], table, sem.at[16])
    load.start()
    me = lax.axis_index("gz")
    first, last, flip = me == 0, me == lax.axis_size("gz") - 1, me % 2 == 1

    def stack(t):
        lanes = tile_lanes(t)
        e = [got_e[c, :, lanes] for c in range(6)]
        o = [got_o[c, :, lanes] for c in range(6)]
        left = [mix(flip, e[c], o[c]) for c in range(6)]
        right = [mix(flip, o[c], e[c]) for c in range(6)]
        for half in range(2):
            rows = [one[t, pl.ds(z * 16 + half * 8, 8), :] for z in range(16)]
            smooth, detail = lift(rows, left[half:4:2], right[half:4:2], first, last, mix)
            for z, v in enumerate(interleave(smooth, detail)):
                out[z, pl.ds(half * 8, 8), lanes] = v
        rows = [two[t, pl.ds(z * 8, 8), :] for z in range(16)]
        to_right, to_left = edges(rows)
        smooth, _ = lift(rows, unpack_two(left[4]), unpack_two(right[4]), first, last, mix)
        left2 = add_pairs(unpack_two(left[5]), own_left(to_left))
        right2 = add_pairs(unpack_two(right[5]), own_right(to_right))
        smooth, detail = lift(smooth, left2, right2, first, last, mix)
        for z, v in enumerate(interleave(smooth, detail)):
            fine[pl.ds(z * 8, 8), lanes] = v

    times(TILES, stack, TILES)
    sends = {z: pltpu.make_async_copy(out.at[z], result.at[z], sem.at[z]) for z in range(16) if z % 4}
    for z in range(1, 16, 2):
        sends[z].start()
    load.wait()
    row = lax.broadcasted_iota(jnp.int32, (16, LANES), 0)
    here = (row % 2 == 0) & (lane_id((16, LANES)) % 2 == 0)
    for z in (1, 3, 5, 7, 0, 2, 4, 6):
        v = lift_lanes(fine[pl.ds(z * 8, 8), :], table, 2)
        for t in range(TILES):
            spread[t, pl.ds(z * 16, 8, stride=2), :] = v[:, tile(t)]
            w = jnp.where(here, spread[t, pl.ds(z * 16, 16), :], out[2 * z, :, tile(t)])
            if z % 2:
                out[2 * z, :, tile(t)] = w
            else:
                fourth[z // 2, :, tile(t)] = w
        if z % 2:
            sends[2 * z].start()
    for send in sends.values():
        send.wait()


def join(tables, got, fourth, base, result, planes, spread, coarse, table, sem):
    load = pltpu.make_async_copy(tables, table, sem.at[4])
    load.start()
    half = WIDE // 2
    total = got[0]
    for k in range(1, got.shape[0]):
        total = total + got[k]
    load.wait()
    three = jnp.concatenate([total[0:4, :half], total[4:8, :half]], axis=1)
    three = lift_lanes(three, table.at[1], 4)
    four = jnp.concatenate([total[t : t + 1, half:] for t in range(TILES)], axis=1)
    four = lift_lanes(four, table.at[2], 8)
    for t in range(TILES):
        v = three[:, tile(t)]
        for r in range(4):
            coarse[t, pl.ds(r, 4, stride=4), :] = pltpu.roll(v, LANES - r, 1) if r else v
        v = four[:, tile(t)]
        here = lane_id((1, LANES)) % 8 == 0
        for k in range(4):
            at = pl.ds((k // 2) * 8 + (k % 2) * 2, 1)
            moved = pltpu.roll(v, LANES - k, 1) if k else v
            coarse[t, at, :] = jnp.where(here, moved, coarse[t, at, :])
    row = lax.broadcasted_iota(jnp.int32, (16, LANES), 0)
    here = (row % 4 == 0) & (lane_id((16, LANES)) % 4 == 0)
    sends = [pltpu.make_async_copy(planes.at[i], result.at[4 * i], sem.at[i]) for i in range(4)]
    for i in range(4):
        for t in range(TILES):
            spread[t, pl.ds(i * 16, 4, stride=4), :] = coarse[t, pl.ds(i * 4, 4), :]
            planes[i, :, tile(t)] = jnp.where(here, spread[t, pl.ds(i * 16, 16), :], fourth[i, :, tile(t)])
        sends[i].start()
    for send in sends:
        send.wait()


def deep_levels(n):
    fixed = lambda c, a, b: a if c else b
    level = lambda rows: lift(rows, (0.0, 0.0), (0.0, 0.0), True, True, fixed)
    cells = level(level(list(np.eye(n)))[0])[0]
    smooth, detail = level(cells)
    return cells, np.stack(interleave(smooth, detail)), np.stack(interleave(*level(smooth)))


def weights_y(devices):
    cells, _, four = deep_levels(16 * devices)
    w3 = np.zeros((devices, 48, 4, 16), np.float64)
    w4 = np.zeros((devices, devices, 2, 2, 2, 16), np.float64)
    for a in range(devices):
        mine = slice(16 * a, 16 * a + 16)
        for row, side, b in ((0, 0, -1), (8, 1, 1), (16, 0, 0), (24, 0, 1), (32, 1, 0), (40, 1, -1)):
            if 0 <= a + b < devices:
                pair = edges(cells[4 * (a + b) : 4 * (a + b) + 4])[side]
                for c in range(2):
                    for z in range(4):
                        w3[a, row + 4 * c + z, z] = pair[c][mine]
        for z in range(2):
            w4[a, :, :, z, z] = four[:, mine].reshape(devices, 2, 16)
    return (
        w3.reshape(devices, 48, 64).astype(np.float32),
        w4.reshape(devices, 4 * devices, 32).astype(np.float32),
    )


def weights_z(devices):
    _, three, four = deep_levels(16 * devices)
    w3 = np.zeros((devices, devices, 4, 4, 4), np.float64)
    w4 = np.zeros((devices, 2, 2, devices, 8, 2, 2), np.float64)
    for a in range(devices):
        for f in range(8):
            for zz in range(4):
                if f < 4:
                    z = 16 * a + zz + 4 * (f // 2) + 8 * (f % 2)
                    w3[a, :, :, f, zz] = three[:, z].reshape(devices, 4)
                if zz < 2:
                    z = 16 * a + zz + 2 * (f // 4) + 4 * (f // 2 % 2) + 8 * (f % 2)
                    for o in range(2):
                        w4[a, :, o, :, f, o, zz] = four[:, z].reshape(devices, 2).T
    return (
        w3.reshape(devices, 4 * devices, 16).astype(np.float32),
        w4.reshape(devices, 4 * devices, 32).astype(np.float32),
    )


def swap(values, axis, start):
    devices = lax.axis_size(axis)
    pairs = []
    for i in range(start, devices - 1, 2):
        pairs += [(i, i + 1), (i + 1, i)]
    return lax.ppermute(values, axis, pairs)


def f32(*shape):
    return jax.ShapeDtypeStruct(shape, jnp.float32)


def call(body, out, scratch=(), cost=4 << 20, **more):
    return pl.pallas_call(
        body,
        out_shape=out,
        scratch_shapes=list(scratch),
        cost_estimate=pl.CostEstimate(flops=cost * 10, bytes_accessed=4 << 20, transcendentals=0),
        compiler_params=pltpu.CompilerParams(vmem_limit_bytes=24 * 1024 * 1024),
        **more,
    )


def per_device(density):
    planes, rows, cells = density.shape
    ny, nz = lax.axis_size("gy"), lax.axis_size("gz")
    vmem = lambda *shape: pltpu.VMEM(shape, jnp.float32)
    sems = lambda count: pltpu.SemaphoreType.DMA((count,))
    far, here = pl.BlockSpec(memory_space=pltpu.HBM), pl.BlockSpec(memory_space=pltpu.VMEM)
    stay = lambda v: pltpu.with_memory_space_constraint(jnp.asarray(v), pltpu.HBM)
    tables = stay(np.stack([lane_factors(s) for s in (2, 4, 8)]))
    tiled = f32(TILES, planes * rows, LANES)

    payload = f32(3, 16, cells)
    x, pay_e, pay_o, e1 = call(
        along_x,
        [tiled, payload, payload, f32(planes * rows // 2, cells)],
        [vmem(planes * rows, cells), sems(4)],
        in_specs=[far],
    )(stay(density.reshape(planes * rows, cells)))
    got_e, got_o = swap(pay_e, "gy", 0), swap(pay_o, "gy", 1)
    own, pay = call(
        thin_y,
        [f32(16, cells), f32(ny, 8, cells * 3 // 2)],
        [vmem(48, 64), vmem(4 * ny, 32), vmem(64, cells), vmem(32, cells), sems(2)],
        cost=40 << 20,
        in_specs=[far, far, here],
    )(*[stay(w) for w in weights_y(ny)], e1)
    got = lax.all_to_all(pay, "gy", 0, 0, tiled=True)

    payload = f32(6, 8, cells)
    one, two, pay_e, pay_o = call(along_y, [tiled, f32(TILES, planes * rows // 2, LANES), payload, payload], cost=400 << 20, input_output_aliases={0: 0})(
        x, got_e, got_o
    )
    got_e, got_o = swap(pay_e, "gz", 0), swap(pay_o, "gz", 1)
    pay = call(
        thin_z,
        f32(nz, 8, cells // 2 + LANES),
        [
            vmem(4 * nz, 16),
            vmem(4 * nz, 32),
            vmem(32, cells),
            vmem(16, cells),
            vmem(16, cells),
            vmem(4, cells),
            vmem(16, cells),
            vmem(32, cells),
            sems(2),
        ],
        cost=40 << 20,
        in_specs=[far, far, here, here, here],
    )(*[stay(w) for w in weights_z(nz)], two, own, got)
    got = lax.all_to_all(pay, "gz", 0, 0, tiled=True)

    base, fourth = call(
        along_z,
        [f32(planes, rows, cells), f32(planes // 4, rows, cells)],
        [vmem(planes, rows, cells), vmem(64, cells), vmem(TILES, 128, LANES), vmem(16, cells), sems(planes + 1)],
        cost=400 << 20,
        in_specs=[far] + [here] * 4,
        out_specs=[far, here],
    )(tables, one, two, got_e, got_o)
    return call(
        join,
        f32(planes, rows, cells),
        [vmem(planes // 4, rows, cells), vmem(TILES, 64, LANES), vmem(TILES, 16, LANES), vmem(3, 16, cells), sems(5)],
        in_specs=[far, here, here, far],
        out_specs=far,
        input_output_aliases={3: 0},
    )(tables, got, fourth, stay(base))


def solution(mesh):
    return jax.shard_map(
        per_device, mesh=mesh, in_specs=(P("gz", "gy", None),), out_specs=P("gz", "gy", None), check_vma=False
    )
```

```python
import functools

import jax
import jax.numpy as jnp
import numpy as np
from jax import lax
from jax.experimental import pallas as pl
from jax.experimental.pallas import tpu as pltpu
from jax.sharding import PartitionSpec as P

A1 = -1.586134342059924
B1 = -0.052980118572961
A2 = 0.882911075530934
B2 = 0.443506852043971
GAIN = 1.230174104914001

WIDE = 1024
LANES = 128
TILES = WIDE // LANES
HIGH = lax.Precision.HIGHEST


def lift(rows, left, right, first, last, choose):
    p, q = left
    s_next, r = right
    smooth, detail = rows[0::2], rows[1::2]
    m = len(smooth)
    s_next = choose(last, smooth[-1], s_next)
    d1 = [detail[i] + A1 * (smooth[i] + (smooth[i + 1] if i + 1 < m else s_next)) for i in range(m)]
    d1_before = choose(first, d1[0], p + A1 * smooth[0])
    s1 = [smooth[i] + B1 * ((d1[i - 1] if i else d1_before) + d1[i]) for i in range(m)]
    s1_after = choose(last, s1[-1], r + B1 * d1[-1])
    d2 = [d1[i] + A2 * (s1[i] + (s1[i + 1] if i + 1 < m else s1_after)) for i in range(m)]
    d2_before = choose(first, d2[0], d1_before + A2 * (q + B1 * d1_before + s1[0]))
    s2 = [s1[i] + B2 * ((d2[i - 1] if i else d2_before) + d2[i]) for i in range(m)]
    return [v * (1.0 / GAIN) for v in s2], [v * (GAIN / 2.0) for v in d2]


def lift_alone(rows):
    zero = jnp.zeros_like(rows[0])
    return lift(rows, (zero, zero), (zero, zero), False, False, lambda c, a, b: a if c else b)[0]


def edges(rows):
    s, d = rows[0::2], rows[1::2]
    to_right = (d[-1] + A1 * s[-1], s[-1] + B1 * (d[-2] + A1 * (s[-2] + s[-1])))
    to_left = (s[0], s[0] + B1 * (d[0] + A1 * (s[0] + s[1])))
    return to_right, to_left


def own_left(to_left):
    s, r = to_left
    c2 = (B2 * A2 * B1 * A1 / GAIN) * s
    c1 = ((B1 * A1 + B2 * A1 + 3 * B2 * A2 * B1 * A1) / GAIN) * s + (B2 * A2 / GAIN) * r
    return c1 + A1 * c2, (1 + B1 * A1) * c2


def own_right(to_right):
    p, q = to_right
    c0 = ((B1 + B2 + 3 * B2 * A2 * B1) / GAIN) * p + (B2 * A2 / GAIN) * q
    c1 = (B2 * A2 * B1 / GAIN) * p
    return c0, c0 + B1 * (c1 + A1 * c0)


def add_pairs(a, b):
    return a[0] + b[0], a[1] + b[1]


def mix(flag, a, b):
    return jnp.where(flag, a, b)


def interleave(smooth, detail):
    return [v for pair in zip(smooth, detail) for v in pair]


def lift_runs(v, stride):
    lane, count = lane_id(v[0].shape), len(v)
    odd = lane // stride % 2 == 1
    for k, a in enumerate((A1, B1, A2, B2)):
        up = [pltpu.roll(x, stride, 1) for x in v]
        down = [pltpu.roll(x, LANES - stride, 1) for x in v]
        before = [jnp.where(lane >= stride, up[t], up[t - 1] if t else down[t]) for t in range(count)]
        after = [jnp.where(lane < LANES - stride, down[t], down[t + 1] if t + 1 < count else up[t]) for t in range(count)]
        factor = jnp.where(odd, 0.0, a) if k % 2 else jnp.where(odd, a, 0.0)
        v = [x + factor * (y + z) for x, y, z in zip(v, before, after)]
    scale = jnp.where(odd, GAIN / 2.0, 1.0 / GAIN)
    return [x * scale for x in v]


def lane_id(shape):
    return lax.broadcasted_iota(jnp.int32, shape, len(shape) - 1)


def pack_two(a, b, even):
    return jnp.where(even, a, pltpu.roll(b, 1, 1))


def unpack_two(w):
    return w, pltpu.roll(w, LANES - 1, 1)


def tile(t):
    return slice(t * LANES, (t + 1) * LANES)


def times(count, body, unroll=1):
    if unroll == count:
        for i in range(count):
            body(i)
        return

    def step(i, carry):
        body(i)
        return carry

    lax.fori_loop(0, count, step, 0, unroll=unroll)


def tile_lanes(t):
    return pl.ds(t * LANES if isinstance(t, int) else pl.multiple_of(t * LANES, LANES), LANES)


def lift_two(a, b, phase):
    lane = lane_id((a[0].shape[0], LANES))
    here = lane % (2 * phase) < phase
    count, reach = len(a), 2 * phase
    s = [jnp.where(here, x, pltpu.roll(y, phase, 1)) for x, y in zip(a, b)]
    d = [jnp.where(here, pltpu.roll(x, LANES - phase, 1), y) for x, y in zip(a, b)]

    def ahead(x):
        r = [pltpu.roll(w, LANES - reach, 1) for w in x]
        return [jnp.where(lane < LANES - reach, r[t], r[t + 1] if t + 1 < count else x[t]) for t in range(count)]

    def behind(x):
        r = [pltpu.roll(w, reach, 1) for w in x]
        return [jnp.where(lane >= reach, r[t], r[t - 1] if t else x[t]) for t in range(count)]

    d = [x + A1 * (y + z) for x, y, z in zip(d, s, ahead(s))]
    s = [x + B1 * (y + z) for x, y, z in zip(s, d, behind(d))]
    d = [x + A2 * (y + z) for x, y, z in zip(d, s, ahead(s))]
    s = [(x + B2 * (y + z)) * (1.0 / GAIN) for x, y, z in zip(s, d, behind(d))]
    return s, [x * (GAIN / 2.0) for x in d]


def separate(s, d, phase):
    here = lane_id(s[0].shape) % (2 * phase) < phase
    a = [jnp.where(here, x, pltpu.roll(y, phase, 1)) for x, y in zip(s, d)]
    b = [jnp.where(here, pltpu.roll(x, LANES - phase, 1), y) for x, y in zip(s, d)]
    return a, b


def tiles_of(ref, at):
    v = ref[at, :]
    return [v[:, tile(t)] for t in range(TILES)]


def put_tiles(ref, at, parts):
    for t, v in enumerate(parts):
        ref[at, tile(t)] = v


def along_x(weights3, weights4, density, out, pay_e, pay_o, e1, w3, w4, x, sem):
    me = lax.axis_index("gy")

    def load(k):
        at = pl.ds(pl.multiple_of(k * 32, 32), 32)
        return pltpu.make_async_copy(density.at[at], x.at[at], sem.at[k])

    for k in range(4):
        load(k).start()
        load(k + 4).start()
    hints = [
        pltpu.make_async_copy(weights3.at[me], w3, sem.at[8]),
        pltpu.make_async_copy(weights4.at[me], w4, sem.at[9]),
    ]
    for hint in hints:
        hint.start()

    def plane(i):
        z, y = i // 2, i % 2
        at = pl.multiple_of(z * 16 + y * 8, 8)
        far = pl.multiple_of(z * 16 + y * 8 + 128, 8)
        s, d = lift_two(tiles_of(x, pl.ds(at, 8)), tiles_of(x, pl.ds(far, 8)), 1)
        put_tiles(e1, pl.ds(at, 8), s)
        a, b = separate(s, d, 1)
        for t in range(TILES):
            out[t, pl.ds(at, 8), :] = a[t]
            out[t, pl.ds(far, 8), :] = b[t]

    def group(k):
        load(k).wait()
        load(k + 4).wait()
        for i in range(4):
            plane(4 * k + i)

    times(4, group)
    flip = me % 2 == 1
    even = lane_id((8, LANES)) % 2 == 0

    def column(t):
        lanes = tile_lanes(t)
        for half in range(2):
            rows = [out[t, pl.ds(half * 128 + y, 8, stride=16), :] for y in range(16)]
            to_right, to_left = edges(rows)
            next_right, next_left = edges(lift_alone(rows))
            going_right = to_right + (pack_two(*next_right, even),)
            going_left = to_left + (pack_two(*next_left, even),)
            for c in range(3):
                pay_e[c, pl.ds(half * 8, 8), lanes] = mix(flip, going_left[c], going_right[c])
                pay_o[c, pl.ds(half * 8, 8), lanes] = mix(flip, going_right[c], going_left[c])

    times(TILES, column, 4)
    for hint in hints:
        hint.wait()


def thin_y(w3, w4, e1, own, result, pay, e2, e3, sem):
    me = lax.axis_index("gy")

    def second(i):
        at = pl.multiple_of(i * 8, 8)
        s, _ = lift_two(tiles_of(e1, pl.ds(at, 8)), tiles_of(e1, pl.ds(at + 64, 8)), 2)
        put_tiles(e2, pl.ds(at, 8), s)

    times(8, second, 4)
    three = jnp.dot(w3[...], e2[...], precision=HIGH, preferred_element_type=jnp.float32)
    own[...] = three[0:16]
    for to in range(pay.shape[0]):
        right = mix(to == me + 1, three[16:24], three[24:32])
        left = mix(to == me - 1, three[32:40], three[40:48])
        pay[to, :, 0:WIDE] = mix(to > me, right, left)
    parts = [pl.ds(0, WIDE), pl.ds(WIDE, WIDE // 2)]
    sends = [pltpu.make_async_copy(pay.at[:, :, p], result.at[:, :, p], sem.at[k]) for k, p in enumerate(parts)]
    sends[0].start()

    def third(i):
        at = pl.multiple_of(i * 8, 8)
        s, _ = lift_two(tiles_of(e2, pl.ds(at, 8)), tiles_of(e2, pl.ds(at + 32, 8)), 4)
        put_tiles(e3, pl.ds(at, 8), s)

    times(4, third, 4)
    four = jnp.dot(w4[...], e3[...], precision=HIGH, preferred_element_type=jnp.float32)
    for to in range(pay.shape[0]):
        pay[to, 0:4, WIDE:] = four[to * 4 : to * 4 + 4, : WIDE // 2]
        pay[to, 4:8, WIDE:] = four[to * 4 : to * 4 + 4, WIDE // 2 :]
    sends[1].start()
    for send in sends:
        send.wait()


def along_y(x, got_e, got_o, one, two, pay_e, pay_o, cells, thick):
    me = lax.axis_index("gy")
    first, last, flip = me == 0, me == lax.axis_size("gy") - 1, me % 2 == 1
    even = lane_id((8, LANES)) % 2 == 0

    def column(t):
        lanes = tile_lanes(t)
        for half in range(2):
            rows = [x[t, pl.ds(half * 128 + y, 8, stride=16), :] for y in range(16)]
            e = [got_e[c, pl.ds(half * 8, 8), lanes] for c in range(3)]
            o = [got_o[c, pl.ds(half * 8, 8), lanes] for c in range(3)]
            left = [mix(flip, e[c], o[c]) for c in range(3)]
            right = [mix(flip, o[c], e[c]) for c in range(3)]
            to_right, to_left = edges(rows)
            smooth, detail = lift(rows, left[:2], right[:2], first, last, mix)
            for y, v in enumerate(interleave(smooth, detail)):
                one[t, pl.ds(half * 128 + y, 8, stride=16), :] = v
            left2 = add_pairs(unpack_two(left[2]), own_left(to_left))
            right2 = add_pairs(unpack_two(right[2]), own_right(to_right))
            smooth, detail = lift(smooth, left2, right2, first, last, mix)
            for y, v in enumerate(interleave(smooth, detail)):
                two[t, pl.ds(half * 64 + y, 8, stride=8), :] = v

    times(TILES, column, TILES)
    flip = lax.axis_index("gz") % 2 == 1

    def stack(t):
        lanes = tile_lanes(t)
        going_right, going_left = [None] * 6, [None] * 6
        for half in range(2):
            rows = [one[t, pl.ds(z * 16 + half * 8, 8), :] for z in range(16)]
            to_right, to_left = edges(rows)
            for c in range(2):
                going_right[2 * c + half] = to_right[c]
                going_left[2 * c + half] = to_left[c]
        rows = [two[t, pl.ds(z * 8, 8), :] for z in range(16)]
        to_right, to_left = edges(rows)
        next_right, next_left = edges(lift_alone(rows))
        going_right[4:] = pack_two(*to_right, even), pack_two(*next_right, even)
        going_left[4:] = pack_two(*to_left, even), pack_two(*next_left, even)
        for c in range(6):
            pay_e[c, :, lanes] = mix(flip, going_left[c], going_right[c])
            pay_o[c, :, lanes] = mix(flip, going_right[c], going_left[c])

    times(TILES, stack, TILES)
    for t in range(TILES):
        for r in range(4):
            low, high = [two[t, pl.ds(64 * half + 2 * r, 8, stride=8), :] for half in range(2)]
            v = pack_two(low, high, even)
            thick[pl.ds(4 * r, 4), tile(t)] = v[0:4]
            thick[pl.ds(16 + 4 * r, 4), tile(t)] = v[4:8]
    for i in range(2):
        s, _ = lift_two(tiles_of(thick, pl.ds(8 * i, 8)), tiles_of(thick, pl.ds(16 + 8 * i, 8)), 2)
        put_tiles(cells, pl.ds(8 * i, 8), s)


def thin_z(weights3, weights4, cells, own, got, result, pay, w3, w4, beyond, held4, turned3, turned4, sem):
    mz = lax.axis_index("gz")
    loads = [
        pltpu.make_async_copy(weights3.at[mz], w3, sem.at[0]),
        pltpu.make_async_copy(weights4.at[mz], w4, sem.at[1]),
    ]
    for load in loads:
        load.start()
    me, count = lax.axis_index("gy"), got.shape[0]
    first, last = me == 0, me == count - 1
    near = lambda k: got[jnp.clip(me + k, 0, count - 1), :, 0:WIDE]
    beyond[0:8] = own[0:8] + (mix(me >= 1, near(-1), 0.0) + mix(me >= 2, near(-2), 0.0))
    beyond[8:16] = own[8:16] + (mix(me < count - 1, near(1), 0.0) + mix(me < count - 2, near(2), 0.0))
    four = got[0, :, WIDE:]
    for k in range(1, count):
        four = four + got[k, :, WIDE:]
    held4[:, 0 : WIDE // 2] = four[0:4]
    held4[:, WIDE // 2 :] = four[4:8]
    lane = lane_id((4, LANES))
    for t in range(TILES):
        at = lambda r: pl.ds(4 * r, 4)
        p, q, s, r = [beyond[at(c), tile(t)] for c in range(4)]
        rows = [cells[at(c), tile(t)] for c in range(4)]
        rows = interleave(*lift(rows, (p, q), (s, r), first, last, mix))
        for f in range(4):
            v = None
            for r in range(4):
                moved = pltpu.roll(rows[r], (r - f) % LANES, 1) if r != f else rows[r]
                v = jnp.where(lane % 4 == r, moved, v) if r else moved
            turned3[at(f), tile(t)] = v
        v = held4[:, tile(t)]
        for f in range(8):
            turned4[at(f), tile(t)] = pltpu.roll(v, LANES - f, 1) if f else v
    for load in loads:
        load.wait()
    count, half = pay.shape[0], WIDE // 2
    parts = [pl.ds(0, half), pl.ds(half, LANES)]
    sends = [pltpu.make_async_copy(pay.at[:, :, p], result.at[:, :, p], sem.at[2 + k]) for k, p in enumerate(parts)]
    three = jnp.dot(w3[...], turned3[...], precision=HIGH, preferred_element_type=jnp.float32)
    for to in range(count):
        pay[to, 0:4, 0:half] = three[to * 4 : to * 4 + 4, :half]
        pay[to, 4:8, 0:half] = three[to * 4 : to * 4 + 4, half:]
    sends[0].start()
    four = jnp.dot(w4[...], turned4[...], precision=HIGH, preferred_element_type=jnp.float32)
    lane = lane_id((count, LANES))
    for t in range(TILES):
        v = four[0:count, tile(t)]
        for k in range(1, 4):
            v = jnp.where(lane % 8 == k, pltpu.roll(four[k * count : (k + 1) * count, tile(t)], k, 1), v)
        pay[:, t, half:] = v
    sends[1].start()
    for send in sends:
        send.wait()


def along_z(one, two, got_e, got_o, result, fourth, out, fine, spread, sem):
    me = lax.axis_index("gz")
    first, last, flip = me == 0, me == lax.axis_size("gz") - 1, me % 2 == 1

    def stack(t):
        lanes = tile_lanes(t)
        e = [got_e[c, :, lanes] for c in range(6)]
        o = [got_o[c, :, lanes] for c in range(6)]
        left = [mix(flip, e[c], o[c]) for c in range(6)]
        right = [mix(flip, o[c], e[c]) for c in range(6)]
        for half in range(2):
            rows = [one[t, pl.ds(z * 16 + half * 8, 8), :] for z in range(16)]
            smooth, detail = lift(rows, left[half:4:2], right[half:4:2], first, last, mix)
            for z, v in enumerate(interleave(smooth, detail)):
                out[z, pl.ds(half * 8, 8), lanes] = v
        rows = [two[t, pl.ds(z * 8, 8), :] for z in range(16)]
        to_right, to_left = edges(rows)
        smooth, _ = lift(rows, unpack_two(left[4]), unpack_two(right[4]), first, last, mix)
        left2 = add_pairs(unpack_two(left[5]), own_left(to_left))
        right2 = add_pairs(unpack_two(right[5]), own_right(to_right))
        smooth, detail = lift(smooth, left2, right2, first, last, mix)
        for z, v in enumerate(interleave(smooth, detail)):
            fine[pl.ds(z * 8, 8), lanes] = v

    times(TILES, stack, TILES)
    sends = {z: pltpu.make_async_copy(out.at[z], result.at[z], sem.at[z]) for z in range(16) if z % 4}
    for z in range(1, 16, 2):
        sends[z].start()
    row = lax.broadcasted_iota(jnp.int32, (16, LANES), 0)
    here = (row % 2 == 0) & (lane_id((16, LANES)) % 2 == 0)
    for z in (1, 3, 5, 7, 0, 2, 4, 6):
        v = lift_runs(tiles_of(fine, pl.ds(z * 8, 8)), 2)
        for t in range(TILES):
            spread[t, pl.ds(z * 16, 8, stride=2), :] = v[t]
            w = jnp.where(here, spread[t, pl.ds(z * 16, 16), :], out[2 * z, :, tile(t)])
            if z % 2:
                out[2 * z, :, tile(t)] = w
            else:
                fourth[z // 2, :, tile(t)] = w
        if z % 2:
            sends[2 * z].start()
    for send in sends.values():
        send.wait()


def join(got, fourth, base, result, planes, spread, sem):
    half = WIDE // 2
    total = got[0]
    for k in range(1, got.shape[0]):
        total = total + got[k]
    three = [total[0:4, tile(t)] for t in range(TILES // 2)] + [total[4:8, tile(t)] for t in range(TILES // 2)]
    three = lift_runs(three, 4)
    four = lift_runs([total[t : t + 1, half:] for t in range(TILES)], 8)
    lane = lane_id((4, LANES))
    row = lax.broadcasted_iota(jnp.int32, (4, LANES), 0)
    for t in range(TILES):
        for r in range(4):
            v = pltpu.roll(three[t], LANES - r, 1) if r else three[t]
            for k in range(r // 2, 4, 2) if r % 2 == 0 else ():
                w = pltpu.roll(four[t], LANES - k, 1) if k else four[t]
                v = jnp.where((lane % 8 == 0) & (row == 2 * (k // 2)), jnp.broadcast_to(w, v.shape), v)
            spread[t, pl.ds(4 * r, 4, stride=16), :] = v
    row = lax.broadcasted_iota(jnp.int32, (16, LANES), 0)
    here = (row % 4 == 0) & (lane_id((16, LANES)) % 4 == 0)
    sends = [pltpu.make_async_copy(planes.at[i], result.at[4 * i], sem.at[i]) for i in range(4)]
    for i in range(4):
        for t in range(TILES):
            planes[i, :, tile(t)] = jnp.where(here, spread[t, pl.ds(i * 16, 16), :], fourth[i, :, tile(t)])
        sends[i].start()
    for send in sends:
        send.wait()


def deep_levels(n):
    fixed = lambda c, a, b: a if c else b
    level = lambda rows: lift(rows, (0.0, 0.0), (0.0, 0.0), True, True, fixed)
    cells = level(level(list(np.eye(n)))[0])[0]
    smooth, detail = level(cells)
    return cells, np.stack(interleave(smooth, detail)), np.stack(interleave(*level(smooth)))


def weights_y(devices):
    cells, _, four = deep_levels(16 * devices)
    w3 = np.zeros((devices, 48, 4, 16), np.float64)
    w4 = np.zeros((devices, devices, 2, 2, 2, 16), np.float64)
    for a in range(devices):
        mine = slice(16 * a, 16 * a + 16)
        for row, side, b in ((0, 0, -1), (8, 1, 1), (16, 0, 0), (24, 0, 1), (32, 1, 0), (40, 1, -1)):
            if 0 <= a + b < devices:
                pair = edges(cells[4 * (a + b) : 4 * (a + b) + 4])[side]
                for c in range(2):
                    for z in range(4):
                        w3[a, row + 4 * c + z, z] = pair[c][mine]
        for z in range(2):
            w4[a, :, :, z, z] = four[:, mine].reshape(devices, 2, 16)
    return (
        w3.reshape(devices, 48, 64).astype(np.float32),
        w4.reshape(devices, 4 * devices, 32).astype(np.float32),
    )


def weights_z(devices):
    _, three, four = deep_levels(16 * devices)
    w3 = np.zeros((devices, devices, 4, 4, 4), np.float64)
    w4 = np.zeros((devices, 2, 2, devices, 8, 2, 2), np.float64)
    for a in range(devices):
        for f in range(8):
            for zz in range(4):
                if f < 4:
                    z = 16 * a + zz + 4 * (f // 2) + 8 * (f % 2)
                    w3[a, :, :, f, zz] = three[:, z].reshape(devices, 4)
                if zz < 2:
                    z = 16 * a + zz + 2 * (f // 4) + 4 * (f // 2 % 2) + 8 * (f % 2)
                    for o in range(2):
                        w4[a, :, o, :, f, o, zz] = four[:, z].reshape(devices, 2).T
    return (
        w3.reshape(devices, 4 * devices, 16).astype(np.float32),
        w4.reshape(devices, 4 * devices, 32).astype(np.float32),
    )


def swap(values, axis, start):
    devices = lax.axis_size(axis)
    pairs = []
    for i in range(start, devices - 1, 2):
        pairs += [(i, i + 1), (i + 1, i)]
    return lax.ppermute(values, axis, pairs)


def f32(*shape):
    return jax.ShapeDtypeStruct(shape, jnp.float32)


def call(body, out, scratch=(), cost=4 << 20, **more):
    return pl.pallas_call(
        body,
        out_shape=out,
        scratch_shapes=list(scratch),
        cost_estimate=pl.CostEstimate(flops=cost * 10, bytes_accessed=4 << 20, transcendentals=0),
        compiler_params=pltpu.CompilerParams(vmem_limit_bytes=24 * 1024 * 1024),
        **more,
    )


def per_device(density):
    planes, rows, cells = density.shape
    ny, nz = lax.axis_size("gy"), lax.axis_size("gz")
    vmem = lambda *shape: pltpu.VMEM(shape, jnp.float32)
    sems = lambda count: pltpu.SemaphoreType.DMA((count,))
    far, here = pl.BlockSpec(memory_space=pltpu.HBM), pl.BlockSpec(memory_space=pltpu.VMEM)
    stay = lambda v: pltpu.with_memory_space_constraint(jnp.asarray(v), pltpu.HBM)
    tiled = f32(TILES, planes * rows, LANES)

    payload = f32(3, 16, cells)
    x, pay_e, pay_o, e1, y3, y4 = call(
        along_x,
        [tiled, payload, payload, f32(planes * rows // 2, cells), f32(48, 64), f32(4 * ny, 32)],
        [vmem(planes * rows, cells), sems(10)],
        in_specs=[far, far, far],
    )(*[stay(w) for w in weights_y(ny)], stay(density.reshape(planes * rows, cells)))
    got_e, got_o = swap(pay_e, "gy", 0), swap(pay_o, "gy", 1)
    pay = (ny, 8, cells * 3 // 2)
    own, pay = call(
        thin_y,
        [f32(16, cells), f32(*pay)],
        [vmem(*pay), vmem(64, cells), vmem(32, cells), sems(2)],
        cost=40 << 20,
        in_specs=[here, here, here],
        out_specs=[here, far],
    )(y3, y4, e1)
    got = lax.all_to_all(pay, "gy", 0, 0, tiled=True)

    payload = f32(6, 8, cells)
    one, two, pay_e, pay_o, third = call(
        along_y,
        [tiled, f32(TILES, planes * rows // 2, LANES), payload, payload, f32(16, cells)],
        [vmem(32, cells)],
        cost=400 << 20,
        input_output_aliases={0: 0},
    )(x, got_e, got_o)
    got_e, got_o = swap(pay_e, "gz", 0), swap(pay_o, "gz", 1)
    pay = (nz, 8, cells // 2 + LANES)
    pay = call(
        thin_z,
        f32(*pay),
        [
            vmem(*pay),
            vmem(4 * nz, 16),
            vmem(4 * nz, 32),
            vmem(16, cells),
            vmem(4, cells),
            vmem(16, cells),
            vmem(32, cells),
            sems(4),
        ],
        cost=40 << 20,
        in_specs=[far, far, here, here, here],
        out_specs=far,
    )(*[stay(w) for w in weights_z(nz)], third, own, got)
    got = lax.all_to_all(pay, "gz", 0, 0, tiled=True)

    base, fourth = call(
        along_z,
        [f32(planes, rows, cells), f32(planes // 4, rows, cells)],
        [vmem(planes, rows, cells), vmem(64, cells), vmem(TILES, 128, LANES), sems(planes)],
        cost=400 << 20,
        out_specs=[far, here],
    )(one, two, got_e, got_o)
    return call(
        join,
        f32(planes, rows, cells),
        [vmem(planes // 4, rows, cells), vmem(TILES, 64, LANES), sems(4)],
        in_specs=[here, here, far],
        out_specs=far,
        input_output_aliases={2: 0},
    )(got, fourth, stay(base))


def solution(mesh):
    return jax.shard_map(
        per_device, mesh=mesh, in_specs=(P("gz", "gy", None),), out_specs=P("gz", "gy", None), check_vma=False
    )
```

```python
import functools

import jax
import jax.numpy as jnp
import ml_dtypes
import numpy as np
from jax import lax
from jax.experimental import pallas as pl
from jax.experimental.pallas import tpu as pltpu
from jax.sharding import PartitionSpec as P

A1 = -1.586134342059924
B1 = -0.052980118572961
A2 = 0.882911075530934
B2 = 0.443506852043971
GAIN = 1.230174104914001

WIDE = 1024
LANES = 128
TILES = WIDE // LANES


def lift(rows, left, right, first, last, choose):
    p, q = left
    s_next, r = right
    smooth, detail = rows[0::2], rows[1::2]
    m = len(smooth)
    s_next = choose(last, smooth[-1], s_next)
    d1 = [detail[i] + A1 * (smooth[i] + (smooth[i + 1] if i + 1 < m else s_next)) for i in range(m)]
    d1_before = choose(first, d1[0], p + A1 * smooth[0])
    s1 = [smooth[i] + B1 * ((d1[i - 1] if i else d1_before) + d1[i]) for i in range(m)]
    s1_after = choose(last, s1[-1], r + B1 * d1[-1])
    d2 = [d1[i] + A2 * (s1[i] + (s1[i + 1] if i + 1 < m else s1_after)) for i in range(m)]
    d2_before = choose(first, d2[0], d1_before + A2 * (q + B1 * d1_before + s1[0]))
    s2 = [s1[i] + B2 * ((d2[i - 1] if i else d2_before) + d2[i]) for i in range(m)]
    return [v * (1.0 / GAIN) for v in s2], [v * (GAIN / 2.0) for v in d2]


def lift_alone(rows):
    zero = jnp.zeros_like(rows[0])
    return lift(rows, (zero, zero), (zero, zero), False, False, lambda c, a, b: a if c else b)[0]


def edges(rows):
    s, d = rows[0::2], rows[1::2]
    to_right = (d[-1] + A1 * s[-1], s[-1] + B1 * (d[-2] + A1 * (s[-2] + s[-1])))
    to_left = (s[0], s[0] + B1 * (d[0] + A1 * (s[0] + s[1])))
    return to_right, to_left


def own_left(to_left):
    s, r = to_left
    c2 = (B2 * A2 * B1 * A1 / GAIN) * s
    c1 = ((B1 * A1 + B2 * A1 + 3 * B2 * A2 * B1 * A1) / GAIN) * s + (B2 * A2 / GAIN) * r
    return c1 + A1 * c2, (1 + B1 * A1) * c2


def own_right(to_right):
    p, q = to_right
    c0 = ((B1 + B2 + 3 * B2 * A2 * B1) / GAIN) * p + (B2 * A2 / GAIN) * q
    c1 = (B2 * A2 * B1 / GAIN) * p
    return c0, c0 + B1 * (c1 + A1 * c0)


def add_pairs(a, b):
    return a[0] + b[0], a[1] + b[1]


def mix(flag, a, b):
    return jnp.where(flag, a, b)


def interleave(smooth, detail):
    return [v for pair in zip(smooth, detail) for v in pair]


def filters():
    fixed = lambda c, a, b: a if c else b
    smooth, detail = lift(list(np.eye(32)), (0.0, 0.0), (0.0, 0.0), True, True, fixed)
    return [float(v) for v in smooth[8][16:21]], [float(v) for v in detail[8][17:21]]


def moved(tiles, step):
    if step == 0:
        return list(tiles)
    lane, count = lane_id(tiles[0].shape), len(tiles)
    r = [pltpu.roll(x, -step % LANES, 1) for x in tiles]
    if step > 0:
        return [jnp.where(lane < LANES - step, r[t], r[t + 1]) if t + 1 < count else r[t] for t in range(count)]
    return [jnp.where(lane >= -step, r[t], r[t - 1]) if t else r[t] for t in range(count)]


def lift_runs(v, stride):
    run = lane_id(v[0].shape) // stride
    ends = LANES // stride - 1
    at = {k: moved(v, k * stride) for k in range(-4, 5)}
    for k in range(1, 5):
        for j in range(k):
            at[-k][0] = jnp.where(run == j, at[k - 2 * j][0], at[-k][0])
    for k in range(1, 5):
        for j in range(k):
            at[k][-1] = jnp.where(run == ends - j, at[2 * j - k][-1], at[k][-1])
    smooth, detail = filters()
    weight = [jnp.where(run % 2 == 0, a, b) for a, b in zip(smooth, detail + [0.0])]
    out = [weight[0] * x for x in v]
    for k in range(1, 5):
        out = [x + weight[k] * (y + z) for x, y, z in zip(out, at[-k], at[k])]
    return out


def split_left(w):
    parts = []
    for _ in range(3):
        parts.append((w - sum(p.astype(np.float32) for p in parts)).astype(ml_dtypes.bfloat16))
    one, two, three = parts
    return np.concatenate([one, one, two, one, two, three], axis=-1)


def product(left, x):
    one = x.astype(jnp.bfloat16)
    rest = x - one.astype(jnp.float32)
    two = rest.astype(jnp.bfloat16)
    three = (rest - two.astype(jnp.float32)).astype(jnp.bfloat16)
    right = jnp.concatenate([one, two, one, three, two, one], axis=0)
    return jnp.dot(left, right, preferred_element_type=jnp.float32)


def lane_id(shape):
    return lax.broadcasted_iota(jnp.int32, shape, len(shape) - 1)


def pack_two(a, b, even):
    return jnp.where(even, a, pltpu.roll(b, 1, 1))


def unpack_two(w):
    return w, pltpu.roll(w, LANES - 1, 1)


def tile(t):
    return slice(t * LANES, (t + 1) * LANES)


def times(count, body, unroll=1):
    if unroll == count:
        for i in range(count):
            body(i)
        return

    def step(i, carry):
        body(i)
        return carry

    lax.fori_loop(0, count, step, 0, unroll=unroll)


def tile_lanes(t):
    return pl.ds(t * LANES if isinstance(t, int) else pl.multiple_of(t * LANES, LANES), LANES)


def lift_two(a, b, phase):
    lane = lane_id((a[0].shape[0], LANES))
    here = lane % (2 * phase) < phase
    count, reach = len(a), 2 * phase
    s = [jnp.where(here, x, pltpu.roll(y, phase, 1)) for x, y in zip(a, b)]
    d = [jnp.where(here, pltpu.roll(x, LANES - phase, 1), y) for x, y in zip(a, b)]

    def ahead(x):
        r = [pltpu.roll(w, LANES - reach, 1) for w in x]
        return [jnp.where(lane < LANES - reach, r[t], r[t + 1] if t + 1 < count else x[t]) for t in range(count)]

    def behind(x):
        r = [pltpu.roll(w, reach, 1) for w in x]
        return [jnp.where(lane >= reach, r[t], r[t - 1] if t else x[t]) for t in range(count)]

    d = [x + A1 * (y + z) for x, y, z in zip(d, s, ahead(s))]
    s = [x + B1 * (y + z) for x, y, z in zip(s, d, behind(d))]
    d = [x + A2 * (y + z) for x, y, z in zip(d, s, ahead(s))]
    s = [(x + B2 * (y + z)) * (1.0 / GAIN) for x, y, z in zip(s, d, behind(d))]
    return s, [x * (GAIN / 2.0) for x in d]


def separate(s, d, phase):
    here = lane_id(s[0].shape) % (2 * phase) < phase
    a = [jnp.where(here, x, pltpu.roll(y, phase, 1)) for x, y in zip(s, d)]
    b = [jnp.where(here, pltpu.roll(x, LANES - phase, 1), y) for x, y in zip(s, d)]
    return a, b


def tiles_of(ref, at):
    v = ref[at, :]
    return [v[:, tile(t)] for t in range(TILES)]


def put_tiles(ref, at, parts):
    for t, v in enumerate(parts):
        ref[at, tile(t)] = v


def along_x(weights3, weights4, density, out, pay_e, pay_o, e1, w3, w4, x, sem):
    me = lax.axis_index("gy")

    def load(k):
        at = pl.ds(pl.multiple_of(k * 32, 32), 32)
        return pltpu.make_async_copy(density.at[at], x.at[at], sem.at[k])

    for k in range(4):
        load(k).start()
        load(k + 4).start()
    hints = [
        pltpu.make_async_copy(weights3.at[me], w3, sem.at[8]),
        pltpu.make_async_copy(weights4.at[me], w4, sem.at[9]),
    ]
    for hint in hints:
        hint.start()

    def plane(i):
        z, y = i // 2, i % 2
        at = pl.multiple_of(z * 16 + y * 8, 8)
        far = pl.multiple_of(z * 16 + y * 8 + 128, 8)
        s, d = lift_two(tiles_of(x, pl.ds(at, 8)), tiles_of(x, pl.ds(far, 8)), 1)
        put_tiles(e1, pl.ds(at, 8), s)
        a, b = separate(s, d, 1)
        for t in range(TILES):
            out[t, pl.ds(at, 8), :] = a[t]
            out[t, pl.ds(far, 8), :] = b[t]

    def group(k):
        load(k).wait()
        load(k + 4).wait()
        for i in range(4):
            plane(4 * k + i)

    times(4, group)
    flip = me % 2 == 1
    even = lane_id((8, LANES)) % 2 == 0

    def column(t):
        lanes = tile_lanes(t)
        for half in range(2):
            rows = [out[t, pl.ds(half * 128 + y, 8, stride=16), :] for y in range(16)]
            to_right, to_left = edges(rows)
            next_right, next_left = edges(lift_alone(rows))
            going_right = to_right + (pack_two(*next_right, even),)
            going_left = to_left + (pack_two(*next_left, even),)
            for c in range(3):
                pay_e[c, pl.ds(half * 8, 8), lanes] = mix(flip, going_left[c], going_right[c])
                pay_o[c, pl.ds(half * 8, 8), lanes] = mix(flip, going_right[c], going_left[c])

    times(TILES, column, 4)
    for hint in hints:
        hint.wait()


def thin_y(w3, w4, e1, own, result, pay, e2, e3, sem):
    me = lax.axis_index("gy")

    def second(i):
        at = pl.multiple_of(i * 8, 8)
        s, _ = lift_two(tiles_of(e1, pl.ds(at, 8)), tiles_of(e1, pl.ds(at + 64, 8)), 2)
        put_tiles(e2, pl.ds(at, 8), s)

    times(8, second, 8)
    three = product(w3[...], e2[...])
    own[...] = three[0:16]
    for to in range(pay.shape[0]):
        right = mix(to == me + 1, three[16:24], three[24:32])
        left = mix(to == me - 1, three[32:40], three[40:48])
        pay[to, :, 0:WIDE] = mix(to > me, right, left)
    parts = [pl.ds(0, WIDE), pl.ds(WIDE, WIDE // 2)]
    sends = [pltpu.make_async_copy(pay.at[:, :, p], result.at[:, :, p], sem.at[k]) for k, p in enumerate(parts)]
    sends[0].start()

    def third(i):
        at = pl.multiple_of(i * 8, 8)
        s, _ = lift_two(tiles_of(e2, pl.ds(at, 8)), tiles_of(e2, pl.ds(at + 32, 8)), 4)
        put_tiles(e3, pl.ds(at, 8), s)

    times(4, third, 4)
    four = product(w4[...], e3[...])
    for to in range(pay.shape[0]):
        pay[to, 0:4, WIDE:] = four[to * 4 : to * 4 + 4, : WIDE // 2]
        pay[to, 4:8, WIDE:] = four[to * 4 : to * 4 + 4, WIDE // 2 :]
    sends[1].start()
    for send in sends:
        send.wait()


def along_y(x, got_e, got_o, one, two, pay_e, pay_o, cells, thick):
    me = lax.axis_index("gy")
    first, last, flip = me == 0, me == lax.axis_size("gy") - 1, me % 2 == 1
    even = lane_id((8, LANES)) % 2 == 0

    def column(t):
        lanes = tile_lanes(t)
        for half in range(2):
            rows = [x[t, pl.ds(half * 128 + y, 8, stride=16), :] for y in range(16)]
            e = [got_e[c, pl.ds(half * 8, 8), lanes] for c in range(3)]
            o = [got_o[c, pl.ds(half * 8, 8), lanes] for c in range(3)]
            left = [mix(flip, e[c], o[c]) for c in range(3)]
            right = [mix(flip, o[c], e[c]) for c in range(3)]
            to_right, to_left = edges(rows)
            smooth, detail = lift(rows, left[:2], right[:2], first, last, mix)
            for y, v in enumerate(interleave(smooth, detail)):
                one[t, pl.ds(half * 128 + y, 8, stride=16), :] = v
            left2 = add_pairs(unpack_two(left[2]), own_left(to_left))
            right2 = add_pairs(unpack_two(right[2]), own_right(to_right))
            smooth, detail = lift(smooth, left2, right2, first, last, mix)
            for y, v in enumerate(interleave(smooth, detail)):
                two[t, pl.ds(half * 64 + y, 8, stride=8), :] = v

    times(TILES, column, TILES)
    flip = lax.axis_index("gz") % 2 == 1

    def stack(t):
        lanes = tile_lanes(t)
        going_right, going_left = [None] * 6, [None] * 6
        for half in range(2):
            rows = [one[t, pl.ds(z * 16 + half * 8, 8), :] for z in range(16)]
            to_right, to_left = edges(rows)
            for c in range(2):
                going_right[2 * c + half] = to_right[c]
                going_left[2 * c + half] = to_left[c]
        rows = [two[t, pl.ds(z * 8, 8), :] for z in range(16)]
        to_right, to_left = edges(rows)
        next_right, next_left = edges(lift_alone(rows))
        going_right[4:] = pack_two(*to_right, even), pack_two(*next_right, even)
        going_left[4:] = pack_two(*to_left, even), pack_two(*next_left, even)
        for c in range(6):
            pay_e[c, :, lanes] = mix(flip, going_left[c], going_right[c])
            pay_o[c, :, lanes] = mix(flip, going_right[c], going_left[c])

    times(TILES, stack, TILES)
    for t in range(TILES):
        for r in range(4):
            low, high = [two[t, pl.ds(64 * half + 2 * r, 8, stride=8), :] for half in range(2)]
            v = pack_two(low, high, even)
            thick[pl.ds(4 * r, 4), tile(t)] = v[0:4]
            thick[pl.ds(16 + 4 * r, 4), tile(t)] = v[4:8]
    for i in range(2):
        s, _ = lift_two(tiles_of(thick, pl.ds(8 * i, 8)), tiles_of(thick, pl.ds(16 + 8 * i, 8)), 2)
        put_tiles(cells, pl.ds(8 * i, 8), s)


def thin_z(weights3, weights4, cells, own, got, result, pay, w3, w4, beyond, held4, turned3, turned4, sem):
    mz = lax.axis_index("gz")
    loads = [
        pltpu.make_async_copy(weights3.at[mz], w3, sem.at[0]),
        pltpu.make_async_copy(weights4.at[mz], w4, sem.at[1]),
    ]
    for load in loads:
        load.start()
    me, count = lax.axis_index("gy"), got.shape[0]
    first, last = me == 0, me == count - 1
    near = lambda k: got[jnp.clip(me + k, 0, count - 1), :, 0:WIDE]
    beyond[0:8] = own[0:8] + (mix(me >= 1, near(-1), 0.0) + mix(me >= 2, near(-2), 0.0))
    beyond[8:16] = own[8:16] + (mix(me < count - 1, near(1), 0.0) + mix(me < count - 2, near(2), 0.0))
    four = got[0, :, WIDE:]
    for k in range(1, count):
        four = four + got[k, :, WIDE:]
    held4[:, 0 : WIDE // 2] = four[0:4]
    held4[:, WIDE // 2 :] = four[4:8]
    lane = lane_id((4, LANES))
    for t in range(TILES):
        at = lambda r: pl.ds(4 * r, 4)
        p, q, s, r = [beyond[at(c), tile(t)] for c in range(4)]
        rows = [cells[at(c), tile(t)] for c in range(4)]
        rows = interleave(*lift(rows, (p, q), (s, r), first, last, mix))
        for f in range(4):
            v = None
            for r in range(4):
                moved = pltpu.roll(rows[r], (r - f) % LANES, 1) if r != f else rows[r]
                v = jnp.where(lane % 4 == r, moved, v) if r else moved
            turned3[at(f), tile(t)] = v
        v = held4[:, tile(t)]
        for f in range(8):
            turned4[at(f), tile(t)] = pltpu.roll(v, LANES - f, 1) if f else v
    for load in loads:
        load.wait()
    count, half = pay.shape[0], WIDE // 2
    parts = [pl.ds(0, half), pl.ds(half, LANES)]
    sends = [pltpu.make_async_copy(pay.at[:, :, p], result.at[:, :, p], sem.at[2 + k]) for k, p in enumerate(parts)]
    three = product(w3[...], turned3[...])
    for to in range(count):
        pay[to, 0:4, 0:half] = three[to * 4 : to * 4 + 4, :half]
        pay[to, 4:8, 0:half] = three[to * 4 : to * 4 + 4, half:]
    sends[0].start()
    four = product(w4[...], turned4[...])
    lane = lane_id((count, LANES))
    for t in range(TILES):
        v = four[0:count, tile(t)]
        for k in range(1, 4):
            v = jnp.where(lane % 8 == k, pltpu.roll(four[k * count : (k + 1) * count, tile(t)], k, 1), v)
        pay[:, t, half:] = v
    sends[1].start()
    for send in sends:
        send.wait()


def along_z(one, two, got_e, got_o, result, fourth, out, fine, spread, sem):
    me = lax.axis_index("gz")
    first, last, flip = me == 0, me == lax.axis_size("gz") - 1, me % 2 == 1

    def stack(t):
        lanes = tile_lanes(t)
        e = [got_e[c, :, lanes] for c in range(6)]
        o = [got_o[c, :, lanes] for c in range(6)]
        left = [mix(flip, e[c], o[c]) for c in range(6)]
        right = [mix(flip, o[c], e[c]) for c in range(6)]
        for half in range(2):
            rows = [one[t, pl.ds(z * 16 + half * 8, 8), :] for z in range(16)]
            smooth, detail = lift(rows, left[half:4:2], right[half:4:2], first, last, mix)
            for z, v in enumerate(interleave(smooth, detail)):
                out[z, pl.ds(half * 8, 8), lanes] = v
        rows = [two[t, pl.ds(z * 8, 8), :] for z in range(16)]
        to_right, to_left = edges(rows)
        smooth, _ = lift(rows, unpack_two(left[4]), unpack_two(right[4]), first, last, mix)
        left2 = add_pairs(unpack_two(left[5]), own_left(to_left))
        right2 = add_pairs(unpack_two(right[5]), own_right(to_right))
        smooth, detail = lift(smooth, left2, right2, first, last, mix)
        for z, v in enumerate(interleave(smooth, detail)):
            fine[pl.ds(z * 8, 8), lanes] = v

    times(TILES, stack, TILES)
    sends = {z: pltpu.make_async_copy(out.at[z], result.at[z], sem.at[z]) for z in range(16) if z % 4}
    for z in range(1, 16, 2):
        sends[z].start()
    row = lax.broadcasted_iota(jnp.int32, (16, LANES), 0)
    here = (row % 2 == 0) & (lane_id((16, LANES)) % 2 == 0)
    for z in (1, 3, 5, 7, 0, 2, 4, 6):
        v = lift_runs(tiles_of(fine, pl.ds(z * 8, 8)), 2)
        for t in range(TILES):
            spread[t, pl.ds(z * 16, 8, stride=2), :] = v[t]
            w = jnp.where(here, spread[t, pl.ds(z * 16, 16), :], out[2 * z, :, tile(t)])
            if z % 2:
                out[2 * z, :, tile(t)] = w
            else:
                fourth[z // 2, :, tile(t)] = w
        if z % 2:
            sends[2 * z].start()
    for send in sends.values():
        send.wait()


def join(got, fourth, base, result, planes, spread, sem):
    half = WIDE // 2
    total = got[0]
    for k in range(1, got.shape[0]):
        total = total + got[k]
    three = [total[0:4, tile(t)] for t in range(TILES // 2)] + [total[4:8, tile(t)] for t in range(TILES // 2)]
    three = lift_runs(three, 4)
    four = lift_runs([total[t : t + 1, half:] for t in range(TILES)], 8)
    lane = lane_id((4, LANES))
    row = lax.broadcasted_iota(jnp.int32, (4, LANES), 0)
    for t in range(TILES):
        for r in range(4):
            v = pltpu.roll(three[t], LANES - r, 1) if r else three[t]
            for k in range(r // 2, 4, 2) if r % 2 == 0 else ():
                w = pltpu.roll(four[t], LANES - k, 1) if k else four[t]
                v = jnp.where((lane % 8 == 0) & (row == 2 * (k // 2)), jnp.broadcast_to(w, v.shape), v)
            spread[t, pl.ds(4 * r, 4, stride=16), :] = v
    row = lax.broadcasted_iota(jnp.int32, (16, LANES), 0)
    here = (row % 4 == 0) & (lane_id((16, LANES)) % 4 == 0)
    sends = [pltpu.make_async_copy(planes.at[i], result.at[4 * i], sem.at[i]) for i in range(4)]
    for i in range(4):
        for t in range(TILES):
            planes[i, :, tile(t)] = jnp.where(here, spread[t, pl.ds(i * 16, 16), :], fourth[i, :, tile(t)])
        sends[i].start()
    for send in sends:
        send.wait()


def deep_levels(n):
    fixed = lambda c, a, b: a if c else b
    level = lambda rows: lift(rows, (0.0, 0.0), (0.0, 0.0), True, True, fixed)
    cells = level(level(list(np.eye(n)))[0])[0]
    smooth, detail = level(cells)
    return cells, np.stack(interleave(smooth, detail)), np.stack(interleave(*level(smooth)))


def weights_y(devices):
    cells, _, four = deep_levels(16 * devices)
    w3 = np.zeros((devices, 48, 4, 16), np.float64)
    w4 = np.zeros((devices, devices, 2, 2, 2, 16), np.float64)
    for a in range(devices):
        mine = slice(16 * a, 16 * a + 16)
        for row, side, b in ((0, 0, -1), (8, 1, 1), (16, 0, 0), (24, 0, 1), (32, 1, 0), (40, 1, -1)):
            if 0 <= a + b < devices:
                pair = edges(cells[4 * (a + b) : 4 * (a + b) + 4])[side]
                for c in range(2):
                    for z in range(4):
                        w3[a, row + 4 * c + z, z] = pair[c][mine]
        for z in range(2):
            w4[a, :, :, z, z] = four[:, mine].reshape(devices, 2, 16)
    return (
        split_left(w3.reshape(devices, 48, 64).astype(np.float32)),
        split_left(w4.reshape(devices, 4 * devices, 32).astype(np.float32)),
    )


def weights_z(devices):
    _, three, four = deep_levels(16 * devices)
    w3 = np.zeros((devices, devices, 4, 4, 4), np.float64)
    w4 = np.zeros((devices, 2, 2, devices, 8, 2, 2), np.float64)
    for a in range(devices):
        for f in range(8):
            for zz in range(4):
                if f < 4:
                    z = 16 * a + zz + 4 * (f // 2) + 8 * (f % 2)
                    w3[a, :, :, f, zz] = three[:, z].reshape(devices, 4)
                if zz < 2:
                    z = 16 * a + zz + 2 * (f // 4) + 4 * (f // 2 % 2) + 8 * (f % 2)
                    for o in range(2):
                        w4[a, :, o, :, f, o, zz] = four[:, z].reshape(devices, 2).T
    return (
        split_left(w3.reshape(devices, 4 * devices, 16).astype(np.float32)),
        split_left(w4.reshape(devices, 4 * devices, 32).astype(np.float32)),
    )


def swap(values, axis, start):
    devices = lax.axis_size(axis)
    pairs = []
    for i in range(start, devices - 1, 2):
        pairs += [(i, i + 1), (i + 1, i)]
    return lax.ppermute(values, axis, pairs)


def f32(*shape):
    return jax.ShapeDtypeStruct(shape, jnp.float32)


def bf16(*shape):
    return jax.ShapeDtypeStruct(shape, jnp.bfloat16)


def call(body, out, scratch=(), cost=4 << 20, **more):
    return pl.pallas_call(
        body,
        out_shape=out,
        scratch_shapes=list(scratch),
        cost_estimate=pl.CostEstimate(flops=cost * 10, bytes_accessed=4 << 20, transcendentals=0),
        compiler_params=pltpu.CompilerParams(vmem_limit_bytes=24 * 1024 * 1024),
        **more,
    )


def per_device(density):
    planes, rows, cells = density.shape
    ny, nz = lax.axis_size("gy"), lax.axis_size("gz")
    vmem = lambda *shape: pltpu.VMEM(shape, jnp.float32)
    sems = lambda count: pltpu.SemaphoreType.DMA((count,))
    far, here = pl.BlockSpec(memory_space=pltpu.HBM), pl.BlockSpec(memory_space=pltpu.VMEM)
    stay = lambda v: pltpu.with_memory_space_constraint(jnp.asarray(v), pltpu.HBM)
    tiled = f32(TILES, planes * rows, LANES)

    payload = f32(3, 16, cells)
    x, pay_e, pay_o, e1, y3, y4 = call(
        along_x,
        [tiled, payload, payload, f32(planes * rows // 2, cells), bf16(48, 6 * 64), bf16(4 * ny, 6 * 32)],
        [vmem(planes * rows, cells), sems(10)],
        in_specs=[far, far, far],
    )(*[stay(w) for w in weights_y(ny)], stay(density.reshape(planes * rows, cells)))
    got_e, got_o = swap(pay_e, "gy", 0), swap(pay_o, "gy", 1)
    pay = (ny, 8, cells * 3 // 2)
    own, pay = call(
        thin_y,
        [f32(16, cells), f32(*pay)],
        [vmem(*pay), vmem(64, cells), vmem(32, cells), sems(2)],
        cost=40 << 20,
        in_specs=[here, here, here],
        out_specs=[here, far],
    )(y3, y4, e1)
    got = lax.all_to_all(pay, "gy", 0, 0, tiled=True)

    payload = f32(6, 8, cells)
    one, two, pay_e, pay_o, third = call(
        along_y,
        [tiled, f32(TILES, planes * rows // 2, LANES), payload, payload, f32(16, cells)],
        [vmem(32, cells)],
        cost=400 << 20,
        input_output_aliases={0: 0},
    )(x, got_e, got_o)
    got_e, got_o = swap(pay_e, "gz", 0), swap(pay_o, "gz", 1)
    pay = (nz, 8, cells // 2 + LANES)
    pay = call(
        thin_z,
        f32(*pay),
        [
            vmem(*pay),
            pltpu.VMEM((4 * nz, 6 * 16), jnp.bfloat16),
            pltpu.VMEM((4 * nz, 6 * 32), jnp.bfloat16),
            vmem(16, cells),
            vmem(4, cells),
            vmem(16, cells),
            vmem(32, cells),
            sems(4),
        ],
        cost=40 << 20,
        in_specs=[far, far, here, here, here],
        out_specs=far,
    )(*[stay(w) for w in weights_z(nz)], third, own, got)
    got = lax.all_to_all(pay, "gz", 0, 0, tiled=True)

    base, fourth = call(
        along_z,
        [f32(planes, rows, cells), f32(planes // 4, rows, cells)],
        [vmem(planes, rows, cells), vmem(64, cells), vmem(TILES, 128, LANES), sems(planes)],
        cost=400 << 20,
        out_specs=[far, here],
    )(one, two, got_e, got_o)
    return call(
        join,
        f32(planes, rows, cells),
        [vmem(planes // 4, rows, cells), vmem(TILES, 64, LANES), sems(4)],
        in_specs=[here, here, far],
        out_specs=far,
        input_output_aliases={2: 0},
    )(got, fourth, stay(base))


def solution(mesh):
    return jax.shard_map(
        per_device, mesh=mesh, in_specs=(P("gz", "gy", None),), out_specs=P("gz", "gy", None), check_vma=False
    )
```

```python
import functools

import jax
import jax.numpy as jnp
import ml_dtypes
import numpy as np
from jax import lax
from jax.experimental import pallas as pl
from jax.experimental.pallas import tpu as pltpu
from jax.sharding import PartitionSpec as P

A1 = -1.586134342059924
B1 = -0.052980118572961
A2 = 0.882911075530934
B2 = 0.443506852043971
GAIN = 1.230174104914001

WIDE = 1024
LANES = 128
TILES = WIDE // LANES


def lift(rows, left, right, first, last, choose):
    p, q = left
    s_next, r = right
    smooth, detail = rows[0::2], rows[1::2]
    m = len(smooth)
    s_next = choose(last, smooth[-1], s_next)
    d1 = [detail[i] + A1 * (smooth[i] + (smooth[i + 1] if i + 1 < m else s_next)) for i in range(m)]
    d1_before = choose(first, d1[0], p + A1 * smooth[0])
    s1 = [smooth[i] + B1 * ((d1[i - 1] if i else d1_before) + d1[i]) for i in range(m)]
    s1_after = choose(last, s1[-1], r + B1 * d1[-1])
    d2 = [d1[i] + A2 * (s1[i] + (s1[i + 1] if i + 1 < m else s1_after)) for i in range(m)]
    d2_before = choose(first, d2[0], d1_before + A2 * (q + B1 * d1_before + s1[0]))
    s2 = [s1[i] + B2 * ((d2[i - 1] if i else d2_before) + d2[i]) for i in range(m)]
    return [v * (1.0 / GAIN) for v in s2], [v * (GAIN / 2.0) for v in d2]


def lift_alone(rows):
    zero = jnp.zeros_like(rows[0])
    return lift(rows, (zero, zero), (zero, zero), False, False, lambda c, a, b: a if c else b)[0]


def edges(rows):
    s, d = rows[0::2], rows[1::2]
    to_right = (d[-1] + A1 * s[-1], s[-1] + B1 * (d[-2] + A1 * (s[-2] + s[-1])))
    to_left = (s[0], s[0] + B1 * (d[0] + A1 * (s[0] + s[1])))
    return to_right, to_left


def own_left(to_left):
    s, r = to_left
    c2 = (B2 * A2 * B1 * A1 / GAIN) * s
    c1 = ((B1 * A1 + B2 * A1 + 3 * B2 * A2 * B1 * A1) / GAIN) * s + (B2 * A2 / GAIN) * r
    return c1 + A1 * c2, (1 + B1 * A1) * c2


def own_right(to_right):
    p, q = to_right
    c0 = ((B1 + B2 + 3 * B2 * A2 * B1) / GAIN) * p + (B2 * A2 / GAIN) * q
    c1 = (B2 * A2 * B1 / GAIN) * p
    return c0, c0 + B1 * (c1 + A1 * c0)


def add_pairs(a, b):
    return a[0] + b[0], a[1] + b[1]


def mix(flag, a, b):
    return jnp.where(flag, a, b)


def interleave(smooth, detail):
    return [v for pair in zip(smooth, detail) for v in pair]


def filters():
    fixed = lambda c, a, b: a if c else b
    smooth, detail = lift(list(np.eye(32)), (0.0, 0.0), (0.0, 0.0), True, True, fixed)
    return [float(v) for v in smooth[8][16:21]], [float(v) for v in detail[8][17:21]]


def moved(tiles, step):
    if step == 0:
        return list(tiles)
    lane, count = lane_id(tiles[0].shape), len(tiles)
    r = [pltpu.roll(x, -step % LANES, 1) for x in tiles]
    if step > 0:
        return [jnp.where(lane < LANES - step, r[t], r[t + 1]) if t + 1 < count else r[t] for t in range(count)]
    return [jnp.where(lane >= -step, r[t], r[t - 1]) if t else r[t] for t in range(count)]


def lift_runs(v, stride):
    run = lane_id(v[0].shape) // stride
    ends = LANES // stride - 1
    at = {k: moved(v, k * stride) for k in range(-4, 5)}
    for k in range(1, 5):
        for j in range(k):
            at[-k][0] = jnp.where(run == j, at[k - 2 * j][0], at[-k][0])
    for k in range(1, 5):
        for j in range(k):
            at[k][-1] = jnp.where(run == ends - j, at[2 * j - k][-1], at[k][-1])
    smooth, detail = filters()
    weight = [jnp.where(run % 2 == 0, a, b) for a, b in zip(smooth, detail + [0.0])]
    out = [weight[0] * x for x in v]
    for k in range(1, 5):
        out = [x + weight[k] * (y + z) for x, y, z in zip(out, at[-k], at[k])]
    return out


def split_left(w):
    parts = []
    for _ in range(3):
        parts.append((w - sum(p.astype(np.float32) for p in parts)).astype(ml_dtypes.bfloat16))
    one, two, three = parts
    return np.concatenate([one, one, two, one, two, three], axis=-1)


def product(left, x):
    one = x.astype(jnp.bfloat16)
    rest = x - one.astype(jnp.float32)
    two = rest.astype(jnp.bfloat16)
    three = (rest - two.astype(jnp.float32)).astype(jnp.bfloat16)
    right = jnp.concatenate([one, two, one, three, two, one], axis=0)
    return jnp.dot(left, right, preferred_element_type=jnp.float32)


def lane_id(shape):
    return lax.broadcasted_iota(jnp.int32, shape, len(shape) - 1)


def pack_two(a, b, even):
    return jnp.where(even, a, pltpu.roll(b, 1, 1))


def unpack_two(w):
    return w, pltpu.roll(w, LANES - 1, 1)


def tile(t):
    return slice(t * LANES, (t + 1) * LANES)


def times(count, body, unroll=1):
    if unroll == count:
        for i in range(count):
            body(i)
        return

    def step(i, carry):
        body(i)
        return carry

    lax.fori_loop(0, count, step, 0, unroll=unroll)


def tile_lanes(t):
    return pl.ds(t * LANES if isinstance(t, int) else pl.multiple_of(t * LANES, LANES), LANES)


def lift_two(a, b, phase):
    lane = lane_id((a[0].shape[0], LANES))
    here = lane % (2 * phase) < phase
    count, reach = len(a), 2 * phase
    s = [jnp.where(here, x, pltpu.roll(y, phase, 1)) for x, y in zip(a, b)]
    d = [jnp.where(here, pltpu.roll(x, LANES - phase, 1), y) for x, y in zip(a, b)]

    def ahead(x):
        r = [pltpu.roll(w, LANES - reach, 1) for w in x]
        return [jnp.where(lane < LANES - reach, r[t], r[t + 1] if t + 1 < count else x[t]) for t in range(count)]

    def behind(x):
        r = [pltpu.roll(w, reach, 1) for w in x]
        return [jnp.where(lane >= reach, r[t], r[t - 1] if t else x[t]) for t in range(count)]

    d = [x + A1 * (y + z) for x, y, z in zip(d, s, ahead(s))]
    s = [x + B1 * (y + z) for x, y, z in zip(s, d, behind(d))]
    d = [x + A2 * (y + z) for x, y, z in zip(d, s, ahead(s))]
    s = [(x + B2 * (y + z)) * (1.0 / GAIN) for x, y, z in zip(s, d, behind(d))]
    return s, [x * (GAIN / 2.0) for x in d]


def separate(s, d, phase):
    here = lane_id(s[0].shape) % (2 * phase) < phase
    a = [jnp.where(here, x, pltpu.roll(y, phase, 1)) for x, y in zip(s, d)]
    b = [jnp.where(here, pltpu.roll(x, LANES - phase, 1), y) for x, y in zip(s, d)]
    return a, b


def tiles_of(ref, at):
    v = ref[at, :]
    return [v[:, tile(t)] for t in range(TILES)]


def put_tiles(ref, at, parts):
    for t, v in enumerate(parts):
        ref[at, tile(t)] = v


def along_x(weights3, weights4, density, out, pay_e, pay_o, e1, w3, w4, x, sem):
    me = lax.axis_index("gy")

    def load(k):
        at = pl.ds(pl.multiple_of(k * 32, 32), 32)
        return pltpu.make_async_copy(density.at[at], x.at[at], sem.at[k])

    for k in range(4):
        load(k).start()
        load(k + 4).start()
    hints = [
        pltpu.make_async_copy(weights3.at[me], w3, sem.at[8]),
        pltpu.make_async_copy(weights4.at[me], w4, sem.at[9]),
    ]
    for hint in hints:
        hint.start()

    def plane(i):
        z, y = i // 2, i % 2
        at = pl.multiple_of(z * 16 + y * 8, 8)
        far = pl.multiple_of(z * 16 + y * 8 + 128, 8)
        s, d = lift_two(tiles_of(x, pl.ds(at, 8)), tiles_of(x, pl.ds(far, 8)), 1)
        put_tiles(e1, pl.ds(at, 8), s)
        a, b = separate(s, d, 1)
        for t in range(TILES):
            out[t, pl.ds(at, 8), :] = a[t]
            out[t, pl.ds(far, 8), :] = b[t]

    def group(k):
        load(k).wait()
        load(k + 4).wait()
        for i in range(4):
            plane(4 * k + i)

    times(4, group)
    flip = me % 2 == 1
    even = lane_id((8, LANES)) % 2 == 0

    def column(t):
        lanes = tile_lanes(t)
        for half in range(2):
            rows = [out[t, pl.ds(half * 128 + y, 8, stride=16), :] for y in range(16)]
            to_right, to_left = edges(rows)
            next_right, next_left = edges(lift_alone(rows))
            going_right = to_right + (pack_two(*next_right, even),)
            going_left = to_left + (pack_two(*next_left, even),)
            for c in range(3):
                pay_e[c, pl.ds(half * 8, 8), lanes] = mix(flip, going_left[c], going_right[c])
                pay_o[c, pl.ds(half * 8, 8), lanes] = mix(flip, going_right[c], going_left[c])

    times(TILES, column, 4)
    for hint in hints:
        hint.wait()


def thin_y(w3, w4, e1, own, result, pay, e2, e3, sem):
    me = lax.axis_index("gy")

    def second(i):
        at = pl.multiple_of(i * 8, 8)
        s, _ = lift_two(tiles_of(e1, pl.ds(at, 8)), tiles_of(e1, pl.ds(at + 64, 8)), 2)
        put_tiles(e2, pl.ds(at, 8), s)

    times(8, second, 8)
    def third(i):
        at = pl.multiple_of(i * 8, 8)
        s, _ = lift_two(tiles_of(e2, pl.ds(at, 8)), tiles_of(e2, pl.ds(at + 32, 8)), 4)
        put_tiles(e3, pl.ds(at, 8), s)

    times(4, third, 4)
    three = product(w3[...], e2[...])
    four = product(w4[...], e3[...])
    own[...] = three[0:16]
    for to in range(pay.shape[0]):
        right = mix(to == me + 1, three[16:24], three[24:32])
        left = mix(to == me - 1, three[32:40], three[40:48])
        pay[to, :, 0:WIDE] = mix(to > me, right, left)
    parts = [pl.ds(0, WIDE), pl.ds(WIDE, WIDE // 2)]
    sends = [pltpu.make_async_copy(pay.at[:, :, p], result.at[:, :, p], sem.at[k]) for k, p in enumerate(parts)]
    sends[0].start()

    for to in range(pay.shape[0]):
        pay[to, 0:4, WIDE:] = four[to * 4 : to * 4 + 4, : WIDE // 2]
        pay[to, 4:8, WIDE:] = four[to * 4 : to * 4 + 4, WIDE // 2 :]
    sends[1].start()
    for send in sends:
        send.wait()


def along_y(weights3, weights4, x, got_e, got_o, one, two, pay_e, pay_o, cells, w3, w4, thick, sem):
    mz = lax.axis_index("gz")
    hints = [
        pltpu.make_async_copy(weights3.at[mz], w3, sem.at[0]),
        pltpu.make_async_copy(weights4.at[mz], w4, sem.at[1]),
    ]
    for hint in hints:
        hint.start()
    me = lax.axis_index("gy")
    first, last, flip = me == 0, me == lax.axis_size("gy") - 1, me % 2 == 1
    even = lane_id((8, LANES)) % 2 == 0

    def column(t):
        lanes = tile_lanes(t)
        for half in range(2):
            rows = [x[t, pl.ds(half * 128 + y, 8, stride=16), :] for y in range(16)]
            e = [got_e[c, pl.ds(half * 8, 8), lanes] for c in range(3)]
            o = [got_o[c, pl.ds(half * 8, 8), lanes] for c in range(3)]
            left = [mix(flip, e[c], o[c]) for c in range(3)]
            right = [mix(flip, o[c], e[c]) for c in range(3)]
            to_right, to_left = edges(rows)
            smooth, detail = lift(rows, left[:2], right[:2], first, last, mix)
            for y, v in enumerate(interleave(smooth, detail)):
                one[t, pl.ds(half * 128 + y, 8, stride=16), :] = v
            left2 = add_pairs(unpack_two(left[2]), own_left(to_left))
            right2 = add_pairs(unpack_two(right[2]), own_right(to_right))
            smooth, detail = lift(smooth, left2, right2, first, last, mix)
            for y, v in enumerate(interleave(smooth, detail)):
                two[t, pl.ds(half * 64 + y, 8, stride=8), :] = v

    times(TILES, column, TILES)
    flip = mz % 2 == 1

    def stack(t):
        lanes = tile_lanes(t)
        going_right, going_left = [None] * 6, [None] * 6
        for half in range(2):
            rows = [one[t, pl.ds(z * 16 + half * 8, 8), :] for z in range(16)]
            to_right, to_left = edges(rows)
            for c in range(2):
                going_right[2 * c + half] = to_right[c]
                going_left[2 * c + half] = to_left[c]
        rows = [two[t, pl.ds(z * 8, 8), :] for z in range(16)]
        to_right, to_left = edges(rows)
        next_right, next_left = edges(lift_alone(rows))
        going_right[4:] = pack_two(*to_right, even), pack_two(*next_right, even)
        going_left[4:] = pack_two(*to_left, even), pack_two(*next_left, even)
        for c in range(6):
            pay_e[c, :, lanes] = mix(flip, going_left[c], going_right[c])
            pay_o[c, :, lanes] = mix(flip, going_right[c], going_left[c])

    times(TILES, stack, TILES)
    for t in range(TILES):
        for r in range(4):
            low, high = [two[t, pl.ds(64 * half + 2 * r, 8, stride=8), :] for half in range(2)]
            v = pack_two(low, high, even)
            thick[pl.ds(4 * r, 4), tile(t)] = v[0:4]
            thick[pl.ds(16 + 4 * r, 4), tile(t)] = v[4:8]
    for i in range(2):
        s, _ = lift_two(tiles_of(thick, pl.ds(8 * i, 8)), tiles_of(thick, pl.ds(16 + 8 * i, 8)), 2)
        put_tiles(cells, pl.ds(8 * i, 8), s)
    for hint in hints:
        hint.wait()


def thin_z(w3, w4, cells, own, got, result, pay, beyond, held4, turned3, turned4, sem):
    me, count = lax.axis_index("gy"), got.shape[0]
    first, last = me == 0, me == count - 1
    near = lambda k: got[jnp.clip(me + k, 0, count - 1), :, 0:WIDE]
    beyond[0:8] = own[0:8] + (mix(me >= 1, near(-1), 0.0) + mix(me >= 2, near(-2), 0.0))
    beyond[8:16] = own[8:16] + (mix(me < count - 1, near(1), 0.0) + mix(me < count - 2, near(2), 0.0))
    four = got[0, :, WIDE:]
    for k in range(1, count):
        four = four + got[k, :, WIDE:]
    held4[:, 0 : WIDE // 2] = four[0:4]
    held4[:, WIDE // 2 :] = four[4:8]
    lane = lane_id((4, LANES))
    for t in range(TILES):
        at = lambda r: pl.ds(4 * r, 4)
        p, q, s, r = [beyond[at(c), tile(t)] for c in range(4)]
        rows = [cells[at(c), tile(t)] for c in range(4)]
        rows = interleave(*lift(rows, (p, q), (s, r), first, last, mix))
        for f in range(4):
            v = None
            for r in range(4):
                moved = pltpu.roll(rows[r], (r - f) % LANES, 1) if r != f else rows[r]
                v = jnp.where(lane % 4 == r, moved, v) if r else moved
            turned3[at(f), tile(t)] = v
        v = held4[:, tile(t)]
        for f in range(8):
            turned4[at(f), tile(t)] = pltpu.roll(v, LANES - f, 1) if f else v
    count = pay.shape[0]
    parts = [pl.ds(0, WIDE), pl.ds(WIDE, LANES)]
    sends = [pltpu.make_async_copy(pay.at[:, :, p], result.at[:, :, p], sem.at[k]) for k, p in enumerate(parts)]
    three = product(w3[...], turned3[...])
    four = product(w4[...], turned4[...])
    for to in range(count):
        pay[to, :, 0:WIDE] = three[to * 4 : to * 4 + 4]
    sends[0].start()
    lane = lane_id((count, LANES))
    for t in range(TILES // 2):
        v = four[0:count, tile(t)]
        for k in range(1, 8):
            w = four[k % 4 * count : (k % 4 + 1) * count, tile(t + k // 4 * (TILES // 2))]
            v = jnp.where(lane % 8 == k, pltpu.roll(w, k, 1), v)
        pay[:, t, WIDE:] = v
    sends[1].start()
    for send in sends:
        send.wait()


def along_z(one, two, got_e, got_o, result, fourth, out, fine, spread, sem):
    me = lax.axis_index("gz")
    first, last, flip = me == 0, me == lax.axis_size("gz") - 1, me % 2 == 1

    def stack(t):
        lanes = tile_lanes(t)
        e = [got_e[c, :, lanes] for c in range(6)]
        o = [got_o[c, :, lanes] for c in range(6)]
        left = [mix(flip, e[c], o[c]) for c in range(6)]
        right = [mix(flip, o[c], e[c]) for c in range(6)]
        for half in range(2):
            rows = [one[t, pl.ds(z * 16 + half * 8, 8), :] for z in range(16)]
            smooth, detail = lift(rows, left[half:4:2], right[half:4:2], first, last, mix)
            for z, v in enumerate(interleave(smooth, detail)):
                out[z, pl.ds(half * 8, 8), lanes] = v
        rows = [two[t, pl.ds(z * 8, 8), :] for z in range(16)]
        to_right, to_left = edges(rows)
        smooth, _ = lift(rows, unpack_two(left[4]), unpack_two(right[4]), first, last, mix)
        left2 = add_pairs(unpack_two(left[5]), own_left(to_left))
        right2 = add_pairs(unpack_two(right[5]), own_right(to_right))
        smooth, detail = lift(smooth, left2, right2, first, last, mix)
        for z, v in enumerate(interleave(smooth, detail)):
            fine[pl.ds(z * 8, 8), lanes] = v

    times(TILES, stack, TILES)
    sends = {z: pltpu.make_async_copy(out.at[z], result.at[z], sem.at[z]) for z in range(16) if z % 4}
    for z in range(1, 16, 2):
        sends[z].start()
    row = lax.broadcasted_iota(jnp.int32, (16, LANES), 0)
    here = (row % 2 == 0) & (lane_id((16, LANES)) % 2 == 0)
    for z in (1, 3, 5, 7, 0, 2, 4, 6):
        v = lift_runs(tiles_of(fine, pl.ds(z * 8, 8)), 2)
        for t in range(TILES):
            spread[t, pl.ds(z * 16, 8, stride=2), :] = v[t]
            w = jnp.where(here, spread[t, pl.ds(z * 16, 16), :], out[2 * z, :, tile(t)])
            if z % 2:
                out[2 * z, :, tile(t)] = w
            else:
                fourth[z // 2, :, tile(t)] = w
        if z % 2:
            sends[2 * z].start()
    for send in sends.values():
        send.wait()


def join(got, fourth, base, result, planes, spread, sem):
    total = got[0]
    for k in range(1, got.shape[0]):
        total = total + got[k]
    three = lift_runs([total[:, tile(t)] for t in range(TILES)], 4)
    four = [total[t : t + 1, WIDE:] for t in range(TILES // 2)]
    four = lift_runs(four + [pltpu.roll(x, LANES - 4, 1) for x in four], 8)
    lane = lane_id((4, LANES))
    row = lax.broadcasted_iota(jnp.int32, (4, LANES), 0)
    for t in range(TILES):
        for r in range(4):
            v = pltpu.roll(three[t], LANES - r, 1) if r else three[t]
            for k in range(r // 2, 4, 2) if r % 2 == 0 else ():
                w = pltpu.roll(four[t], LANES - k, 1) if k else four[t]
                v = jnp.where((lane % 8 == 0) & (row == 2 * (k // 2)), jnp.broadcast_to(w, v.shape), v)
            spread[t, pl.ds(4 * r, 4, stride=16), :] = v
    row = lax.broadcasted_iota(jnp.int32, (16, LANES), 0)
    here = (row % 4 == 0) & (lane_id((16, LANES)) % 4 == 0)
    sends = [pltpu.make_async_copy(planes.at[i], result.at[4 * i], sem.at[i]) for i in range(4)]
    for i in range(4):
        for t in range(TILES):
            planes[i, :, tile(t)] = jnp.where(here, spread[t, pl.ds(i * 16, 16), :], fourth[i, :, tile(t)])
        sends[i].start()
    for send in sends:
        send.wait()


def deep_levels(n):
    fixed = lambda c, a, b: a if c else b
    level = lambda rows: lift(rows, (0.0, 0.0), (0.0, 0.0), True, True, fixed)
    cells = level(level(list(np.eye(n)))[0])[0]
    smooth, detail = level(cells)
    return cells, np.stack(interleave(smooth, detail)), np.stack(interleave(*level(smooth)))


def weights_y(devices):
    cells, _, four = deep_levels(16 * devices)
    w3 = np.zeros((devices, 48, 4, 16), np.float64)
    w4 = np.zeros((devices, devices, 2, 2, 2, 16), np.float64)
    for a in range(devices):
        mine = slice(16 * a, 16 * a + 16)
        for row, side, b in ((0, 0, -1), (8, 1, 1), (16, 0, 0), (24, 0, 1), (32, 1, 0), (40, 1, -1)):
            if 0 <= a + b < devices:
                pair = edges(cells[4 * (a + b) : 4 * (a + b) + 4])[side]
                for c in range(2):
                    for z in range(4):
                        w3[a, row + 4 * c + z, z] = pair[c][mine]
        for z in range(2):
            w4[a, :, :, z, z] = four[:, mine].reshape(devices, 2, 16)
    return (
        split_left(w3.reshape(devices, 48, 64).astype(np.float32)),
        split_left(w4.reshape(devices, 4 * devices, 32).astype(np.float32)),
    )


def weights_z(devices):
    _, three, four = deep_levels(16 * devices)
    w3 = np.zeros((devices, devices, 4, 4, 4), np.float64)
    w4 = np.zeros((devices, 2, 2, devices, 8, 2, 2), np.float64)
    for a in range(devices):
        for f in range(8):
            for zz in range(4):
                if f < 4:
                    z = 16 * a + zz + 4 * (f // 2) + 8 * (f % 2)
                    w3[a, :, :, f, zz] = three[:, z].reshape(devices, 4)
                if zz < 2:
                    z = 16 * a + zz + 2 * (f // 4) + 4 * (f // 2 % 2) + 8 * (f % 2)
                    for o in range(2):
                        w4[a, :, o, :, f, o, zz] = four[:, z].reshape(devices, 2).T
    return (
        split_left(w3.reshape(devices, 4 * devices, 16).astype(np.float32)),
        split_left(w4.reshape(devices, 4 * devices, 32).astype(np.float32)),
    )


def swap(values, axis, start):
    devices = lax.axis_size(axis)
    pairs = []
    for i in range(start, devices - 1, 2):
        pairs += [(i, i + 1), (i + 1, i)]
    return lax.ppermute(values, axis, pairs)


def f32(*shape):
    return jax.ShapeDtypeStruct(shape, jnp.float32)


def bf16(*shape):
    return jax.ShapeDtypeStruct(shape, jnp.bfloat16)


def call(body, out, scratch=(), cost=4 << 20, **more):
    return pl.pallas_call(
        body,
        out_shape=out,
        scratch_shapes=list(scratch),
        cost_estimate=pl.CostEstimate(flops=cost * 10, bytes_accessed=4 << 20, transcendentals=0),
        compiler_params=pltpu.CompilerParams(vmem_limit_bytes=24 * 1024 * 1024),
        **more,
    )


def per_device(density):
    planes, rows, cells = density.shape
    ny, nz = lax.axis_size("gy"), lax.axis_size("gz")
    vmem = lambda *shape: pltpu.VMEM(shape, jnp.float32)
    sems = lambda count: pltpu.SemaphoreType.DMA((count,))
    far, here = pl.BlockSpec(memory_space=pltpu.HBM), pl.BlockSpec(memory_space=pltpu.VMEM)
    stay = lambda v: pltpu.with_memory_space_constraint(jnp.asarray(v), pltpu.HBM)
    tiled = f32(TILES, planes * rows, LANES)

    payload = f32(3, 16, cells)
    x, pay_e, pay_o, e1, y3, y4 = call(
        along_x,
        [tiled, payload, payload, f32(planes * rows // 2, cells), bf16(48, 6 * 64), bf16(4 * ny, 6 * 32)],
        [vmem(planes * rows, cells), sems(10)],
        in_specs=[far, far, far],
    )(*[stay(w) for w in weights_y(ny)], stay(density.reshape(planes * rows, cells)))
    got_e, got_o = swap(pay_e, "gy", 0), swap(pay_o, "gy", 1)
    pay = (ny, 8, cells * 3 // 2)
    own, pay = call(
        thin_y,
        [f32(16, cells), f32(*pay)],
        [vmem(*pay), vmem(64, cells), vmem(32, cells), sems(2)],
        cost=40 << 20,
        in_specs=[here, here, here],
        out_specs=[here, far],
    )(y3, y4, e1)
    got = lax.all_to_all(pay, "gy", 0, 0, tiled=True)

    payload = f32(6, 8, cells)
    one, two, pay_e, pay_o, third, z3, z4 = call(
        along_y,
        [
            tiled,
            f32(TILES, planes * rows // 2, LANES),
            payload,
            payload,
            f32(16, cells),
            bf16(4 * nz, 6 * 16),
            bf16(4 * nz, 6 * 32),
        ],
        [vmem(32, cells), sems(2)],
        cost=400 << 20,
        in_specs=[far, far, here, here, here],
        input_output_aliases={2: 0},
    )(*[stay(w) for w in weights_z(nz)], x, got_e, got_o)
    got_e, got_o = swap(pay_e, "gz", 0), swap(pay_o, "gz", 1)
    pay = (nz, 4, cells + LANES)
    pay = call(
        thin_z,
        f32(*pay),
        [vmem(*pay), vmem(16, cells), vmem(4, cells), vmem(16, cells), vmem(32, cells), sems(2)],
        cost=40 << 20,
        out_specs=far,
    )(z3, z4, third, own, got)
    got = lax.all_to_all(pay, "gz", 0, 0, tiled=True)

    base, fourth = call(
        along_z,
        [f32(planes, rows, cells), f32(planes // 4, rows, cells)],
        [vmem(planes, rows, cells), vmem(64, cells), vmem(TILES, 128, LANES), sems(planes)],
        cost=400 << 20,
        out_specs=[far, here],
    )(one, two, got_e, got_o)
    return call(
        join,
        f32(planes, rows, cells),
        [vmem(planes // 4, rows, cells), vmem(TILES, 64, LANES), sems(4)],
        in_specs=[here, here, far],
        out_specs=far,
        input_output_aliases={2: 0},
    )(got, fourth, stay(base))


def solution(mesh):
    return jax.shard_map(
        per_device, mesh=mesh, in_specs=(P("gz", "gy", None),), out_specs=P("gz", "gy", None), check_vma=False
    )
```

```python
import functools

import jax
import jax.numpy as jnp
import ml_dtypes
import numpy as np
from jax import lax
from jax.experimental import pallas as pl
from jax.experimental.pallas import tpu as pltpu
from jax.sharding import PartitionSpec as P

A1 = -1.586134342059924
B1 = -0.052980118572961
A2 = 0.882911075530934
B2 = 0.443506852043971
GAIN = 1.230174104914001

WIDE = 1024
LANES = 128
TILES = WIDE // LANES


def lift(rows, left, right, first, last, choose):
    p, q = left
    s_next, r = right
    smooth, detail = rows[0::2], rows[1::2]
    m = len(smooth)
    s_next = choose(last, smooth[-1], s_next)
    d1 = [detail[i] + A1 * (smooth[i] + (smooth[i + 1] if i + 1 < m else s_next)) for i in range(m)]
    d1_before = choose(first, d1[0], p + A1 * smooth[0])
    s1 = [smooth[i] + B1 * ((d1[i - 1] if i else d1_before) + d1[i]) for i in range(m)]
    s1_after = choose(last, s1[-1], r + B1 * d1[-1])
    d2 = [d1[i] + A2 * (s1[i] + (s1[i + 1] if i + 1 < m else s1_after)) for i in range(m)]
    d2_before = choose(first, d2[0], d1_before + A2 * (q + B1 * d1_before + s1[0]))
    s2 = [s1[i] + B2 * ((d2[i - 1] if i else d2_before) + d2[i]) for i in range(m)]
    return [v * (1.0 / GAIN) for v in s2], [v * (GAIN / 2.0) for v in d2]


def lift_alone(rows):
    zero = jnp.zeros_like(rows[0])
    return lift(rows, (zero, zero), (zero, zero), False, False, lambda c, a, b: a if c else b)[0]


def edges(rows):
    s, d = rows[0::2], rows[1::2]
    to_right = (d[-1] + A1 * s[-1], s[-1] + B1 * (d[-2] + A1 * (s[-2] + s[-1])))
    to_left = (s[0], s[0] + B1 * (d[0] + A1 * (s[0] + s[1])))
    return to_right, to_left


def own_left(to_left):
    s, r = to_left
    c2 = (B2 * A2 * B1 * A1 / GAIN) * s
    c1 = ((B1 * A1 + B2 * A1 + 3 * B2 * A2 * B1 * A1) / GAIN) * s + (B2 * A2 / GAIN) * r
    return c1 + A1 * c2, (1 + B1 * A1) * c2


def own_right(to_right):
    p, q = to_right
    c0 = ((B1 + B2 + 3 * B2 * A2 * B1) / GAIN) * p + (B2 * A2 / GAIN) * q
    c1 = (B2 * A2 * B1 / GAIN) * p
    return c0, c0 + B1 * (c1 + A1 * c0)


def add_pairs(a, b):
    return a[0] + b[0], a[1] + b[1]


def mix(flag, a, b):
    return jnp.where(flag, a, b)


def interleave(smooth, detail):
    return [v for pair in zip(smooth, detail) for v in pair]


def filters():
    fixed = lambda c, a, b: a if c else b
    smooth, detail = lift(list(np.eye(32)), (0.0, 0.0), (0.0, 0.0), True, True, fixed)
    return [float(v) for v in smooth[8][16:21]], [float(v) for v in detail[8][17:21]]


def moved(tiles, step):
    if step == 0:
        return list(tiles)
    lane, count = lane_id(tiles[0].shape), len(tiles)
    r = [pltpu.roll(x, -step % LANES, 1) for x in tiles]
    if step > 0:
        return [jnp.where(lane < LANES - step, r[t], r[t + 1]) if t + 1 < count else r[t] for t in range(count)]
    return [jnp.where(lane >= -step, r[t], r[t - 1]) if t else r[t] for t in range(count)]


def lift_runs(v, stride):
    run = lane_id(v[0].shape) // stride
    ends = LANES // stride - 1
    at = {k: moved(v, k * stride) for k in range(-4, 5)}
    for k in range(1, 5):
        for j in range(k):
            at[-k][0] = jnp.where(run == j, at[k - 2 * j][0], at[-k][0])
    for k in range(1, 5):
        for j in range(k):
            at[k][-1] = jnp.where(run == ends - j, at[2 * j - k][-1], at[k][-1])
    smooth, detail = filters()
    weight = [jnp.where(run % 2 == 0, a, b) for a, b in zip(smooth, detail + [0.0])]
    out = [weight[0] * x for x in v]
    for k in range(1, 5):
        out = [x + weight[k] * (y + z) for x, y, z in zip(out, at[-k], at[k])]
    return out


def split_left(w):
    parts = []
    for _ in range(3):
        parts.append((w - sum(p.astype(np.float32) for p in parts)).astype(ml_dtypes.bfloat16))
    one, two, three = parts
    return np.concatenate([one, one, two, one, two, three], axis=-1)


def product(left, x):
    one = x.astype(jnp.bfloat16)
    rest = x - one.astype(jnp.float32)
    two = rest.astype(jnp.bfloat16)
    three = (rest - two.astype(jnp.float32)).astype(jnp.bfloat16)
    right = jnp.concatenate([one, two, one, three, two, one], axis=0)
    return jnp.dot(left, right, preferred_element_type=jnp.float32)


def lane_id(shape):
    return lax.broadcasted_iota(jnp.int32, shape, len(shape) - 1)


def pack_two(a, b, even):
    return jnp.where(even, a, pltpu.roll(b, 1, 1))


def unpack_two(w):
    return w, pltpu.roll(w, LANES - 1, 1)


def tile(t):
    return slice(t * LANES, (t + 1) * LANES)


def times(count, body, unroll=1):
    if unroll == count:
        for i in range(count):
            body(i)
        return

    def step(i, carry):
        body(i)
        return carry

    lax.fori_loop(0, count, step, 0, unroll=unroll)


def tile_lanes(t):
    return pl.ds(t * LANES if isinstance(t, int) else pl.multiple_of(t * LANES, LANES), LANES)


def lift_two(a, b, phase):
    lane = lane_id((a[0].shape[0], LANES))
    here = lane % (2 * phase) < phase
    count, reach = len(a), 2 * phase
    s = [jnp.where(here, x, pltpu.roll(y, phase, 1)) for x, y in zip(a, b)]
    d = [jnp.where(here, pltpu.roll(x, LANES - phase, 1), y) for x, y in zip(a, b)]

    def ahead(x):
        r = [pltpu.roll(w, LANES - reach, 1) for w in x]
        return [jnp.where(lane < LANES - reach, r[t], r[t + 1] if t + 1 < count else x[t]) for t in range(count)]

    def behind(x):
        r = [pltpu.roll(w, reach, 1) for w in x]
        return [jnp.where(lane >= reach, r[t], r[t - 1] if t else x[t]) for t in range(count)]

    d = [x + A1 * (y + z) for x, y, z in zip(d, s, ahead(s))]
    s = [x + B1 * (y + z) for x, y, z in zip(s, d, behind(d))]
    d = [x + A2 * (y + z) for x, y, z in zip(d, s, ahead(s))]
    s = [(x + B2 * (y + z)) * (1.0 / GAIN) for x, y, z in zip(s, d, behind(d))]
    return s, [x * (GAIN / 2.0) for x in d]


def separate(s, d, phase):
    here = lane_id(s[0].shape) % (2 * phase) < phase
    a = [jnp.where(here, x, pltpu.roll(y, phase, 1)) for x, y in zip(s, d)]
    b = [jnp.where(here, pltpu.roll(x, LANES - phase, 1), y) for x, y in zip(s, d)]
    return a, b


def tiles_of(ref, at):
    v = ref[at, :]
    return [v[:, tile(t)] for t in range(TILES)]


def put_tiles(ref, at, parts):
    for t, v in enumerate(parts):
        ref[at, tile(t)] = v


def along_x(
    y3, y4, z3, z4, density, out, pay_e, pay_o, own, result, next3, next4, x, e1, e2, e3, w3, w4, pay, load_sem, sem
):
    me, mz = lax.axis_index("gy"), lax.axis_index("gz")

    def load(k):
        at = pl.ds(pl.multiple_of(k * 32, 32), 32)
        return pltpu.make_async_copy(density.at[at], x.at[at], load_sem.at[k])

    for k in range(4):
        load(k).start()
        load(k + 4).start()
    hints = [
        pltpu.make_async_copy(y3.at[me], w3, sem.at[0]),
        pltpu.make_async_copy(y4.at[me], w4, sem.at[1]),
        pltpu.make_async_copy(z3.at[mz], next3, sem.at[2]),
        pltpu.make_async_copy(z4.at[mz], next4, sem.at[3]),
    ]
    for hint in hints:
        hint.start()

    def plane(i):
        z, y = i // 2, i % 2
        at = pl.multiple_of(z * 16 + y * 8, 8)
        far = pl.multiple_of(z * 16 + y * 8 + 128, 8)
        s, d = lift_two(tiles_of(x, pl.ds(at, 8)), tiles_of(x, pl.ds(far, 8)), 1)
        put_tiles(e1, pl.ds(at, 8), s)
        a, b = separate(s, d, 1)
        for t in range(TILES):
            out[t, pl.ds(at, 8), :] = a[t]
            out[t, pl.ds(far, 8), :] = b[t]

    def group(k):
        load(k).wait()
        load(k + 4).wait()
        for i in range(4):
            plane(4 * k + i)

    times(4, group)
    for hint in hints:
        hint.wait()

    flip = me % 2 == 1
    even = lane_id((8, LANES)) % 2 == 0

    def column(t):
        lanes = tile_lanes(t)
        for half in range(2):
            rows = [out[t, pl.ds(half * 128 + y, 8, stride=16), :] for y in range(16)]
            to_right, to_left = edges(rows)
            next_right, next_left = edges(lift_alone(rows))
            going_right = to_right + (pack_two(*next_right, even),)
            going_left = to_left + (pack_two(*next_left, even),)
            for c in range(3):
                pay_e[c, pl.ds(half * 8, 8), lanes] = mix(flip, going_left[c], going_right[c])
                pay_o[c, pl.ds(half * 8, 8), lanes] = mix(flip, going_right[c], going_left[c])

    def second(i):
        at = pl.multiple_of(i * 8, 8)
        s, _ = lift_two(tiles_of(e1, pl.ds(at, 8)), tiles_of(e1, pl.ds(at + 64, 8)), 2)
        put_tiles(e2, pl.ds(at, 8), s)

    def both(i):
        second(i)
        column(i)

    times(8, both, 4)

    def third(i):
        at = pl.multiple_of(i * 8, 8)
        s, _ = lift_two(tiles_of(e2, pl.ds(at, 8)), tiles_of(e2, pl.ds(at + 32, 8)), 4)
        put_tiles(e3, pl.ds(at, 8), s)

    times(4, third, 4)
    three = product(w3[...], e2[...])
    four = product(w4[...], e3[...])
    own[...] = three[0:16]
    for to in range(pay.shape[0]):
        right = mix(to == me + 1, three[16:24], three[24:32])
        left = mix(to == me - 1, three[32:40], three[40:48])
        pay[to, :, 0:WIDE] = mix(to > me, right, left)
        pay[to, 0:4, WIDE:] = four[to * 4 : to * 4 + 4, : WIDE // 2]
        pay[to, 4:8, WIDE:] = four[to * 4 : to * 4 + 4, WIDE // 2 :]
    send = pltpu.make_async_copy(pay, result, sem.at[4])
    send.start()
    send.wait()


def along_y(x, got_e, got_o, one, two, pay_e, pay_o, cells, thick):
    me = lax.axis_index("gy")
    first, last, flip = me == 0, me == lax.axis_size("gy") - 1, me % 2 == 1
    even = lane_id((8, LANES)) % 2 == 0

    def column(t):
        lanes = tile_lanes(t)
        for half in range(2):
            rows = [x[t, pl.ds(half * 128 + y, 8, stride=16), :] for y in range(16)]
            e = [got_e[c, pl.ds(half * 8, 8), lanes] for c in range(3)]
            o = [got_o[c, pl.ds(half * 8, 8), lanes] for c in range(3)]
            left = [mix(flip, e[c], o[c]) for c in range(3)]
            right = [mix(flip, o[c], e[c]) for c in range(3)]
            to_right, to_left = edges(rows)
            smooth, detail = lift(rows, left[:2], right[:2], first, last, mix)
            for y, v in enumerate(interleave(smooth, detail)):
                one[t, pl.ds(half * 128 + y, 8, stride=16), :] = v
            left2 = add_pairs(unpack_two(left[2]), own_left(to_left))
            right2 = add_pairs(unpack_two(right[2]), own_right(to_right))
            smooth, detail = lift(smooth, left2, right2, first, last, mix)
            for y, v in enumerate(interleave(smooth, detail)):
                two[t, pl.ds(half * 64 + y, 8, stride=8), :] = v

    times(TILES, column, TILES)
    flip = lax.axis_index("gz") % 2 == 1

    def stack(t):
        lanes = tile_lanes(t)
        going_right, going_left = [None] * 6, [None] * 6
        for half in range(2):
            rows = [one[t, pl.ds(z * 16 + half * 8, 8), :] for z in range(16)]
            to_right, to_left = edges(rows)
            for c in range(2):
                going_right[2 * c + half] = to_right[c]
                going_left[2 * c + half] = to_left[c]
        rows = [two[t, pl.ds(z * 8, 8), :] for z in range(16)]
        to_right, to_left = edges(rows)
        next_right, next_left = edges(lift_alone(rows))
        going_right[4:] = pack_two(*to_right, even), pack_two(*next_right, even)
        going_left[4:] = pack_two(*to_left, even), pack_two(*next_left, even)
        for c in range(6):
            pay_e[c, :, lanes] = mix(flip, going_left[c], going_right[c])
            pay_o[c, :, lanes] = mix(flip, going_right[c], going_left[c])

    times(TILES, stack, TILES)
    for t in range(TILES):
        for r in range(4):
            low, high = [two[t, pl.ds(64 * half + 2 * r, 8, stride=8), :] for half in range(2)]
            v = pack_two(low, high, even)
            thick[pl.ds(4 * r, 4), tile(t)] = v[0:4]
            thick[pl.ds(16 + 4 * r, 4), tile(t)] = v[4:8]
    for i in range(2):
        s, _ = lift_two(tiles_of(thick, pl.ds(8 * i, 8)), tiles_of(thick, pl.ds(16 + 8 * i, 8)), 2)
        put_tiles(cells, pl.ds(8 * i, 8), s)


def thin_z(w3, w4, cells, own, got, result, pay, beyond, held4, turned3, turned4, sem):
    me, count = lax.axis_index("gy"), got.shape[0]
    first, last = me == 0, me == count - 1
    near = lambda k: got[jnp.clip(me + k, 0, count - 1), :, 0:WIDE]
    beyond[0:8] = own[0:8] + (mix(me >= 1, near(-1), 0.0) + mix(me >= 2, near(-2), 0.0))
    beyond[8:16] = own[8:16] + (mix(me < count - 1, near(1), 0.0) + mix(me < count - 2, near(2), 0.0))
    four = got[0, :, WIDE:]
    for k in range(1, count):
        four = four + got[k, :, WIDE:]
    held4[:, 0 : WIDE // 2] = four[0:4]
    held4[:, WIDE // 2 :] = four[4:8]
    lane = lane_id((4, LANES))
    for t in range(TILES):
        at = lambda r: pl.ds(4 * r, 4)
        p, q, s, r = [beyond[at(c), tile(t)] for c in range(4)]
        rows = [cells[at(c), tile(t)] for c in range(4)]
        rows = interleave(*lift(rows, (p, q), (s, r), first, last, mix))
        for f in range(4):
            v = None
            for r in range(4):
                moved = pltpu.roll(rows[r], (r - f) % LANES, 1) if r != f else rows[r]
                v = jnp.where(lane % 4 == r, moved, v) if r else moved
            turned3[at(f), tile(t)] = v
        v = held4[:, tile(t)]
        for f in range(8):
            turned4[at(f), tile(t)] = pltpu.roll(v, LANES - f, 1) if f else v
    count = pay.shape[0]
    parts = [pl.ds(0, WIDE), pl.ds(WIDE, LANES)]
    sends = [pltpu.make_async_copy(pay.at[:, :, p], result.at[:, :, p], sem.at[k]) for k, p in enumerate(parts)]
    three = product(w3[...], turned3[...])
    four = product(w4[...], turned4[...])
    for to in range(count):
        pay[to, :, 0:WIDE] = three[to * 4 : to * 4 + 4]
    sends[0].start()
    lane = lane_id((count, LANES))
    for t in range(TILES // 2):
        v = four[0:count, tile(t)]
        for k in range(1, 8):
            w = four[k % 4 * count : (k % 4 + 1) * count, tile(t + k // 4 * (TILES // 2))]
            v = jnp.where(lane % 8 == k, pltpu.roll(w, k, 1), v)
        pay[:, t, WIDE:] = v
    sends[1].start()
    for send in sends:
        send.wait()


def along_z(one, two, got_e, got_o, result, fourth, out, fine, spread, sem):
    me = lax.axis_index("gz")
    first, last, flip = me == 0, me == lax.axis_size("gz") - 1, me % 2 == 1

    def stack(t):
        lanes = tile_lanes(t)
        e = [got_e[c, :, lanes] for c in range(6)]
        o = [got_o[c, :, lanes] for c in range(6)]
        left = [mix(flip, e[c], o[c]) for c in range(6)]
        right = [mix(flip, o[c], e[c]) for c in range(6)]
        for half in range(2):
            rows = [one[t, pl.ds(z * 16 + half * 8, 8), :] for z in range(16)]
            smooth, detail = lift(rows, left[half:4:2], right[half:4:2], first, last, mix)
            for z, v in enumerate(interleave(smooth, detail)):
                out[z, pl.ds(half * 8, 8), lanes] = v
        rows = [two[t, pl.ds(z * 8, 8), :] for z in range(16)]
        to_right, to_left = edges(rows)
        smooth, _ = lift(rows, unpack_two(left[4]), unpack_two(right[4]), first, last, mix)
        left2 = add_pairs(unpack_two(left[5]), own_left(to_left))
        right2 = add_pairs(unpack_two(right[5]), own_right(to_right))
        smooth, detail = lift(smooth, left2, right2, first, last, mix)
        for z, v in enumerate(interleave(smooth, detail)):
            fine[pl.ds(z * 8, 8), lanes] = v

    times(TILES, stack, TILES)
    sends = {z: pltpu.make_async_copy(out.at[z], result.at[z], sem.at[z]) for z in range(16) if z % 4}
    for z in range(1, 16, 2):
        sends[z].start()
    row = lax.broadcasted_iota(jnp.int32, (16, LANES), 0)
    here = (row % 2 == 0) & (lane_id((16, LANES)) % 2 == 0)
    for z in (1, 3, 5, 7, 0, 2, 4, 6):
        v = lift_runs(tiles_of(fine, pl.ds(z * 8, 8)), 2)
        for t in range(TILES):
            spread[t, pl.ds(z * 16, 8, stride=2), :] = v[t]
            w = jnp.where(here, spread[t, pl.ds(z * 16, 16), :], out[2 * z, :, tile(t)])
            if z % 2:
                out[2 * z, :, tile(t)] = w
            else:
                fourth[z // 2, :, tile(t)] = w
        if z % 2:
            sends[2 * z].start()
    for send in sends.values():
        send.wait()


def join(got, fourth, base, result, planes, spread, sem):
    total = got[0]
    for k in range(1, got.shape[0]):
        total = total + got[k]
    three = lift_runs([total[:, tile(t)] for t in range(TILES)], 4)
    four = [total[t : t + 1, WIDE:] for t in range(TILES // 2)]
    four = lift_runs(four + [pltpu.roll(x, LANES - 4, 1) for x in four], 8)
    lane = lane_id((4, LANES))
    row = lax.broadcasted_iota(jnp.int32, (4, LANES), 0)
    for t in range(TILES):
        for r in range(4):
            v = pltpu.roll(three[t], LANES - r, 1) if r else three[t]
            for k in range(r // 2, 4, 2) if r % 2 == 0 else ():
                w = pltpu.roll(four[t], LANES - k, 1) if k else four[t]
                v = jnp.where((lane % 8 == 0) & (row == 2 * (k // 2)), jnp.broadcast_to(w, v.shape), v)
            spread[t, pl.ds(4 * r, 4, stride=16), :] = v
    row = lax.broadcasted_iota(jnp.int32, (16, LANES), 0)
    here = (row % 4 == 0) & (lane_id((16, LANES)) % 4 == 0)
    sends = [pltpu.make_async_copy(planes.at[i], result.at[4 * i], sem.at[i]) for i in range(4)]
    for i in range(4):
        for t in range(TILES):
            planes[i, :, tile(t)] = jnp.where(here, spread[t, pl.ds(i * 16, 16), :], fourth[i, :, tile(t)])
        sends[i].start()
    for send in sends:
        send.wait()


def deep_levels(n):
    fixed = lambda c, a, b: a if c else b
    level = lambda rows: lift(rows, (0.0, 0.0), (0.0, 0.0), True, True, fixed)
    cells = level(level(list(np.eye(n)))[0])[0]
    smooth, detail = level(cells)
    return cells, np.stack(interleave(smooth, detail)), np.stack(interleave(*level(smooth)))


def weights_y(devices):
    cells, _, four = deep_levels(16 * devices)
    w3 = np.zeros((devices, 48, 4, 16), np.float64)
    w4 = np.zeros((devices, devices, 2, 2, 2, 16), np.float64)
    for a in range(devices):
        mine = slice(16 * a, 16 * a + 16)
        for row, side, b in ((0, 0, -1), (8, 1, 1), (16, 0, 0), (24, 0, 1), (32, 1, 0), (40, 1, -1)):
            if 0 <= a + b < devices:
                pair = edges(cells[4 * (a + b) : 4 * (a + b) + 4])[side]
                for c in range(2):
                    for z in range(4):
                        w3[a, row + 4 * c + z, z] = pair[c][mine]
        for z in range(2):
            w4[a, :, :, z, z] = four[:, mine].reshape(devices, 2, 16)
    return (
        split_left(w3.reshape(devices, 48, 64).astype(np.float32)),
        split_left(w4.reshape(devices, 4 * devices, 32).astype(np.float32)),
    )


def weights_z(devices):
    _, three, four = deep_levels(16 * devices)
    w3 = np.zeros((devices, devices, 4, 4, 4), np.float64)
    w4 = np.zeros((devices, 2, 2, devices, 8, 2, 2), np.float64)
    for a in range(devices):
        for f in range(8):
            for zz in range(4):
                if f < 4:
                    z = 16 * a + zz + 4 * (f // 2) + 8 * (f % 2)
                    w3[a, :, :, f, zz] = three[:, z].reshape(devices, 4)
                if zz < 2:
                    z = 16 * a + zz + 2 * (f // 4) + 4 * (f // 2 % 2) + 8 * (f % 2)
                    for o in range(2):
                        w4[a, :, o, :, f, o, zz] = four[:, z].reshape(devices, 2).T
    return (
        split_left(w3.reshape(devices, 4 * devices, 16).astype(np.float32)),
        split_left(w4.reshape(devices, 4 * devices, 32).astype(np.float32)),
    )


def swap(values, axis, start):
    devices = lax.axis_size(axis)
    pairs = []
    for i in range(start, devices - 1, 2):
        pairs += [(i, i + 1), (i + 1, i)]
    return lax.ppermute(values, axis, pairs)


def f32(*shape):
    return jax.ShapeDtypeStruct(shape, jnp.float32)


def bf16(*shape):
    return jax.ShapeDtypeStruct(shape, jnp.bfloat16)


def call(body, out, scratch=(), cost=4 << 20, **more):
    return pl.pallas_call(
        body,
        out_shape=out,
        scratch_shapes=list(scratch),
        cost_estimate=pl.CostEstimate(flops=cost * 10, bytes_accessed=4 << 20, transcendentals=0),
        compiler_params=pltpu.CompilerParams(vmem_limit_bytes=24 * 1024 * 1024),
        **more,
    )


def per_device(density):
    planes, rows, cells = density.shape
    ny, nz = lax.axis_size("gy"), lax.axis_size("gz")
    vmem = lambda *shape: pltpu.VMEM(shape, jnp.float32)
    sems = lambda count: pltpu.SemaphoreType.DMA((count,))
    far, here = pl.BlockSpec(memory_space=pltpu.HBM), pl.BlockSpec(memory_space=pltpu.VMEM)
    stay = lambda v: pltpu.with_memory_space_constraint(jnp.asarray(v), pltpu.HBM)
    tiled = f32(TILES, planes * rows, LANES)

    payload = f32(3, 16, cells)
    pay = (ny, 8, cells * 3 // 2)
    x, pay_e, pay_o, own, pay, z3, z4 = call(
        along_x,
        [tiled, payload, payload, f32(16, cells), f32(*pay), bf16(4 * nz, 6 * 16), bf16(4 * nz, 6 * 32)],
        [
            vmem(planes * rows, cells),
            vmem(128, cells),
            vmem(64, cells),
            vmem(32, cells),
            pltpu.VMEM((48, 6 * 64), jnp.bfloat16),
            pltpu.VMEM((4 * ny, 6 * 32), jnp.bfloat16),
            vmem(*pay),
            sems(8),
            sems(5),
        ],
        in_specs=[far] * 5,
        out_specs=[here, here, here, here, far, here, here],
    )(*[stay(w) for w in weights_y(ny) + weights_z(nz)], stay(density.reshape(planes * rows, cells)))
    got_e, got_o = swap(pay_e, "gy", 0), swap(pay_o, "gy", 1)
    got = lax.all_to_all(pay, "gy", 0, 0, tiled=True)

    payload = f32(6, 8, cells)
    one, two, pay_e, pay_o, third = call(
        along_y,
        [tiled, f32(TILES, planes * rows // 2, LANES), payload, payload, f32(16, cells)],
        [vmem(32, cells)],
        cost=400 << 20,
        input_output_aliases={0: 0},
    )(x, got_e, got_o)
    got_e, got_o = swap(pay_e, "gz", 0), swap(pay_o, "gz", 1)
    pay = (nz, 4, cells + LANES)
    pay = call(
        thin_z,
        f32(*pay),
        [vmem(*pay), vmem(16, cells), vmem(4, cells), vmem(16, cells), vmem(32, cells), sems(2)],
        cost=40 << 20,
        out_specs=far,
    )(z3, z4, third, own, got)
    got = lax.all_to_all(pay, "gz", 0, 0, tiled=True)

    base, fourth = call(
        along_z,
        [f32(planes, rows, cells), f32(planes // 4, rows, cells)],
        [vmem(planes, rows, cells), vmem(64, cells), vmem(TILES, 128, LANES), sems(planes)],
        cost=400 << 20,
        out_specs=[far, here],
    )(one, two, got_e, got_o)
    return call(
        join,
        f32(planes, rows, cells),
        [vmem(planes // 4, rows, cells), vmem(TILES, 64, LANES), sems(4)],
        in_specs=[here, here, far],
        out_specs=far,
        input_output_aliases={2: 0},
    )(got, fourth, stay(base))


def solution(mesh):
    return jax.shard_map(
        per_device, mesh=mesh, in_specs=(P("gz", "gy", None),), out_specs=P("gz", "gy", None), check_vma=False
    )
```

```python
import functools

import jax
import jax.numpy as jnp
import ml_dtypes
import numpy as np
from jax import lax
from jax.experimental import pallas as pl
from jax.experimental.pallas import tpu as pltpu
from jax.sharding import PartitionSpec as P

A1 = -1.586134342059924
B1 = -0.052980118572961
A2 = 0.882911075530934
B2 = 0.443506852043971
GAIN = 1.230174104914001

WIDE = 1024
LANES = 128
TILES = WIDE // LANES


def lift(rows, left, right, first, last, choose):
    p, q = left
    s_next, r = right
    smooth, detail = rows[0::2], rows[1::2]
    m = len(smooth)
    s_next = choose(last, smooth[-1], s_next)
    d1 = [detail[i] + A1 * (smooth[i] + (smooth[i + 1] if i + 1 < m else s_next)) for i in range(m)]
    d1_before = choose(first, d1[0], p + A1 * smooth[0])
    s1 = [smooth[i] + B1 * ((d1[i - 1] if i else d1_before) + d1[i]) for i in range(m)]
    s1_after = choose(last, s1[-1], r + B1 * d1[-1])
    d2 = [d1[i] + A2 * (s1[i] + (s1[i + 1] if i + 1 < m else s1_after)) for i in range(m)]
    d2_before = choose(first, d2[0], d1_before + A2 * (q + B1 * d1_before + s1[0]))
    s2 = [s1[i] + B2 * ((d2[i - 1] if i else d2_before) + d2[i]) for i in range(m)]
    return [v * (1.0 / GAIN) for v in s2], [v * (GAIN / 2.0) for v in d2]


def lift_alone(rows):
    zero = jnp.zeros_like(rows[0])
    return lift(rows, (zero, zero), (zero, zero), False, False, lambda c, a, b: a if c else b)[0]


def edges(rows):
    s, d = rows[0::2], rows[1::2]
    to_right = (d[-1] + A1 * s[-1], s[-1] + B1 * (d[-2] + A1 * (s[-2] + s[-1])))
    to_left = (s[0], s[0] + B1 * (d[0] + A1 * (s[0] + s[1])))
    return to_right, to_left


def own_left(to_left):
    s, r = to_left
    c2 = (B2 * A2 * B1 * A1 / GAIN) * s
    c1 = ((B1 * A1 + B2 * A1 + 3 * B2 * A2 * B1 * A1) / GAIN) * s + (B2 * A2 / GAIN) * r
    return c1 + A1 * c2, (1 + B1 * A1) * c2


def own_right(to_right):
    p, q = to_right
    c0 = ((B1 + B2 + 3 * B2 * A2 * B1) / GAIN) * p + (B2 * A2 / GAIN) * q
    c1 = (B2 * A2 * B1 / GAIN) * p
    return c0, c0 + B1 * (c1 + A1 * c0)


def add_pairs(a, b):
    return a[0] + b[0], a[1] + b[1]


def mix(flag, a, b):
    return jnp.where(flag, a, b)


def interleave(smooth, detail):
    return [v for pair in zip(smooth, detail) for v in pair]


def filters():
    fixed = lambda c, a, b: a if c else b
    smooth, detail = lift(list(np.eye(32)), (0.0, 0.0), (0.0, 0.0), True, True, fixed)
    return [float(v) for v in smooth[8][16:21]], [float(v) for v in detail[8][17:21]]


def moved(tiles, step):
    if step == 0:
        return list(tiles)
    lane, count = lane_id(tiles[0].shape), len(tiles)
    r = [pltpu.roll(x, -step % LANES, 1) for x in tiles]
    if step > 0:
        return [jnp.where(lane < LANES - step, r[t], r[t + 1]) if t + 1 < count else r[t] for t in range(count)]
    return [jnp.where(lane >= -step, r[t], r[t - 1]) if t else r[t] for t in range(count)]


def lift_runs(v, stride):
    run = lane_id(v[0].shape) // stride
    ends = LANES // stride - 1
    at = {k: moved(v, k * stride) for k in range(-4, 5)}
    for k in range(1, 5):
        for j in range(k):
            at[-k][0] = jnp.where(run == j, at[k - 2 * j][0], at[-k][0])
    for k in range(1, 5):
        for j in range(k):
            at[k][-1] = jnp.where(run == ends - j, at[2 * j - k][-1], at[k][-1])
    smooth, detail = filters()
    weight = [jnp.where(run % 2 == 0, a, b) for a, b in zip(smooth, detail + [0.0])]
    out = [weight[0] * x for x in v]
    for k in range(1, 5):
        out = [x + weight[k] * (y + z) for x, y, z in zip(out, at[-k], at[k])]
    return out


def split_left(w):
    parts = []
    for _ in range(3):
        parts.append((w - sum(p.astype(np.float32) for p in parts)).astype(ml_dtypes.bfloat16))
    one, two, three = parts
    return np.concatenate([one, one, two, one, two, three], axis=-1)


def product(left, x):
    one = x.astype(jnp.bfloat16)
    rest = x - one.astype(jnp.float32)
    two = rest.astype(jnp.bfloat16)
    three = (rest - two.astype(jnp.float32)).astype(jnp.bfloat16)
    right = jnp.concatenate([one, two, one, three, two, one], axis=0)
    return jnp.dot(left, right, preferred_element_type=jnp.float32)


def lane_id(shape):
    return lax.broadcasted_iota(jnp.int32, shape, len(shape) - 1)


def in_even(shape):
    return lane_id(shape) % 2 == 0


def back(v):
    return pltpu.roll(v, LANES - 1, 1)


def on(v):
    return pltpu.roll(v, 1, 1)


def pack_right(p, q):
    return jnp.where(in_even(p.shape), back(q), p)


def unpack_right(v):
    return back(v), v


def pack_left(s, r):
    return jnp.where(in_even(s.shape), s, on(r))


def unpack_left(v):
    return on(v), v


def beyond_halves(left, right, to_right, to_left):
    even = in_even(to_right[0].shape)
    return (
        tuple(jnp.where(even, x, on(y)) for x, y in zip(left, to_right)),
        tuple(jnp.where(even, back(y), x) for x, y in zip(right, to_left)),
    )


def tile(t):
    return slice(t * LANES, (t + 1) * LANES)


def times(count, body, unroll=1):
    if unroll == count:
        for i in range(count):
            body(i)
        return

    def step(i, carry):
        body(i)
        return carry

    lax.fori_loop(0, count, step, 0, unroll=unroll)


def tile_lanes(t):
    return pl.ds(t * LANES if isinstance(t, int) else pl.multiple_of(t * LANES, LANES), LANES)


def lift_two(a, b, phase):
    lane = lane_id((a[0].shape[0], LANES))
    here = lane % (2 * phase) < phase
    count, reach = len(a), 2 * phase
    s = [jnp.where(here, x, pltpu.roll(y, phase, 1)) for x, y in zip(a, b)]
    d = [jnp.where(here, pltpu.roll(x, LANES - phase, 1), y) for x, y in zip(a, b)]

    def ahead(x):
        r = [pltpu.roll(w, LANES - reach, 1) for w in x]
        return [jnp.where(lane < LANES - reach, r[t], r[t + 1] if t + 1 < count else x[t]) for t in range(count)]

    def behind(x):
        r = [pltpu.roll(w, reach, 1) for w in x]
        return [jnp.where(lane >= reach, r[t], r[t - 1] if t else x[t]) for t in range(count)]

    d = [x + A1 * (y + z) for x, y, z in zip(d, s, ahead(s))]
    s = [x + B1 * (y + z) for x, y, z in zip(s, d, behind(d))]
    d = [x + A2 * (y + z) for x, y, z in zip(d, s, ahead(s))]
    s = [(x + B2 * (y + z)) * (1.0 / GAIN) for x, y, z in zip(s, d, behind(d))]
    return s, [x * (GAIN / 2.0) for x in d]


def separate(s, d, phase):
    here = lane_id(s[0].shape) % (2 * phase) < phase
    a = [jnp.where(here, x, pltpu.roll(y, phase, 1)) for x, y in zip(s, d)]
    b = [jnp.where(here, pltpu.roll(x, LANES - phase, 1), y) for x, y in zip(s, d)]
    return a, b


def tiles_of(ref, at):
    v = ref[at, :]
    return [v[:, tile(t)] for t in range(TILES)]


def put_tiles(ref, at, parts):
    for t, v in enumerate(parts):
        ref[at, tile(t)] = v


def along_x(
    y3, y4, z3, z4, density, smooth, detail, pay_e, pay_o, own, result, next3, next4, x, e2, e3, w3, w4, pay, load_sem, sem
):
    me, mz = lax.axis_index("gy"), lax.axis_index("gz")

    def load(k):
        at = pl.ds(pl.multiple_of(k * 32, 32), 32)
        return pltpu.make_async_copy(density.at[at], x.at[at], load_sem.at[k])

    for k in range(4):
        load(k).start()
        load(k + 4).start()
    hints = [
        pltpu.make_async_copy(y3.at[me], w3, sem.at[0]),
        pltpu.make_async_copy(y4.at[me], w4, sem.at[1]),
        pltpu.make_async_copy(z3.at[mz], next3, sem.at[2]),
        pltpu.make_async_copy(z4.at[mz], next4, sem.at[3]),
    ]
    for hint in hints:
        hint.start()

    def plane(i):
        z, y = i // 2, i % 2
        at = pl.multiple_of(z * 16 + y * 8, 8)
        far = pl.multiple_of(z * 16 + y * 8 + 128, 8)
        s, d = lift_two(tiles_of(x, pl.ds(at, 8)), tiles_of(x, pl.ds(far, 8)), 1)
        for t in range(TILES):
            smooth[t, pl.ds(at, 8), :] = s[t]
            detail[t, pl.ds(at, 8), :] = d[t]

    def group(k):
        load(k).wait()
        load(k + 4).wait()
        for i in range(4):
            plane(4 * k + i)

    times(4, group)
    for hint in hints:
        hint.wait()

    def second(i):
        at = pl.multiple_of(i * 8, 8)
        near, far = [[smooth[t, pl.ds(at + k, 8), :] for t in range(TILES)] for k in (0, 64)]
        s, _ = lift_two(near, far, 2)
        put_tiles(e2, pl.ds(at, 8), s)

    times(8, second, 8)

    def third(i):
        at = pl.multiple_of(i * 8, 8)
        s, _ = lift_two(tiles_of(e2, pl.ds(at, 8)), tiles_of(e2, pl.ds(at + 32, 8)), 4)
        put_tiles(e3, pl.ds(at, 8), s)

    times(4, third, 4)
    three = product(w3[...], e2[...])
    four = product(w4[...], e3[...])
    own[...] = three[0:16]
    for to in range(pay.shape[0]):
        right = mix(to == me + 1, three[16:24], three[24:32])
        left = mix(to == me - 1, three[32:40], three[40:48])
        pay[to, :, 0:WIDE] = mix(to > me, right, left)
        pay[to, 0:4, WIDE:] = four[to * 4 : to * 4 + 4, : WIDE // 2]
        pay[to, 4:8, WIDE:] = four[to * 4 : to * 4 + 4, WIDE // 2 :]
    send = pltpu.make_async_copy(pay, result, sem.at[4])
    send.start()
    flip = me % 2 == 1

    def column(t):
        lanes = tile_lanes(t)
        rows = [smooth[t, pl.ds(y, 8, stride=16), :] for y in range(16)]
        parts = [edges(rows), edges(lift_alone(rows))]
        parts.append(edges([detail[t, pl.ds(y, 8, stride=16), :] for y in range(16)]))
        for c in range(6):
            right, left = [parts[c // 2][side][c % 2] for side in range(2)]
            pay_e[c, :, lanes] = mix(flip, left, right)
            pay_o[c, :, lanes] = mix(flip, right, left)

    times(TILES, column, 4)
    send.wait()


def along_y(smooth, detail, got_e, got_o, one_s, one_d, two, pay_e, pay_o, cells, thick):
    me = lax.axis_index("gy")
    first, last, flip = me == 0, me == lax.axis_size("gy") - 1, me % 2 == 1

    def column(t):
        lanes = tile_lanes(t)
        e = [got_e[c, :, lanes] for c in range(6)]
        o = [got_o[c, :, lanes] for c in range(6)]
        left = [mix(flip, e[c], o[c]) for c in range(6)]
        right = [mix(flip, o[c], e[c]) for c in range(6)]
        for k, (source, to) in enumerate(((detail, one_d), (smooth, one_s))):
            rows = [source[t, pl.ds(y, 8, stride=16), :] for y in range(16)]
            at = slice(0, 2) if k else slice(4, 6)
            low, high = lift(rows, left[at], right[at], first, last, mix)
            for y, v in enumerate(interleave(low, high)):
                to[t, pl.ds(y, 8, stride=16), :] = v
        to_right, to_left = edges(rows)
        left2, right2 = add_pairs(left[2:4], own_left(to_left)), add_pairs(right[2:4], own_right(to_right))
        low, high = lift(low, left2, right2, first, last, mix)
        for y, v in enumerate(interleave(low, high)):
            two[t, pl.ds(y, 8, stride=8), :] = v
        for r, v in enumerate(low):
            thick[pl.ds(4 * r, 4), lanes] = v[0:4]
            thick[pl.ds(16 + 4 * r, 4), lanes] = v[4:8]

    times(TILES, column, TILES)
    flip = lax.axis_index("gz") % 2 == 1

    def stack(t):
        lanes = tile_lanes(t)
        going_right, going_left = [], []

        def add(rows):
            to_right, to_left = edges(rows)
            going_right.append(pack_right(*to_right))
            going_left.append(pack_left(*to_left))
            return to_right, to_left

        for source in (one_s, one_d):
            for half in range(2):
                add([source[t, pl.ds(z * 16 + half * 8, 8), :] for z in range(8)])
        rows = [two[t, pl.ds(z * 8, 8), :] for z in range(8)]
        nothing = jnp.zeros_like(rows[0])
        left, right = beyond_halves((nothing, nothing), (nothing, nothing), *add(rows))
        add(lift(rows, left, right, False, False, lambda c, a, b: b)[0])
        for c in range(6):
            pay_e[c, :, lanes] = mix(flip, going_left[c], going_right[c])
            pay_o[c, :, lanes] = mix(flip, going_right[c], going_left[c])

    times(TILES, stack, TILES)
    for i in range(2):
        s, _ = lift_two(tiles_of(thick, pl.ds(8 * i, 8)), tiles_of(thick, pl.ds(16 + 8 * i, 8)), 2)
        put_tiles(cells, pl.ds(8 * i, 8), s)


def thin_z(w3, w4, cells, own, got, result, pay, beyond, held4, turned3, turned4, sem):
    me, count = lax.axis_index("gy"), got.shape[0]
    first, last = me == 0, me == count - 1
    near = lambda k: got[jnp.clip(me + k, 0, count - 1), :, 0:WIDE]
    beyond[0:8] = own[0:8] + (mix(me >= 1, near(-1), 0.0) + mix(me >= 2, near(-2), 0.0))
    beyond[8:16] = own[8:16] + (mix(me < count - 1, near(1), 0.0) + mix(me < count - 2, near(2), 0.0))
    four = got[0, :, WIDE:]
    for k in range(1, count):
        four = four + got[k, :, WIDE:]
    held4[:, 0 : WIDE // 2] = four[0:4]
    held4[:, WIDE // 2 :] = four[4:8]
    lane = lane_id((4, LANES))
    for t in range(TILES):
        at = lambda r: pl.ds(4 * r, 4)
        p, q, s, r = [beyond[at(c), tile(t)] for c in range(4)]
        rows = [cells[at(c), tile(t)] for c in range(4)]
        rows = interleave(*lift(rows, (p, q), (s, r), first, last, mix))
        for f in range(4):
            v = None
            for r in range(4):
                moved = pltpu.roll(rows[r], (r - f) % LANES, 1) if r != f else rows[r]
                v = jnp.where(lane % 4 == r, moved, v) if r else moved
            turned3[at(f), tile(t)] = v
        v = held4[:, tile(t)]
        for f in range(8):
            turned4[at(f), tile(t)] = pltpu.roll(v, LANES - f, 1) if f else v
    count = pay.shape[0]
    parts = [pl.ds(0, WIDE), pl.ds(WIDE, LANES)]
    sends = [pltpu.make_async_copy(pay.at[:, :, p], result.at[:, :, p], sem.at[k]) for k, p in enumerate(parts)]
    three = product(w3[...], turned3[...])
    four = product(w4[...], turned4[...])
    for to in range(count):
        pay[to, :, 0:WIDE] = three[to * 4 : to * 4 + 4]
    sends[0].start()
    lane = lane_id((count, LANES))
    for t in range(TILES // 2):
        v = four[0:count, tile(t)]
        for k in range(1, 8):
            w = four[k % 4 * count : (k % 4 + 1) * count, tile(t + k // 4 * (TILES // 2))]
            v = jnp.where(lane % 8 == k, pltpu.roll(w, k, 1), v)
        pay[:, t, WIDE:] = v
    sends[1].start()
    for send in sends:
        send.wait()


def along_z(one_s, one_d, two, got_e, got_o, result, fourth, out, fine, spread, sem):
    me = lax.axis_index("gz")
    flip, side = me % 2 == 1, lane_id((8, LANES)) % 2
    first = side == jnp.where(me == 0, 0, 2)
    last = side == jnp.where(me == lax.axis_size("gz") - 1, 1, 2)

    def stack(t):
        lanes = tile_lanes(t)
        e = [got_e[c, :, lanes] for c in range(6)]
        o = [got_o[c, :, lanes] for c in range(6)]
        left = [unpack_right(mix(flip, e[c], o[c])) for c in range(6)]
        right = [unpack_left(mix(flip, o[c], e[c])) for c in range(6)]
        for half in range(2):
            lifted = []
            for k, source in enumerate((one_s, one_d)):
                rows = [source[t, pl.ds(z * 16 + half * 8, 8), :] for z in range(8)]
                ends = beyond_halves(left[2 * k + half], right[2 * k + half], *edges(rows))
                lifted.append(interleave(*lift(rows, *ends, first, last, mix)))
            near, far = separate(*lifted, 1)
            for z in range(8):
                out[z, pl.ds(half * 8, 8), lanes] = near[z]
                out[z + 8, pl.ds(half * 8, 8), lanes] = far[z]
        rows = [two[t, pl.ds(z * 8, 8), :] for z in range(8)]
        to_right, to_left = edges(rows)
        rows, _ = lift(rows, *beyond_halves(left[4], right[4], to_right, to_left), first, last, mix)
        left2, right2 = add_pairs(left[5], own_left(to_left)), add_pairs(right[5], own_right(to_right))
        ends = beyond_halves(left2, right2, *edges(rows))
        for z, v in enumerate(interleave(*lift(rows, *ends, first, last, mix))):
            fine[pl.ds(z * 8, 8), lanes] = v

    times(TILES, stack, TILES)
    sends = {z: pltpu.make_async_copy(out.at[z], result.at[z], sem.at[z]) for z in range(16) if z % 4}
    for z in range(1, 16, 2):
        sends[z].start()
    row = lax.broadcasted_iota(jnp.int32, (16, LANES), 0)
    here = (row % 2 == 0) & in_even((16, LANES))
    for i in (1, 3, 0, 2):
        v = lift_runs(tiles_of(fine, pl.ds(i * 8, 8)), 2)
        for z in (i, i + 4):
            for t in range(TILES):
                spread[t, pl.ds(z * 16, 8, stride=2), :] = v[t] if z == i else back(v[t])
                w = jnp.where(here, spread[t, pl.ds(z * 16, 16), :], out[2 * z, :, tile(t)])
                if z % 2:
                    out[2 * z, :, tile(t)] = w
                else:
                    fourth[z // 2, :, tile(t)] = w
            if z % 2:
                sends[2 * z].start()
    for send in sends.values():
        send.wait()


def join(got, fourth, base, result, planes, spread, sem):
    total = got[0]
    for k in range(1, got.shape[0]):
        total = total + got[k]
    three = lift_runs([total[:, tile(t)] for t in range(TILES)], 4)
    four = [total[t : t + 1, WIDE:] for t in range(TILES // 2)]
    four = lift_runs(four + [pltpu.roll(x, LANES - 4, 1) for x in four], 8)
    lane = lane_id((4, LANES))
    row = lax.broadcasted_iota(jnp.int32, (4, LANES), 0)
    for t in range(TILES):
        for r in range(4):
            v = pltpu.roll(three[t], LANES - r, 1) if r else three[t]
            for k in range(r // 2, 4, 2) if r % 2 == 0 else ():
                w = pltpu.roll(four[t], LANES - k, 1) if k else four[t]
                v = jnp.where((lane % 8 == 0) & (row == 2 * (k // 2)), jnp.broadcast_to(w, v.shape), v)
            spread[t, pl.ds(4 * r, 4, stride=16), :] = v
    row = lax.broadcasted_iota(jnp.int32, (16, LANES), 0)
    here = (row % 4 == 0) & (lane_id((16, LANES)) % 4 == 0)
    sends = [pltpu.make_async_copy(planes.at[i], result.at[4 * i], sem.at[i]) for i in range(4)]
    for i in range(4):
        for t in range(TILES):
            planes[i, :, tile(t)] = jnp.where(here, spread[t, pl.ds(i * 16, 16), :], fourth[i, :, tile(t)])
        sends[i].start()
    for send in sends:
        send.wait()


def deep_levels(n):
    fixed = lambda c, a, b: a if c else b
    level = lambda rows: lift(rows, (0.0, 0.0), (0.0, 0.0), True, True, fixed)
    cells = level(level(list(np.eye(n)))[0])[0]
    smooth, detail = level(cells)
    return cells, np.stack(interleave(smooth, detail)), np.stack(interleave(*level(smooth)))


def weights_y(devices):
    cells, _, four = deep_levels(16 * devices)
    w3 = np.zeros((devices, 48, 4, 16), np.float64)
    w4 = np.zeros((devices, devices, 2, 2, 2, 16), np.float64)
    for a in range(devices):
        mine = slice(16 * a, 16 * a + 16)
        for row, side, b in ((0, 0, -1), (8, 1, 1), (16, 0, 0), (24, 0, 1), (32, 1, 0), (40, 1, -1)):
            if 0 <= a + b < devices:
                pair = edges(cells[4 * (a + b) : 4 * (a + b) + 4])[side]
                for c in range(2):
                    for z in range(4):
                        w3[a, row + 4 * c + z, z] = pair[c][mine]
        for z in range(2):
            w4[a, :, :, z, z] = four[:, mine].reshape(devices, 2, 16)
    return (
        split_left(w3.reshape(devices, 48, 64).astype(np.float32)),
        split_left(w4.reshape(devices, 4 * devices, 32).astype(np.float32)),
    )


def weights_z(devices):
    _, three, four = deep_levels(16 * devices)
    w3 = np.zeros((devices, devices, 4, 4, 4), np.float64)
    w4 = np.zeros((devices, 2, 2, devices, 8, 2, 2), np.float64)
    for a in range(devices):
        for f in range(8):
            for zz in range(4):
                if f < 4:
                    z = 16 * a + zz + 4 * (f // 2) + 8 * (f % 2)
                    w3[a, :, :, f, zz] = three[:, z].reshape(devices, 4)
                if zz < 2:
                    z = 16 * a + zz + 2 * (f // 4) + 4 * (f // 2 % 2) + 8 * (f % 2)
                    for o in range(2):
                        w4[a, :, o, :, f, o, zz] = four[:, z].reshape(devices, 2).T
    return (
        split_left(w3.reshape(devices, 4 * devices, 16).astype(np.float32)),
        split_left(w4.reshape(devices, 4 * devices, 32).astype(np.float32)),
    )


def swap(values, axis, start):
    devices = lax.axis_size(axis)
    pairs = []
    for i in range(start, devices - 1, 2):
        pairs += [(i, i + 1), (i + 1, i)]
    return lax.ppermute(values, axis, pairs)


def f32(*shape):
    return jax.ShapeDtypeStruct(shape, jnp.float32)


def bf16(*shape):
    return jax.ShapeDtypeStruct(shape, jnp.bfloat16)


def call(body, out, scratch=(), cost=4 << 20, **more):
    return pl.pallas_call(
        body,
        out_shape=out,
        scratch_shapes=list(scratch),
        cost_estimate=pl.CostEstimate(flops=cost * 10, bytes_accessed=4 << 20, transcendentals=0),
        compiler_params=pltpu.CompilerParams(vmem_limit_bytes=24 * 1024 * 1024),
        **more,
    )


def per_device(density):
    planes, rows, cells = density.shape
    ny, nz = lax.axis_size("gy"), lax.axis_size("gz")
    vmem = lambda *shape: pltpu.VMEM(shape, jnp.float32)
    sems = lambda count: pltpu.SemaphoreType.DMA((count,))
    far, here = pl.BlockSpec(memory_space=pltpu.HBM), pl.BlockSpec(memory_space=pltpu.VMEM)
    stay = lambda v: pltpu.with_memory_space_constraint(jnp.asarray(v), pltpu.HBM)
    tiled = f32(TILES, planes * rows // 2, LANES)
    payload = f32(6, 8, cells)
    pay = (ny, 8, cells * 3 // 2)
    smooth, detail, pay_e, pay_o, own, pay, z3, z4 = call(
        along_x,
        [tiled, tiled, payload, payload, f32(16, cells), f32(*pay), bf16(4 * nz, 6 * 16), bf16(4 * nz, 6 * 32)],
        [
            vmem(planes * rows, cells),
            vmem(64, cells),
            vmem(32, cells),
            pltpu.VMEM((48, 6 * 64), jnp.bfloat16),
            pltpu.VMEM((4 * ny, 6 * 32), jnp.bfloat16),
            vmem(*pay),
            sems(8),
            sems(5),
        ],
        in_specs=[far] * 5,
        out_specs=[here] * 5 + [far, here, here],
    )(*[stay(w) for w in weights_y(ny) + weights_z(nz)], stay(density.reshape(planes * rows, cells)))
    got_e, got_o = swap(pay_e, "gy", 0), swap(pay_o, "gy", 1)
    got = lax.all_to_all(pay, "gy", 0, 0, tiled=True)

    one_s, one_d, two, pay_e, pay_o, third = call(
        along_y,
        [tiled, tiled, f32(TILES, planes * rows // 4, LANES), payload, payload, f32(16, cells)],
        [vmem(32, cells)],
        cost=400 << 20,
        input_output_aliases={0: 0, 1: 1},
    )(smooth, detail, got_e, got_o)
    got_e, got_o = swap(pay_e, "gz", 0), swap(pay_o, "gz", 1)
    pay = (nz, 4, cells + LANES)
    pay = call(
        thin_z,
        f32(*pay),
        [vmem(*pay), vmem(16, cells), vmem(4, cells), vmem(16, cells), vmem(32, cells), sems(2)],
        cost=40 << 20,
        out_specs=far,
    )(z3, z4, third, own, got)
    got = lax.all_to_all(pay, "gz", 0, 0, tiled=True)

    base, fourth = call(
        along_z,
        [f32(planes, rows, cells), f32(planes // 4, rows, cells)],
        [vmem(planes, rows, cells), vmem(32, cells), vmem(TILES, 128, LANES), sems(planes)],
        cost=400 << 20,
        out_specs=[far, here],
    )(one_s, one_d, two, got_e, got_o)
    return call(
        join,
        f32(planes, rows, cells),
        [vmem(planes // 4, rows, cells), vmem(TILES, 64, LANES), sems(4)],
        in_specs=[here, here, far],
        out_specs=far,
        input_output_aliases={2: 0},
    )(got, fourth, stay(base))


def solution(mesh):
    return jax.shard_map(
        per_device, mesh=mesh, in_specs=(P("gz", "gy", None),), out_specs=P("gz", "gy", None), check_vma=False
    )
```

```python
import functools

import jax
import jax.numpy as jnp
import ml_dtypes
import numpy as np
from jax import lax
from jax.experimental import pallas as pl
from jax.experimental.pallas import tpu as pltpu
from jax.sharding import PartitionSpec as P

A1 = -1.586134342059924
B1 = -0.052980118572961
A2 = 0.882911075530934
B2 = 0.443506852043971
GAIN = 1.230174104914001

WIDE = 1024
LANES = 128
TILES = WIDE // LANES


def lift(rows, left, right, first, last, choose):
    p, q = left
    s_next, r = right
    smooth, detail = rows[0::2], rows[1::2]
    m = len(smooth)
    s_next = choose(last, smooth[-1], s_next)
    d1 = [detail[i] + A1 * (smooth[i] + (smooth[i + 1] if i + 1 < m else s_next)) for i in range(m)]
    d1_before = choose(first, d1[0], p + A1 * smooth[0])
    s1 = [smooth[i] + B1 * ((d1[i - 1] if i else d1_before) + d1[i]) for i in range(m)]
    s1_after = choose(last, s1[-1], r + B1 * d1[-1])
    d2 = [d1[i] + A2 * (s1[i] + (s1[i + 1] if i + 1 < m else s1_after)) for i in range(m)]
    d2_before = choose(first, d2[0], d1_before + A2 * (q + B1 * d1_before + s1[0]))
    s2 = [s1[i] + B2 * ((d2[i - 1] if i else d2_before) + d2[i]) for i in range(m)]
    return [v * (1.0 / GAIN) for v in s2], [v * (GAIN / 2.0) for v in d2]


def lift_alone(rows):
    zero = jnp.zeros_like(rows[0])
    return lift(rows, (zero, zero), (zero, zero), False, False, lambda c, a, b: a if c else b)[0]


def edges(rows):
    s, d = rows[0::2], rows[1::2]
    to_right = (d[-1] + A1 * s[-1], s[-1] + B1 * (d[-2] + A1 * (s[-2] + s[-1])))
    to_left = (s[0], s[0] + B1 * (d[0] + A1 * (s[0] + s[1])))
    return to_right, to_left


def own_left(to_left):
    s, r = to_left
    c2 = (B2 * A2 * B1 * A1 / GAIN) * s
    c1 = ((B1 * A1 + B2 * A1 + 3 * B2 * A2 * B1 * A1) / GAIN) * s + (B2 * A2 / GAIN) * r
    return c1 + A1 * c2, (1 + B1 * A1) * c2


def own_right(to_right):
    p, q = to_right
    c0 = ((B1 + B2 + 3 * B2 * A2 * B1) / GAIN) * p + (B2 * A2 / GAIN) * q
    c1 = (B2 * A2 * B1 / GAIN) * p
    return c0, c0 + B1 * (c1 + A1 * c0)


def add_pairs(a, b):
    return a[0] + b[0], a[1] + b[1]


def mix(flag, a, b):
    return jnp.where(flag, a, b)


def interleave(smooth, detail):
    return [v for pair in zip(smooth, detail) for v in pair]


def filters():
    fixed = lambda c, a, b: a if c else b
    smooth, detail = lift(list(np.eye(32)), (0.0, 0.0), (0.0, 0.0), True, True, fixed)
    return [float(v) for v in smooth[8][16:21]], [float(v) for v in detail[8][17:21]]


def moved(tiles, step):
    if step == 0:
        return list(tiles)
    lane, count = lane_id(tiles[0].shape), len(tiles)
    r = [pltpu.roll(x, -step % LANES, 1) for x in tiles]
    if step > 0:
        return [jnp.where(lane < LANES - step, r[t], r[t + 1]) if t + 1 < count else r[t] for t in range(count)]
    return [jnp.where(lane >= -step, r[t], r[t - 1]) if t else r[t] for t in range(count)]


def lift_runs(v, stride):
    run = lane_id(v[0].shape) // stride
    ends = LANES // stride - 1
    at = {k: moved(v, k * stride) for k in range(-4, 5)}
    for k in range(1, 5):
        for j in range(k):
            at[-k][0] = jnp.where(run == j, at[k - 2 * j][0], at[-k][0])
    for k in range(1, 5):
        for j in range(k):
            at[k][-1] = jnp.where(run == ends - j, at[2 * j - k][-1], at[k][-1])
    smooth, detail = filters()
    weight = [jnp.where(run % 2 == 0, a, b) for a, b in zip(smooth, detail + [0.0])]
    out = [weight[0] * x for x in v]
    for k in range(1, 5):
        out = [x + weight[k] * (y + z) for x, y, z in zip(out, at[-k], at[k])]
    return out


def split_left(w):
    parts = []
    for _ in range(3):
        parts.append((w - sum(p.astype(np.float32) for p in parts)).astype(ml_dtypes.bfloat16))
    one, two, three = parts
    return np.concatenate([one, one, two, one, two, three], axis=-1)


def product(left, x):
    one = x.astype(jnp.bfloat16)
    rest = x - one.astype(jnp.float32)
    two = rest.astype(jnp.bfloat16)
    three = (rest - two.astype(jnp.float32)).astype(jnp.bfloat16)
    right = jnp.concatenate([one, two, one, three, two, one], axis=0)
    return jnp.dot(left, right, preferred_element_type=jnp.float32)


def lane_id(shape):
    return lax.broadcasted_iota(jnp.int32, shape, len(shape) - 1)


def in_even(shape):
    return lane_id(shape) % 2 == 0


def back(v):
    return pltpu.roll(v, LANES - 1, 1)


def on(v):
    return pltpu.roll(v, 1, 1)


def pack_right(p, q):
    return jnp.where(in_even(p.shape), back(q), p)


def unpack_right(v):
    return back(v), v


def pack_left(s, r):
    return jnp.where(in_even(s.shape), s, on(r))


def unpack_left(v):
    return on(v), v


def beyond_halves(left, right, to_right, to_left):
    even = in_even(to_right[0].shape)
    return (
        tuple(jnp.where(even, x, on(y)) for x, y in zip(left, to_right)),
        tuple(jnp.where(even, back(y), x) for x, y in zip(right, to_left)),
    )


def tile(t):
    return slice(t * LANES, (t + 1) * LANES)


def times(count, body, unroll=1):
    if unroll == count:
        for i in range(count):
            body(i)
        return

    def step(i, carry):
        body(i)
        return carry

    lax.fori_loop(0, count, step, 0, unroll=unroll)


def tile_lanes(t):
    return pl.ds(t * LANES if isinstance(t, int) else pl.multiple_of(t * LANES, LANES), LANES)


def lift_two(a, b, phase):
    lane = lane_id((a[0].shape[0], LANES))
    here = lane % (2 * phase) < phase
    count, reach = len(a), 2 * phase
    other = jnp.where(here, lane + phase, lane - phase)
    m = [jnp.take_along_axis(jnp.where(here, y, x), other, axis=1, mode="promise_in_bounds") for x, y in zip(a, b)]
    s = [jnp.where(here, x, y) for x, y in zip(a, m)]
    d = [jnp.where(here, y, x) for x, y in zip(b, m)]

    def ahead(x):
        r = [pltpu.roll(w, LANES - reach, 1) for w in x]
        return [jnp.where(lane < LANES - reach, r[t], r[t + 1] if t + 1 < count else x[t]) for t in range(count)]

    def behind(x):
        r = [pltpu.roll(w, reach, 1) for w in x]
        return [jnp.where(lane >= reach, r[t], r[t - 1] if t else x[t]) for t in range(count)]

    d = [x + A1 * (y + z) for x, y, z in zip(d, s, ahead(s))]
    s = [x + B1 * (y + z) for x, y, z in zip(s, d, behind(d))]
    d = [x + A2 * (y + z) for x, y, z in zip(d, s, ahead(s))]
    s = [(x + B2 * (y + z)) * (1.0 / GAIN) for x, y, z in zip(s, d, behind(d))]
    return s, [x * (GAIN / 2.0) for x in d]


def separate(s, d, phase):
    lane = lane_id(s[0].shape)
    here = lane % (2 * phase) < phase
    other = jnp.where(here, lane + phase, lane - phase)
    m = [jnp.take_along_axis(jnp.where(here, y, x), other, axis=1, mode="promise_in_bounds") for x, y in zip(s, d)]
    return [jnp.where(here, x, y) for x, y in zip(s, m)], [jnp.where(here, y, x) for x, y in zip(d, m)]


def tiles_of(ref, at):
    v = ref[at, :]
    return [v[:, tile(t)] for t in range(TILES)]


def put_tiles(ref, at, parts):
    for t, v in enumerate(parts):
        ref[at, tile(t)] = v


def along_x(
    y3, y4, z3, z4, density, smooth, detail, pay_e, pay_o, own, result, next3, next4, x, e2, e3, w3, w4, pay, load_sem, sem
):
    me, mz = lax.axis_index("gy"), lax.axis_index("gz")

    def load(k):
        at = pl.ds(pl.multiple_of(k * 32, 32), 32)
        return pltpu.make_async_copy(density.at[at], x.at[at], load_sem.at[k])

    for k in range(4):
        load(k).start()
        load(k + 4).start()
    hints = [
        pltpu.make_async_copy(y3.at[me], w3, sem.at[0]),
        pltpu.make_async_copy(y4.at[me], w4, sem.at[1]),
        pltpu.make_async_copy(z3.at[mz], next3, sem.at[2]),
        pltpu.make_async_copy(z4.at[mz], next4, sem.at[3]),
    ]
    for hint in hints:
        hint.start()

    def plane(i):
        z, y = i // 2, i % 2
        at = pl.multiple_of(z * 16 + y * 8, 8)
        far = pl.multiple_of(z * 16 + y * 8 + 128, 8)
        s, d = lift_two(tiles_of(x, pl.ds(at, 8)), tiles_of(x, pl.ds(far, 8)), 1)
        for t in range(TILES):
            smooth[t, pl.ds(at, 8), :] = s[t]
            detail[t, pl.ds(at, 8), :] = d[t]

    def group(k):
        load(k).wait()
        load(k + 4).wait()
        for i in range(4):
            plane(4 * k + i)

    times(4, group)
    for hint in hints:
        hint.wait()

    def second(i):
        at = pl.multiple_of(i * 8, 8)
        near, far = [[smooth[t, pl.ds(at + k, 8), :] for t in range(TILES)] for k in (0, 64)]
        s, _ = lift_two(near, far, 2)
        put_tiles(e2, pl.ds(at, 8), s)

    times(8, second, 8)

    def third(i):
        at = pl.multiple_of(i * 8, 8)
        s, _ = lift_two(tiles_of(e2, pl.ds(at, 8)), tiles_of(e2, pl.ds(at + 32, 8)), 4)
        put_tiles(e3, pl.ds(at, 8), s)

    times(4, third, 4)
    three = product(w3[...], e2[...])
    four = product(w4[...], e3[...])
    own[...] = three[0:16]
    for to in range(pay.shape[0]):
        right = mix(to == me + 1, three[16:24], three[24:32])
        left = mix(to == me - 1, three[32:40], three[40:48])
        pay[to, :, 0:WIDE] = mix(to > me, right, left)
        pay[to, 0:4, WIDE:] = four[to * 4 : to * 4 + 4, : WIDE // 2]
        pay[to, 4:8, WIDE:] = four[to * 4 : to * 4 + 4, WIDE // 2 :]
    send = pltpu.make_async_copy(pay, result, sem.at[4])
    send.start()
    flip = me % 2 == 1

    def column(t):
        lanes = tile_lanes(t)
        rows = [smooth[t, pl.ds(y, 8, stride=16), :] for y in range(16)]
        parts = [edges(rows), edges(lift_alone(rows))]
        parts.append(edges([detail[t, pl.ds(y, 8, stride=16), :] for y in range(16)]))
        for c in range(6):
            right, left = [parts[c // 2][side][c % 2] for side in range(2)]
            pay_e[c, :, lanes] = mix(flip, left, right)
            pay_o[c, :, lanes] = mix(flip, right, left)

    times(TILES, column, 4)
    send.wait()


def along_y(smooth, detail, got_e, got_o, one_s, one_d, two, pay_e, pay_o, cells, thick):
    me = lax.axis_index("gy")
    first, last, flip = me == 0, me == lax.axis_size("gy") - 1, me % 2 == 1

    def column(t):
        lanes = tile_lanes(t)
        e = [got_e[c, :, lanes] for c in range(6)]
        o = [got_o[c, :, lanes] for c in range(6)]
        left = [mix(flip, e[c], o[c]) for c in range(6)]
        right = [mix(flip, o[c], e[c]) for c in range(6)]
        for k, (source, to) in enumerate(((detail, one_d), (smooth, one_s))):
            rows = [source[t, pl.ds(y, 8, stride=16), :] for y in range(16)]
            at = slice(0, 2) if k else slice(4, 6)
            low, high = lift(rows, left[at], right[at], first, last, mix)
            for y, v in enumerate(interleave(low, high)):
                to[t, pl.ds(y, 8, stride=16), :] = v
        to_right, to_left = edges(rows)
        left2, right2 = add_pairs(left[2:4], own_left(to_left)), add_pairs(right[2:4], own_right(to_right))
        low, high = lift(low, left2, right2, first, last, mix)
        for y, v in enumerate(interleave(low, high)):
            two[t, pl.ds(y, 8, stride=8), :] = v
        for r, v in enumerate(low):
            thick[pl.ds(4 * r, 4), lanes] = v[0:4]
            thick[pl.ds(16 + 4 * r, 4), lanes] = v[4:8]

    times(TILES, column, TILES)
    flip = lax.axis_index("gz") % 2 == 1

    def stack(t):
        lanes = tile_lanes(t)
        going_right, going_left = [], []

        def add(rows):
            to_right, to_left = edges(rows)
            going_right.append(pack_right(*to_right))
            going_left.append(pack_left(*to_left))
            return to_right, to_left

        for source in (one_s, one_d):
            for half in range(2):
                add([source[t, pl.ds(z * 16 + half * 8, 8), :] for z in range(8)])
        rows = [two[t, pl.ds(z * 8, 8), :] for z in range(8)]
        nothing = jnp.zeros_like(rows[0])
        left, right = beyond_halves((nothing, nothing), (nothing, nothing), *add(rows))
        add(lift(rows, left, right, False, False, lambda c, a, b: b)[0])
        for c in range(6):
            pay_e[c, :, lanes] = mix(flip, going_left[c], going_right[c])
            pay_o[c, :, lanes] = mix(flip, going_right[c], going_left[c])

    times(TILES, stack, TILES)
    for i in range(2):
        s, _ = lift_two(tiles_of(thick, pl.ds(8 * i, 8)), tiles_of(thick, pl.ds(16 + 8 * i, 8)), 2)
        put_tiles(cells, pl.ds(8 * i, 8), s)


def thin_z(w3, w4, cells, own, got, result, pay, beyond, held4, turned3, turned4, sem):
    me, count = lax.axis_index("gy"), got.shape[0]
    first, last = me == 0, me == count - 1
    near = lambda k: got[jnp.clip(me + k, 0, count - 1), :, 0:WIDE]
    beyond[0:8] = own[0:8] + (mix(me >= 1, near(-1), 0.0) + mix(me >= 2, near(-2), 0.0))
    beyond[8:16] = own[8:16] + (mix(me < count - 1, near(1), 0.0) + mix(me < count - 2, near(2), 0.0))
    four = got[0, :, WIDE:]
    for k in range(1, count):
        four = four + got[k, :, WIDE:]
    held4[:, 0 : WIDE // 2] = four[0:4]
    held4[:, WIDE // 2 :] = four[4:8]
    lane = lane_id((4, LANES))
    for t in range(TILES):
        at = lambda r: pl.ds(4 * r, 4)
        p, q, s, r = [beyond[at(c), tile(t)] for c in range(4)]
        rows = [cells[at(c), tile(t)] for c in range(4)]
        rows = interleave(*lift(rows, (p, q), (s, r), first, last, mix))
        for f in range(4):
            v = None
            for r in range(4):
                moved = pltpu.roll(rows[r], (r - f) % LANES, 1) if r != f else rows[r]
                v = jnp.where(lane % 4 == r, moved, v) if r else moved
            turned3[at(f), tile(t)] = v
        v = held4[:, tile(t)]
        for f in range(8):
            turned4[at(f), tile(t)] = pltpu.roll(v, LANES - f, 1) if f else v
    count = pay.shape[0]
    parts = [pl.ds(0, WIDE), pl.ds(WIDE, LANES)]
    sends = [pltpu.make_async_copy(pay.at[:, :, p], result.at[:, :, p], sem.at[k]) for k, p in enumerate(parts)]
    three = product(w3[...], turned3[...])
    four = product(w4[...], turned4[...])
    for to in range(count):
        pay[to, :, 0:WIDE] = three[to * 4 : to * 4 + 4]
    sends[0].start()
    lane = lane_id((count, LANES))
    for t in range(TILES // 2):
        v = four[0:count, tile(t)]
        for k in range(1, 8):
            w = four[k % 4 * count : (k % 4 + 1) * count, tile(t + k // 4 * (TILES // 2))]
            v = jnp.where(lane % 8 == k, pltpu.roll(w, k, 1), v)
        pay[:, t, WIDE:] = v
    sends[1].start()
    for send in sends:
        send.wait()


def along_z(one_s, one_d, two, got_e, got_o, result, fourth, out, fine, spread, sem):
    me = lax.axis_index("gz")
    flip, side = me % 2 == 1, lane_id((8, LANES)) % 2
    first = side == jnp.where(me == 0, 0, 2)
    last = side == jnp.where(me == lax.axis_size("gz") - 1, 1, 2)

    def stack(t):
        lanes = tile_lanes(t)
        e = [got_e[c, :, lanes] for c in range(6)]
        o = [got_o[c, :, lanes] for c in range(6)]
        left = [unpack_right(mix(flip, e[c], o[c])) for c in range(6)]
        right = [unpack_left(mix(flip, o[c], e[c])) for c in range(6)]
        for half in range(2):
            lifted = []
            for k, source in enumerate((one_s, one_d)):
                rows = [source[t, pl.ds(z * 16 + half * 8, 8), :] for z in range(8)]
                ends = beyond_halves(left[2 * k + half], right[2 * k + half], *edges(rows))
                lifted.append(interleave(*lift(rows, *ends, first, last, mix)))
            near, far = separate(*lifted, 1)
            for z in range(8):
                out[z, pl.ds(half * 8, 8), lanes] = near[z]
                out[z + 8, pl.ds(half * 8, 8), lanes] = far[z]
        rows = [two[t, pl.ds(z * 8, 8), :] for z in range(8)]
        to_right, to_left = edges(rows)
        rows, _ = lift(rows, *beyond_halves(left[4], right[4], to_right, to_left), first, last, mix)
        left2, right2 = add_pairs(left[5], own_left(to_left)), add_pairs(right[5], own_right(to_right))
        ends = beyond_halves(left2, right2, *edges(rows))
        for z, v in enumerate(interleave(*lift(rows, *ends, first, last, mix))):
            fine[pl.ds(z * 8, 8), lanes] = v

    times(TILES, stack, TILES)
    sends = {z: pltpu.make_async_copy(out.at[z], result.at[z], sem.at[z]) for z in range(16) if z % 4}
    for z in range(1, 16, 2):
        sends[z].start()
    row = lax.broadcasted_iota(jnp.int32, (16, LANES), 0)
    here = (row % 2 == 0) & in_even((16, LANES))
    for i in (1, 3, 0, 2):
        v = lift_runs(tiles_of(fine, pl.ds(i * 8, 8)), 2)
        for z in (i, i + 4):
            for t in range(TILES):
                spread[t, pl.ds(z * 16, 8, stride=2), :] = v[t] if z == i else back(v[t])
                w = jnp.where(here, spread[t, pl.ds(z * 16, 16), :], out[2 * z, :, tile(t)])
                if z % 2:
                    out[2 * z, :, tile(t)] = w
                else:
                    fourth[z // 2, :, tile(t)] = w
            if z % 2:
                sends[2 * z].start()
    for send in sends.values():
        send.wait()


def join(got, fourth, base, result, planes, spread, sem):
    total = got[0]
    for k in range(1, got.shape[0]):
        total = total + got[k]
    three = lift_runs([total[:, tile(t)] for t in range(TILES)], 4)
    four = [total[t : t + 1, WIDE:] for t in range(TILES // 2)]
    four = lift_runs(four + [pltpu.roll(x, LANES - 4, 1) for x in four], 8)
    lane = lane_id((4, LANES))
    row = lax.broadcasted_iota(jnp.int32, (4, LANES), 0)
    for t in range(TILES):
        for r in range(4):
            v = pltpu.roll(three[t], LANES - r, 1) if r else three[t]
            for k in range(r // 2, 4, 2) if r % 2 == 0 else ():
                w = pltpu.roll(four[t], LANES - k, 1) if k else four[t]
                v = jnp.where((lane % 8 == 0) & (row == 2 * (k // 2)), jnp.broadcast_to(w, v.shape), v)
            spread[t, pl.ds(4 * r, 4, stride=16), :] = v
    row = lax.broadcasted_iota(jnp.int32, (16, LANES), 0)
    here = (row % 4 == 0) & (lane_id((16, LANES)) % 4 == 0)
    sends = [pltpu.make_async_copy(planes.at[i], result.at[4 * i], sem.at[i]) for i in range(4)]
    for i in range(4):
        for t in range(TILES):
            planes[i, :, tile(t)] = jnp.where(here, spread[t, pl.ds(i * 16, 16), :], fourth[i, :, tile(t)])
        sends[i].start()
    for send in sends:
        send.wait()


def deep_levels(n):
    fixed = lambda c, a, b: a if c else b
    level = lambda rows: lift(rows, (0.0, 0.0), (0.0, 0.0), True, True, fixed)
    cells = level(level(list(np.eye(n)))[0])[0]
    smooth, detail = level(cells)
    return cells, np.stack(interleave(smooth, detail)), np.stack(interleave(*level(smooth)))


def weights_y(devices):
    cells, _, four = deep_levels(16 * devices)
    w3 = np.zeros((devices, 48, 4, 16), np.float64)
    w4 = np.zeros((devices, devices, 2, 2, 2, 16), np.float64)
    for a in range(devices):
        mine = slice(16 * a, 16 * a + 16)
        for row, side, b in ((0, 0, -1), (8, 1, 1), (16, 0, 0), (24, 0, 1), (32, 1, 0), (40, 1, -1)):
            if 0 <= a + b < devices:
                pair = edges(cells[4 * (a + b) : 4 * (a + b) + 4])[side]
                for c in range(2):
                    for z in range(4):
                        w3[a, row + 4 * c + z, z] = pair[c][mine]
        for z in range(2):
            w4[a, :, :, z, z] = four[:, mine].reshape(devices, 2, 16)
    return (
        split_left(w3.reshape(devices, 48, 64).astype(np.float32)),
        split_left(w4.reshape(devices, 4 * devices, 32).astype(np.float32)),
    )


def weights_z(devices):
    _, three, four = deep_levels(16 * devices)
    w3 = np.zeros((devices, devices, 4, 4, 4), np.float64)
    w4 = np.zeros((devices, 2, 2, devices, 8, 2, 2), np.float64)
    for a in range(devices):
        for f in range(8):
            for zz in range(4):
                if f < 4:
                    z = 16 * a + zz + 4 * (f // 2) + 8 * (f % 2)
                    w3[a, :, :, f, zz] = three[:, z].reshape(devices, 4)
                if zz < 2:
                    z = 16 * a + zz + 2 * (f // 4) + 4 * (f // 2 % 2) + 8 * (f % 2)
                    for o in range(2):
                        w4[a, :, o, :, f, o, zz] = four[:, z].reshape(devices, 2).T
    return (
        split_left(w3.reshape(devices, 4 * devices, 16).astype(np.float32)),
        split_left(w4.reshape(devices, 4 * devices, 32).astype(np.float32)),
    )


def swap(values, axis, start):
    devices = lax.axis_size(axis)
    pairs = []
    for i in range(start, devices - 1, 2):
        pairs += [(i, i + 1), (i + 1, i)]
    return lax.ppermute(values, axis, pairs)


def f32(*shape):
    return jax.ShapeDtypeStruct(shape, jnp.float32)


def bf16(*shape):
    return jax.ShapeDtypeStruct(shape, jnp.bfloat16)


def call(body, out, scratch=(), cost=4 << 20, **more):
    return pl.pallas_call(
        body,
        out_shape=out,
        scratch_shapes=list(scratch),
        cost_estimate=pl.CostEstimate(flops=cost * 10, bytes_accessed=4 << 20, transcendentals=0),
        compiler_params=pltpu.CompilerParams(vmem_limit_bytes=24 * 1024 * 1024),
        **more,
    )


def per_device(density):
    planes, rows, cells = density.shape
    ny, nz = lax.axis_size("gy"), lax.axis_size("gz")
    vmem = lambda *shape: pltpu.VMEM(shape, jnp.float32)
    sems = lambda count: pltpu.SemaphoreType.DMA((count,))
    far, here = pl.BlockSpec(memory_space=pltpu.HBM), pl.BlockSpec(memory_space=pltpu.VMEM)
    stay = lambda v: pltpu.with_memory_space_constraint(jnp.asarray(v), pltpu.HBM)
    tiled = f32(TILES, planes * rows // 2, LANES)
    payload = f32(6, 8, cells)
    pay = (ny, 8, cells * 3 // 2)
    smooth, detail, pay_e, pay_o, own, pay, z3, z4 = call(
        along_x,
        [tiled, tiled, payload, payload, f32(16, cells), f32(*pay), bf16(4 * nz, 6 * 16), bf16(4 * nz, 6 * 32)],
        [
            vmem(planes * rows, cells),
            vmem(64, cells),
            vmem(32, cells),
            pltpu.VMEM((48, 6 * 64), jnp.bfloat16),
            pltpu.VMEM((4 * ny, 6 * 32), jnp.bfloat16),
            vmem(*pay),
            sems(8),
            sems(5),
        ],
        in_specs=[far] * 5,
        out_specs=[here] * 5 + [far, here, here],
    )(*[stay(w) for w in weights_y(ny) + weights_z(nz)], stay(density.reshape(planes * rows, cells)))
    got_e, got_o = swap(pay_e, "gy", 0), swap(pay_o, "gy", 1)
    got = lax.all_to_all(pay, "gy", 0, 0, tiled=True)

    one_s, one_d, two, pay_e, pay_o, third = call(
        along_y,
        [tiled, tiled, f32(TILES, planes * rows // 4, LANES), payload, payload, f32(16, cells)],
        [vmem(32, cells)],
        cost=400 << 20,
        input_output_aliases={0: 0, 1: 1},
    )(smooth, detail, got_e, got_o)
    got_e, got_o = swap(pay_e, "gz", 0), swap(pay_o, "gz", 1)
    pay = (nz, 4, cells + LANES)
    pay = call(
        thin_z,
        f32(*pay),
        [vmem(*pay), vmem(16, cells), vmem(4, cells), vmem(16, cells), vmem(32, cells), sems(2)],
        cost=40 << 20,
        out_specs=far,
    )(z3, z4, third, own, got)
    got = lax.all_to_all(pay, "gz", 0, 0, tiled=True)

    base, fourth = call(
        along_z,
        [f32(planes, rows, cells), f32(planes // 4, rows, cells)],
        [vmem(planes, rows, cells), vmem(32, cells), vmem(TILES, 128, LANES), sems(planes)],
        cost=400 << 20,
        out_specs=[far, here],
    )(one_s, one_d, two, got_e, got_o)
    return call(
        join,
        f32(planes, rows, cells),
        [vmem(planes // 4, rows, cells), vmem(TILES, 64, LANES), sems(4)],
        in_specs=[here, here, far],
        out_specs=far,
        input_output_aliases={2: 0},
    )(got, fourth, stay(base))


def solution(mesh):
    return jax.shard_map(
        per_device, mesh=mesh, in_specs=(P("gz", "gy", None),), out_specs=P("gz", "gy", None), check_vma=False
    )
```

```python
import functools

import jax
import jax.numpy as jnp
import ml_dtypes
import numpy as np
from jax import lax
from jax.experimental import pallas as pl
from jax.experimental.pallas import tpu as pltpu
from jax.sharding import PartitionSpec as P

A1 = -1.586134342059924
B1 = -0.052980118572961
A2 = 0.882911075530934
B2 = 0.443506852043971
GAIN = 1.230174104914001

WIDE = 1024
LANES = 128
TILES = WIDE // LANES


def lift(rows, left, right, first, last, choose):
    p, q = left
    s_next, r = right
    smooth, detail = rows[0::2], rows[1::2]
    m = len(smooth)
    s_next = choose(last, smooth[-1], s_next)
    d1 = [detail[i] + A1 * (smooth[i] + (smooth[i + 1] if i + 1 < m else s_next)) for i in range(m)]
    d1_before = choose(first, d1[0], p + A1 * smooth[0])
    s1 = [smooth[i] + B1 * ((d1[i - 1] if i else d1_before) + d1[i]) for i in range(m)]
    s1_after = choose(last, s1[-1], r + B1 * d1[-1])
    d2 = [d1[i] + A2 * (s1[i] + (s1[i + 1] if i + 1 < m else s1_after)) for i in range(m)]
    d2_before = choose(first, d2[0], d1_before + A2 * (q + B1 * d1_before + s1[0]))
    s2 = [s1[i] + B2 * ((d2[i - 1] if i else d2_before) + d2[i]) for i in range(m)]
    return [v * (1.0 / GAIN) for v in s2], [v * (GAIN / 2.0) for v in d2]


def lift_alone(rows):
    zero = jnp.zeros_like(rows[0])
    return lift(rows, (zero, zero), (zero, zero), False, False, lambda c, a, b: a if c else b)[0]


def edges(rows):
    s, d = rows[0::2], rows[1::2]
    to_right = (d[-1] + A1 * s[-1], s[-1] + B1 * (d[-2] + A1 * (s[-2] + s[-1])))
    to_left = (s[0], s[0] + B1 * (d[0] + A1 * (s[0] + s[1])))
    return to_right, to_left


def own_left(to_left):
    s, r = to_left
    c2 = (B2 * A2 * B1 * A1 / GAIN) * s
    c1 = ((B1 * A1 + B2 * A1 + 3 * B2 * A2 * B1 * A1) / GAIN) * s + (B2 * A2 / GAIN) * r
    return c1 + A1 * c2, (1 + B1 * A1) * c2


def own_right(to_right):
    p, q = to_right
    c0 = ((B1 + B2 + 3 * B2 * A2 * B1) / GAIN) * p + (B2 * A2 / GAIN) * q
    c1 = (B2 * A2 * B1 / GAIN) * p
    return c0, c0 + B1 * (c1 + A1 * c0)


def add_pairs(a, b):
    return a[0] + b[0], a[1] + b[1]


def mix(flag, a, b):
    return jnp.where(flag, a, b)


def interleave(smooth, detail):
    return [v for pair in zip(smooth, detail) for v in pair]


def filters():
    fixed = lambda c, a, b: a if c else b
    smooth, detail = lift(list(np.eye(32)), (0.0, 0.0), (0.0, 0.0), True, True, fixed)
    return [float(v) for v in smooth[8][16:21]], [float(v) for v in detail[8][17:21]]


def moved(tiles, step):
    if step == 0:
        return list(tiles)
    lane, count = lane_id(tiles[0].shape), len(tiles)
    r = [pltpu.roll(x, -step % LANES, 1) for x in tiles]
    if step > 0:
        return [jnp.where(lane < LANES - step, r[t], r[t + 1]) if t + 1 < count else r[t] for t in range(count)]
    return [jnp.where(lane >= -step, r[t], r[t - 1]) if t else r[t] for t in range(count)]


def lift_runs(v, stride):
    run = lane_id(v[0].shape) // stride
    ends = LANES // stride - 1
    at = {k: moved(v, k * stride) for k in range(-4, 5)}
    for k in range(1, 5):
        for j in range(k):
            at[-k][0] = jnp.where(run == j, at[k - 2 * j][0], at[-k][0])
    for k in range(1, 5):
        for j in range(k):
            at[k][-1] = jnp.where(run == ends - j, at[2 * j - k][-1], at[k][-1])
    smooth, detail = filters()
    weight = [jnp.where(run % 2 == 0, a, b) for a, b in zip(smooth, detail + [0.0])]
    out = [weight[0] * x for x in v]
    for k in range(1, 5):
        out = [x + weight[k] * (y + z) for x, y, z in zip(out, at[-k], at[k])]
    return out


def split_left(w):
    parts = []
    for _ in range(3):
        parts.append((w - sum(p.astype(np.float32) for p in parts)).astype(ml_dtypes.bfloat16))
    one, two, three = parts
    return np.concatenate([one, one, two, one, two, three], axis=-1)


def product(left, x):
    one = x.astype(jnp.bfloat16)
    rest = x - one.astype(jnp.float32)
    two = rest.astype(jnp.bfloat16)
    three = (rest - two.astype(jnp.float32)).astype(jnp.bfloat16)
    right = jnp.concatenate([one, two, one, three, two, one], axis=0)
    return jnp.dot(left, right, preferred_element_type=jnp.float32)


def lane_id(shape):
    return lax.broadcasted_iota(jnp.int32, shape, len(shape) - 1)


def in_even(shape):
    return lane_id(shape) % 2 == 0


def back(v):
    return pltpu.roll(v, LANES - 1, 1)


def on(v):
    return pltpu.roll(v, 1, 1)


def pack_right(p, q):
    return jnp.where(in_even(p.shape), back(q), p)


def unpack_right(v):
    return back(v), v


def pack_left(s, r):
    return jnp.where(in_even(s.shape), s, on(r))


def unpack_left(v):
    return on(v), v


def beyond_halves(left, right, to_right, to_left):
    even = in_even(to_right[0].shape)
    return (
        tuple(jnp.where(even, x, on(y)) for x, y in zip(left, to_right)),
        tuple(jnp.where(even, back(y), x) for x, y in zip(right, to_left)),
    )


def tile(t):
    return slice(t * LANES, (t + 1) * LANES)


def times(count, body, unroll=1):
    if unroll == count:
        for i in range(count):
            body(i)
        return

    def step(i, carry):
        body(i)
        return carry

    lax.fori_loop(0, count, step, 0, unroll=unroll)


def tile_lanes(t):
    return pl.ds(t * LANES if isinstance(t, int) else pl.multiple_of(t * LANES, LANES), LANES)


def lift_two(a, b, phase):
    lane = lane_id((a[0].shape[0], LANES))
    here = lane % (2 * phase) < phase
    count, reach = len(a), 2 * phase
    other = jnp.where(here, lane + phase, lane - phase)
    m = [jnp.take_along_axis(jnp.where(here, y, x), other, axis=1, mode="promise_in_bounds") for x, y in zip(a, b)]
    s = [jnp.where(here, x, y) for x, y in zip(a, m)]
    d = [jnp.where(here, y, x) for x, y in zip(b, m)]

    def ahead(x):
        r = [pltpu.roll(w, LANES - reach, 1) for w in x]
        return [jnp.where(lane < LANES - reach, r[t], r[t + 1] if t + 1 < count else x[t]) for t in range(count)]

    def behind(x):
        r = [pltpu.roll(w, reach, 1) for w in x]
        return [jnp.where(lane >= reach, r[t], r[t - 1] if t else x[t]) for t in range(count)]

    d = [x + A1 * (y + z) for x, y, z in zip(d, s, ahead(s))]
    s = [x + B1 * (y + z) for x, y, z in zip(s, d, behind(d))]
    d = [x + A2 * (y + z) for x, y, z in zip(d, s, ahead(s))]
    s = [(x + B2 * (y + z)) * (1.0 / GAIN) for x, y, z in zip(s, d, behind(d))]
    return s, [x * (GAIN / 2.0) for x in d]


def separate(s, d, phase):
    lane = lane_id(s[0].shape)
    here = lane % (2 * phase) < phase
    other = jnp.where(here, lane + phase, lane - phase)
    m = [jnp.take_along_axis(jnp.where(here, y, x), other, axis=1, mode="promise_in_bounds") for x, y in zip(s, d)]
    return [jnp.where(here, x, y) for x, y in zip(s, m)], [jnp.where(here, y, x) for x, y in zip(d, m)]


def tiles_of(ref, at):
    v = ref[at, :]
    return [v[:, tile(t)] for t in range(TILES)]


def put_tiles(ref, at, parts):
    for t, v in enumerate(parts):
        ref[at, tile(t)] = v


def along_x(
    y3, y4, z3, z4, density, smooth, detail, pay_e, pay_o, own, result, next3, next4, x, e2, e3, w3, w4, pay, load_sem, sem
):
    me, mz = lax.axis_index("gy"), lax.axis_index("gz")

    def load(k):
        at = pl.ds(pl.multiple_of(k * 32, 32), 32)
        return pltpu.make_async_copy(density.at[at], x.at[at], load_sem.at[k])

    for k in range(4):
        load(k).start()
        load(k + 4).start()
    hints = [
        pltpu.make_async_copy(y3.at[me], w3, sem.at[0]),
        pltpu.make_async_copy(y4.at[me], w4, sem.at[1]),
        pltpu.make_async_copy(z3.at[mz], next3, sem.at[2]),
        pltpu.make_async_copy(z4.at[mz], next4, sem.at[3]),
    ]
    for hint in hints:
        hint.start()

    def plane(i):
        z, y = i // 2, i % 2
        at = pl.multiple_of(z * 16 + y * 8, 8)
        far = pl.multiple_of(z * 16 + y * 8 + 128, 8)
        s, d = lift_two(tiles_of(x, pl.ds(at, 8)), tiles_of(x, pl.ds(far, 8)), 1)
        for t in range(TILES):
            smooth[t, pl.ds(at, 8), :] = s[t]
            detail[t, pl.ds(at, 8), :] = d[t]

    def group(k):
        for j in range(2):
            load(2 * k + j).wait()
            load(2 * k + j + 4).wait()
        for i in range(8):
            plane(8 * k + i)

    times(2, group)
    for hint in hints:
        hint.wait()

    def second(i):
        at = pl.multiple_of(i * 8, 8)
        near, far = [[smooth[t, pl.ds(at + k, 8), :] for t in range(TILES)] for k in (0, 64)]
        s, _ = lift_two(near, far, 2)
        put_tiles(e2, pl.ds(at, 8), s)

    times(8, second, 8)

    def third(i):
        at = pl.multiple_of(i * 8, 8)
        s, _ = lift_two(tiles_of(e2, pl.ds(at, 8)), tiles_of(e2, pl.ds(at + 32, 8)), 4)
        put_tiles(e3, pl.ds(at, 8), s)

    times(4, third, 4)
    three = product(w3[...], e2[...])
    four = product(w4[...], e3[...])
    own[...] = three[0:16]
    for to in range(pay.shape[0]):
        right = mix(to == me + 1, three[16:24], three[24:32])
        left = mix(to == me - 1, three[32:40], three[40:48])
        pay[to, :, 0:WIDE] = mix(to > me, right, left)
    parts = [pl.ds(0, WIDE), pl.ds(WIDE, WIDE // 2)]
    sends = [pltpu.make_async_copy(pay.at[:, :, p], result.at[:, :, p], sem.at[4 + k]) for k, p in enumerate(parts)]
    sends[0].start()
    for to in range(pay.shape[0]):
        pay[to, 0:4, WIDE:] = four[to * 4 : to * 4 + 4, : WIDE // 2]
        pay[to, 4:8, WIDE:] = four[to * 4 : to * 4 + 4, WIDE // 2 :]
    sends[1].start()
    flip = me % 2 == 1

    def column(t):
        lanes = tile_lanes(t)
        rows = [smooth[t, pl.ds(y, 8, stride=16), :] for y in range(16)]
        parts = [edges(rows), edges(lift_alone(rows))]
        parts.append(edges([detail[t, pl.ds(y, 8, stride=16), :] for y in range(16)]))
        for c in range(6):
            right, left = [parts[c // 2][side][c % 2] for side in range(2)]
            pay_e[c, :, lanes] = mix(flip, left, right)
            pay_o[c, :, lanes] = mix(flip, right, left)

    times(TILES, column, 4)
    for send in sends:
        send.wait()


def along_y(smooth, detail, got_e, got_o, one_s, one_d, two, pay_e, pay_o, cells, thick):
    me = lax.axis_index("gy")
    first, last, flip = me == 0, me == lax.axis_size("gy") - 1, me % 2 == 1

    def column(t):
        lanes = tile_lanes(t)
        e = [got_e[c, :, lanes] for c in range(6)]
        o = [got_o[c, :, lanes] for c in range(6)]
        left = [mix(flip, e[c], o[c]) for c in range(6)]
        right = [mix(flip, o[c], e[c]) for c in range(6)]
        for k, (source, to) in enumerate(((detail, one_d), (smooth, one_s))):
            rows = [source[t, pl.ds(y, 8, stride=16), :] for y in range(16)]
            at = slice(0, 2) if k else slice(4, 6)
            low, high = lift(rows, left[at], right[at], first, last, mix)
            for y, v in enumerate(interleave(low, high)):
                to[t, pl.ds(y, 8, stride=16), :] = v
        to_right, to_left = edges(rows)
        left2, right2 = add_pairs(left[2:4], own_left(to_left)), add_pairs(right[2:4], own_right(to_right))
        low, high = lift(low, left2, right2, first, last, mix)
        for y, v in enumerate(interleave(low, high)):
            two[t, pl.ds(y, 8, stride=8), :] = v
        for r, v in enumerate(low):
            thick[pl.ds(4 * r, 4), lanes] = v[0:4]
            thick[pl.ds(16 + 4 * r, 4), lanes] = v[4:8]

    times(TILES, column, TILES)
    flip = lax.axis_index("gz") % 2 == 1

    def stack(t):
        lanes = tile_lanes(t)
        going_right, going_left = [], []

        def add(rows):
            to_right, to_left = edges(rows)
            going_right.append(pack_right(*to_right))
            going_left.append(pack_left(*to_left))
            return to_right, to_left

        for source in (one_s, one_d):
            for half in range(2):
                add([source[t, pl.ds(z * 16 + half * 8, 8), :] for z in range(8)])
        rows = [two[t, pl.ds(z * 8, 8), :] for z in range(8)]
        nothing = jnp.zeros_like(rows[0])
        left, right = beyond_halves((nothing, nothing), (nothing, nothing), *add(rows))
        add(lift(rows, left, right, False, False, lambda c, a, b: b)[0])
        for c in range(6):
            pay_e[c, :, lanes] = mix(flip, going_left[c], going_right[c])
            pay_o[c, :, lanes] = mix(flip, going_right[c], going_left[c])

    times(TILES, stack, TILES)
    for i in range(2):
        s, _ = lift_two(tiles_of(thick, pl.ds(8 * i, 8)), tiles_of(thick, pl.ds(16 + 8 * i, 8)), 2)
        put_tiles(cells, pl.ds(8 * i, 8), s)


def thin_z(w3, w4, cells, own, got, result, pay, beyond, held4, turned3, turned4, sem):
    me, count = lax.axis_index("gy"), got.shape[0]
    first, last = me == 0, me == count - 1
    near = lambda k: got[jnp.clip(me + k, 0, count - 1), :, 0:WIDE]
    beyond[0:8] = own[0:8] + (mix(me >= 1, near(-1), 0.0) + mix(me >= 2, near(-2), 0.0))
    beyond[8:16] = own[8:16] + (mix(me < count - 1, near(1), 0.0) + mix(me < count - 2, near(2), 0.0))
    four = got[0, :, WIDE:]
    for k in range(1, count):
        four = four + got[k, :, WIDE:]
    held4[:, 0 : WIDE // 2] = four[0:4]
    held4[:, WIDE // 2 :] = four[4:8]
    lane = lane_id((4, LANES))
    for t in range(TILES):
        at = lambda r: pl.ds(4 * r, 4)
        p, q, s, r = [beyond[at(c), tile(t)] for c in range(4)]
        rows = [cells[at(c), tile(t)] for c in range(4)]
        rows = interleave(*lift(rows, (p, q), (s, r), first, last, mix))
        for f in range(4):
            v = None
            for r in range(4):
                moved = pltpu.roll(rows[r], (r - f) % LANES, 1) if r != f else rows[r]
                v = jnp.where(lane % 4 == r, moved, v) if r else moved
            turned3[at(f), tile(t)] = v
        v = held4[:, tile(t)]
        for f in range(8):
            turned4[at(f), tile(t)] = pltpu.roll(v, LANES - f, 1) if f else v
    count = pay.shape[0]
    parts = [pl.ds(0, WIDE), pl.ds(WIDE, LANES)]
    sends = [pltpu.make_async_copy(pay.at[:, :, p], result.at[:, :, p], sem.at[k]) for k, p in enumerate(parts)]
    three = product(w3[...], turned3[...])
    four = product(w4[...], turned4[...])
    for to in range(count):
        pay[to, :, 0:WIDE] = three[to * 4 : to * 4 + 4]
    sends[0].start()
    lane = lane_id((count, LANES))
    for t in range(TILES // 2):
        v = four[0:count, tile(t)]
        for k in range(1, 8):
            w = four[k % 4 * count : (k % 4 + 1) * count, tile(t + k // 4 * (TILES // 2))]
            v = jnp.where(lane % 8 == k, pltpu.roll(w, k, 1), v)
        pay[:, t, WIDE:] = v
    sends[1].start()
    for send in sends:
        send.wait()


def along_z(one_s, one_d, two, got_e, got_o, result, fourth, out, fine, spread, sem):
    me = lax.axis_index("gz")
    flip, side = me % 2 == 1, lane_id((8, LANES)) % 2
    first = side == jnp.where(me == 0, 0, 2)
    last = side == jnp.where(me == lax.axis_size("gz") - 1, 1, 2)

    def stack(t):
        lanes = tile_lanes(t)
        e = [got_e[c, :, lanes] for c in range(6)]
        o = [got_o[c, :, lanes] for c in range(6)]
        left = [unpack_right(mix(flip, e[c], o[c])) for c in range(6)]
        right = [unpack_left(mix(flip, o[c], e[c])) for c in range(6)]
        for half in range(2):
            lifted = []
            for k, source in enumerate((one_s, one_d)):
                rows = [source[t, pl.ds(z * 16 + half * 8, 8), :] for z in range(8)]
                ends = beyond_halves(left[2 * k + half], right[2 * k + half], *edges(rows))
                lifted.append(interleave(*lift(rows, *ends, first, last, mix)))
            near, far = separate(*lifted, 1)
            for z in range(8):
                out[z, pl.ds(half * 8, 8), lanes] = near[z]
                out[z + 8, pl.ds(half * 8, 8), lanes] = far[z]
        rows = [two[t, pl.ds(z * 8, 8), :] for z in range(8)]
        to_right, to_left = edges(rows)
        rows, _ = lift(rows, *beyond_halves(left[4], right[4], to_right, to_left), first, last, mix)
        left2, right2 = add_pairs(left[5], own_left(to_left)), add_pairs(right[5], own_right(to_right))
        ends = beyond_halves(left2, right2, *edges(rows))
        for z, v in enumerate(interleave(*lift(rows, *ends, first, last, mix))):
            fine[pl.ds(z * 8, 8), lanes] = v

    times(TILES, stack, TILES)
    sends = {z: pltpu.make_async_copy(out.at[z], result.at[z], sem.at[z]) for z in range(16) if z % 4}
    for z in range(1, 16, 2):
        sends[z].start()
    row = lax.broadcasted_iota(jnp.int32, (16, LANES), 0)
    here = (row % 2 == 0) & in_even((16, LANES))
    for i in (1, 3, 0, 2):
        v = lift_runs(tiles_of(fine, pl.ds(i * 8, 8)), 2)
        for z in (i, i + 4):
            for t in range(TILES):
                spread[t, pl.ds(z * 16, 8, stride=2), :] = v[t] if z == i else back(v[t])
                w = jnp.where(here, spread[t, pl.ds(z * 16, 16), :], out[2 * z, :, tile(t)])
                if z % 2:
                    out[2 * z, :, tile(t)] = w
                else:
                    fourth[z // 2, :, tile(t)] = w
            if z % 2:
                sends[2 * z].start()
    for send in sends.values():
        send.wait()


def join(got, fourth, base, result, planes, spread, sem):
    total = got[0]
    for k in range(1, got.shape[0]):
        total = total + got[k]
    three = lift_runs([total[:, tile(t)] for t in range(TILES)], 4)
    four = [total[t : t + 1, WIDE:] for t in range(TILES // 2)]
    four = lift_runs(four + [pltpu.roll(x, LANES - 4, 1) for x in four], 8)
    lane = lane_id((4, LANES))
    row = lax.broadcasted_iota(jnp.int32, (4, LANES), 0)
    for t in range(TILES):
        for r in range(4):
            v = pltpu.roll(three[t], LANES - r, 1) if r else three[t]
            for k in range(r // 2, 4, 2) if r % 2 == 0 else ():
                w = pltpu.roll(four[t], LANES - k, 1) if k else four[t]
                v = jnp.where((lane % 8 == 0) & (row == 2 * (k // 2)), jnp.broadcast_to(w, v.shape), v)
            spread[t, pl.ds(4 * r, 4, stride=16), :] = v
    row = lax.broadcasted_iota(jnp.int32, (16, LANES), 0)
    here = (row % 4 == 0) & (lane_id((16, LANES)) % 4 == 0)
    sends = [pltpu.make_async_copy(planes.at[i], result.at[4 * i], sem.at[i]) for i in range(4)]
    for i in range(4):
        for t in range(TILES):
            planes[i, :, tile(t)] = jnp.where(here, spread[t, pl.ds(i * 16, 16), :], fourth[i, :, tile(t)])
        sends[i].start()
    for send in sends:
        send.wait()


def deep_levels(n):
    fixed = lambda c, a, b: a if c else b
    level = lambda rows: lift(rows, (0.0, 0.0), (0.0, 0.0), True, True, fixed)
    cells = level(level(list(np.eye(n)))[0])[0]
    smooth, detail = level(cells)
    return cells, np.stack(interleave(smooth, detail)), np.stack(interleave(*level(smooth)))


def weights_y(devices):
    cells, _, four = deep_levels(16 * devices)
    w3 = np.zeros((devices, 48, 4, 16), np.float64)
    w4 = np.zeros((devices, devices, 2, 2, 2, 16), np.float64)
    for a in range(devices):
        mine = slice(16 * a, 16 * a + 16)
        for row, side, b in ((0, 0, -1), (8, 1, 1), (16, 0, 0), (24, 0, 1), (32, 1, 0), (40, 1, -1)):
            if 0 <= a + b < devices:
                pair = edges(cells[4 * (a + b) : 4 * (a + b) + 4])[side]
                for c in range(2):
                    for z in range(4):
                        w3[a, row + 4 * c + z, z] = pair[c][mine]
        for z in range(2):
            w4[a, :, :, z, z] = four[:, mine].reshape(devices, 2, 16)
    return (
        split_left(w3.reshape(devices, 48, 64).astype(np.float32)),
        split_left(w4.reshape(devices, 4 * devices, 32).astype(np.float32)),
    )


def weights_z(devices):
    _, three, four = deep_levels(16 * devices)
    w3 = np.zeros((devices, devices, 4, 4, 4), np.float64)
    w4 = np.zeros((devices, 2, 2, devices, 8, 2, 2), np.float64)
    for a in range(devices):
        for f in range(8):
            for zz in range(4):
                if f < 4:
                    z = 16 * a + zz + 4 * (f // 2) + 8 * (f % 2)
                    w3[a, :, :, f, zz] = three[:, z].reshape(devices, 4)
                if zz < 2:
                    z = 16 * a + zz + 2 * (f // 4) + 4 * (f // 2 % 2) + 8 * (f % 2)
                    for o in range(2):
                        w4[a, :, o, :, f, o, zz] = four[:, z].reshape(devices, 2).T
    return (
        split_left(w3.reshape(devices, 4 * devices, 16).astype(np.float32)),
        split_left(w4.reshape(devices, 4 * devices, 32).astype(np.float32)),
    )


def swap(values, axis, start):
    devices = lax.axis_size(axis)
    pairs = []
    for i in range(start, devices - 1, 2):
        pairs += [(i, i + 1), (i + 1, i)]
    return lax.ppermute(values, axis, pairs)


def f32(*shape):
    return jax.ShapeDtypeStruct(shape, jnp.float32)


def bf16(*shape):
    return jax.ShapeDtypeStruct(shape, jnp.bfloat16)


def call(body, out, scratch=(), cost=4 << 20, **more):
    return pl.pallas_call(
        body,
        out_shape=out,
        scratch_shapes=list(scratch),
        cost_estimate=pl.CostEstimate(flops=cost * 10, bytes_accessed=4 << 20, transcendentals=0),
        compiler_params=pltpu.CompilerParams(vmem_limit_bytes=24 * 1024 * 1024),
        **more,
    )


def per_device(density):
    planes, rows, cells = density.shape
    ny, nz = lax.axis_size("gy"), lax.axis_size("gz")
    vmem = lambda *shape: pltpu.VMEM(shape, jnp.float32)
    sems = lambda count: pltpu.SemaphoreType.DMA((count,))
    far, here = pl.BlockSpec(memory_space=pltpu.HBM), pl.BlockSpec(memory_space=pltpu.VMEM)
    stay = lambda v: pltpu.with_memory_space_constraint(jnp.asarray(v), pltpu.HBM)
    tiled = f32(TILES, planes * rows // 2, LANES)
    payload = f32(6, 8, cells)
    pay = (ny, 8, cells * 3 // 2)
    smooth, detail, pay_e, pay_o, own, pay, z3, z4 = call(
        along_x,
        [tiled, tiled, payload, payload, f32(16, cells), f32(*pay), bf16(4 * nz, 6 * 16), bf16(4 * nz, 6 * 32)],
        [
            vmem(planes * rows, cells),
            vmem(64, cells),
            vmem(32, cells),
            pltpu.VMEM((48, 6 * 64), jnp.bfloat16),
            pltpu.VMEM((4 * ny, 6 * 32), jnp.bfloat16),
            vmem(*pay),
            sems(8),
            sems(6),
        ],
        in_specs=[far] * 5,
        out_specs=[here] * 5 + [far, here, here],
    )(*[stay(w) for w in weights_y(ny) + weights_z(nz)], stay(density.reshape(planes * rows, cells)))
    got_e, got_o = swap(pay_e, "gy", 0), swap(pay_o, "gy", 1)
    got = lax.all_to_all(pay, "gy", 0, 0, tiled=True)

    one_s, one_d, two, pay_e, pay_o, third = call(
        along_y,
        [tiled, tiled, f32(TILES, planes * rows // 4, LANES), payload, payload, f32(16, cells)],
        [vmem(32, cells)],
        cost=400 << 20,
        input_output_aliases={0: 0, 1: 1},
    )(smooth, detail, got_e, got_o)
    got_e, got_o = swap(pay_e, "gz", 0), swap(pay_o, "gz", 1)
    pay = (nz, 4, cells + LANES)
    pay = call(
        thin_z,
        f32(*pay),
        [vmem(*pay), vmem(16, cells), vmem(4, cells), vmem(16, cells), vmem(32, cells), sems(2)],
        cost=40 << 20,
        out_specs=far,
    )(z3, z4, third, own, got)
    got = lax.all_to_all(pay, "gz", 0, 0, tiled=True)

    base, fourth = call(
        along_z,
        [f32(planes, rows, cells), f32(planes // 4, rows, cells)],
        [vmem(planes, rows, cells), vmem(32, cells), vmem(TILES, 128, LANES), sems(planes)],
        cost=400 << 20,
        out_specs=[far, here],
    )(one_s, one_d, two, got_e, got_o)
    return call(
        join,
        f32(planes, rows, cells),
        [vmem(planes // 4, rows, cells), vmem(TILES, 64, LANES), sems(4)],
        in_specs=[here, here, far],
        out_specs=far,
        input_output_aliases={2: 0},
    )(got, fourth, stay(base))


def solution(mesh):
    return jax.shard_map(
        per_device, mesh=mesh, in_specs=(P("gz", "gy", None),), out_specs=P("gz", "gy", None), check_vma=False
    )
```

```python
import functools

import jax
import jax.numpy as jnp
import ml_dtypes
import numpy as np
from jax import lax
from jax.experimental import pallas as pl
from jax.experimental.pallas import tpu as pltpu
from jax.sharding import PartitionSpec as P

A1 = -1.586134342059924
B1 = -0.052980118572961
A2 = 0.882911075530934
B2 = 0.443506852043971
GAIN = 1.230174104914001

WIDE = 1024
LANES = 128
TILES = WIDE // LANES


def lift(rows, left, right, first, last, choose):
    p, q = left
    s_next, r = right
    smooth, detail = rows[0::2], rows[1::2]
    m = len(smooth)
    s_next = choose(last, smooth[-1], s_next)
    d1 = [detail[i] + A1 * (smooth[i] + (smooth[i + 1] if i + 1 < m else s_next)) for i in range(m)]
    d1_before = choose(first, d1[0], p + A1 * smooth[0])
    s1 = [smooth[i] + B1 * ((d1[i - 1] if i else d1_before) + d1[i]) for i in range(m)]
    s1_after = choose(last, s1[-1], r + B1 * d1[-1])
    d2 = [d1[i] + A2 * (s1[i] + (s1[i + 1] if i + 1 < m else s1_after)) for i in range(m)]
    d2_before = choose(first, d2[0], d1_before + A2 * (q + B1 * d1_before + s1[0]))
    s2 = [s1[i] + B2 * ((d2[i - 1] if i else d2_before) + d2[i]) for i in range(m)]
    return [v * (1.0 / GAIN) for v in s2], [v * (GAIN / 2.0) for v in d2]


def lift_alone(rows):
    zero = jnp.zeros_like(rows[0])
    return lift(rows, (zero, zero), (zero, zero), False, False, lambda c, a, b: a if c else b)[0]


def edges(rows):
    s, d = rows[0::2], rows[1::2]
    to_right = (d[-1] + A1 * s[-1], s[-1] + B1 * (d[-2] + A1 * (s[-2] + s[-1])))
    to_left = (s[0], s[0] + B1 * (d[0] + A1 * (s[0] + s[1])))
    return to_right, to_left


def own_left(to_left):
    s, r = to_left
    c2 = (B2 * A2 * B1 * A1 / GAIN) * s
    c1 = ((B1 * A1 + B2 * A1 + 3 * B2 * A2 * B1 * A1) / GAIN) * s + (B2 * A2 / GAIN) * r
    return c1 + A1 * c2, (1 + B1 * A1) * c2


def own_right(to_right):
    p, q = to_right
    c0 = ((B1 + B2 + 3 * B2 * A2 * B1) / GAIN) * p + (B2 * A2 / GAIN) * q
    c1 = (B2 * A2 * B1 / GAIN) * p
    return c0, c0 + B1 * (c1 + A1 * c0)


def add_pairs(a, b):
    return a[0] + b[0], a[1] + b[1]


def mix(flag, a, b):
    return jnp.where(flag, a, b)


def interleave(smooth, detail):
    return [v for pair in zip(smooth, detail) for v in pair]


def filters():
    fixed = lambda c, a, b: a if c else b
    smooth, detail = lift(list(np.eye(32)), (0.0, 0.0), (0.0, 0.0), True, True, fixed)
    return [float(v) for v in smooth[8][16:21]], [float(v) for v in detail[8][17:21]]


def moved(tiles, step):
    if step == 0:
        return list(tiles)
    lane, count = lane_id(tiles[0].shape), len(tiles)
    r = [pltpu.roll(x, -step % LANES, 1) for x in tiles]
    if step > 0:
        return [jnp.where(lane < LANES - step, r[t], r[t + 1]) if t + 1 < count else r[t] for t in range(count)]
    return [jnp.where(lane >= -step, r[t], r[t - 1]) if t else r[t] for t in range(count)]


def lift_runs(v, stride):
    run = lane_id(v[0].shape) // stride
    ends = LANES // stride - 1
    at = {k: moved(v, k * stride) for k in range(-4, 5)}
    for k in range(1, 5):
        for j in range(k):
            at[-k][0] = jnp.where(run == j, at[k - 2 * j][0], at[-k][0])
    for k in range(1, 5):
        for j in range(k):
            at[k][-1] = jnp.where(run == ends - j, at[2 * j - k][-1], at[k][-1])
    smooth, detail = filters()
    weight = [jnp.where(run % 2 == 0, a, b) for a, b in zip(smooth, detail + [0.0])]
    out = [weight[0] * x for x in v]
    for k in range(1, 5):
        out = [x + weight[k] * (y + z) for x, y, z in zip(out, at[-k], at[k])]
    return out


def split_left(w):
    parts = []
    for _ in range(3):
        parts.append((w - sum(p.astype(np.float32) for p in parts)).astype(ml_dtypes.bfloat16))
    one, two, three = parts
    return np.concatenate([one, one, two, one, two, three], axis=-1)


def product(left, x):
    one = x.astype(jnp.bfloat16)
    rest = x - one.astype(jnp.float32)
    two = rest.astype(jnp.bfloat16)
    three = (rest - two.astype(jnp.float32)).astype(jnp.bfloat16)
    right = jnp.concatenate([one, two, one, three, two, one], axis=0)
    return jnp.dot(left, right, preferred_element_type=jnp.float32)


def lane_id(shape):
    return lax.broadcasted_iota(jnp.int32, shape, len(shape) - 1)


def in_even(shape):
    return lane_id(shape) % 2 == 0


def back(v):
    return pltpu.roll(v, LANES - 1, 1)


def on(v):
    return pltpu.roll(v, 1, 1)


def pack_right(p, q):
    return jnp.where(in_even(p.shape), back(q), p)


def unpack_right(v):
    return back(v), v


def pack_left(s, r):
    return jnp.where(in_even(s.shape), s, on(r))


def unpack_left(v):
    return on(v), v


def beyond_halves(left, right, to_right, to_left):
    even = in_even(to_right[0].shape)
    return (
        tuple(jnp.where(even, x, on(y)) for x, y in zip(left, to_right)),
        tuple(jnp.where(even, back(y), x) for x, y in zip(right, to_left)),
    )


def tile(t):
    return slice(t * LANES, (t + 1) * LANES)


def times(count, body, unroll=1):
    if unroll == count:
        for i in range(count):
            body(i)
        return

    def step(i, carry):
        body(i)
        return carry

    lax.fori_loop(0, count, step, 0, unroll=unroll)


def tile_lanes(t):
    return pl.ds(t * LANES if isinstance(t, int) else pl.multiple_of(t * LANES, LANES), LANES)


def lift_two(a, b, phase):
    lane = lane_id((a[0].shape[0], LANES))
    here = lane % (2 * phase) < phase
    count, reach = len(a), 2 * phase
    other = jnp.where(here, lane + phase, lane - phase)
    m = [jnp.take_along_axis(jnp.where(here, y, x), other, axis=1, mode="promise_in_bounds") for x, y in zip(a, b)]
    s = [jnp.where(here, x, y) for x, y in zip(a, m)]
    d = [jnp.where(here, y, x) for x, y in zip(b, m)]

    def ahead(x):
        r = [pltpu.roll(w, LANES - reach, 1) for w in x]
        return [jnp.where(lane < LANES - reach, r[t], r[t + 1] if t + 1 < count else x[t]) for t in range(count)]

    def behind(x):
        r = [pltpu.roll(w, reach, 1) for w in x]
        return [jnp.where(lane >= reach, r[t], r[t - 1] if t else x[t]) for t in range(count)]

    d = [x + A1 * (y + z) for x, y, z in zip(d, s, ahead(s))]
    s = [x + B1 * (y + z) for x, y, z in zip(s, d, behind(d))]
    d = [x + A2 * (y + z) for x, y, z in zip(d, s, ahead(s))]
    s = [(x + B2 * (y + z)) * (1.0 / GAIN) for x, y, z in zip(s, d, behind(d))]
    return s, [x * (GAIN / 2.0) for x in d]


def separate(s, d, phase):
    lane = lane_id(s[0].shape)
    here = lane % (2 * phase) < phase
    other = jnp.where(here, lane + phase, lane - phase)
    m = [jnp.take_along_axis(jnp.where(here, y, x), other, axis=1, mode="promise_in_bounds") for x, y in zip(s, d)]
    return [jnp.where(here, x, y) for x, y in zip(s, m)], [jnp.where(here, y, x) for x, y in zip(d, m)]


def tiles_of(ref, at):
    v = ref[at, :]
    return [v[:, tile(t)] for t in range(TILES)]


def put_tiles(ref, at, parts):
    for t, v in enumerate(parts):
        ref[at, tile(t)] = v


def along_x(
    y3, y4, z3, z4, density, smooth, detail, pay_e, pay_o, own, result, next3, next4, x, e2, e3, w3, w4, pay, load_sem, sem
):
    me, mz = lax.axis_index("gy"), lax.axis_index("gz")

    def load(k):
        at = pl.ds(pl.multiple_of(k * 64, 64), 64)
        return pltpu.make_async_copy(density.at[at], x.at[at], load_sem.at[k])

    for k in range(2):
        load(k).start()
        load(k + 2).start()
    hints = [
        pltpu.make_async_copy(y3.at[me], w3, sem.at[0]),
        pltpu.make_async_copy(y4.at[me], w4, sem.at[1]),
        pltpu.make_async_copy(z3.at[mz], next3, sem.at[2]),
        pltpu.make_async_copy(z4.at[mz], next4, sem.at[3]),
    ]
    for hint in hints:
        hint.start()

    def plane(i):
        z, y = i // 2, i % 2
        at = pl.multiple_of(z * 16 + y * 8, 8)
        far = pl.multiple_of(z * 16 + y * 8 + 128, 8)
        s, d = lift_two(tiles_of(x, pl.ds(at, 8)), tiles_of(x, pl.ds(far, 8)), 1)
        for t in range(TILES):
            smooth[t, pl.ds(at, 8), :] = s[t]
            detail[t, pl.ds(at, 8), :] = d[t]

    def group(k):
        load(k).wait()
        load(k + 2).wait()
        for i in range(8):
            plane(8 * k + i)

    times(2, group)
    for hint in hints:
        hint.wait()

    def second(i):
        at = pl.multiple_of(i * 8, 8)
        near, far = [[smooth[t, pl.ds(at + k, 8), :] for t in range(TILES)] for k in (0, 64)]
        s, _ = lift_two(near, far, 2)
        put_tiles(e2, pl.ds(at, 8), s)

    times(8, second, 8)

    def third(i):
        at = pl.multiple_of(i * 8, 8)
        s, _ = lift_two(tiles_of(e2, pl.ds(at, 8)), tiles_of(e2, pl.ds(at + 32, 8)), 4)
        put_tiles(e3, pl.ds(at, 8), s)

    times(4, third, 4)
    three = product(w3[...], e2[...])
    four = product(w4[...], e3[...])
    own[...] = three[0:16]
    for to in range(pay.shape[0]):
        right = mix(to == me + 1, three[16:24], three[24:32])
        left = mix(to == me - 1, three[32:40], three[40:48])
        pay[to, :, 0:WIDE] = mix(to > me, right, left)
    parts = [pl.ds(0, WIDE), pl.ds(WIDE, WIDE // 2)]
    sends = [pltpu.make_async_copy(pay.at[:, :, p], result.at[:, :, p], sem.at[4 + k]) for k, p in enumerate(parts)]
    sends[0].start()
    for to in range(pay.shape[0]):
        pay[to, 0:4, WIDE:] = four[to * 4 : to * 4 + 4, : WIDE // 2]
        pay[to, 4:8, WIDE:] = four[to * 4 : to * 4 + 4, WIDE // 2 :]
    sends[1].start()
    flip = me % 2 == 1

    def column(t):
        lanes = tile_lanes(t)
        rows = [smooth[t, pl.ds(y, 8, stride=16), :] for y in range(16)]
        parts = [edges(rows), edges(lift_alone(rows))]
        parts.append(edges([detail[t, pl.ds(y, 8, stride=16), :] for y in range(16)]))
        for c in range(6):
            right, left = [parts[c // 2][side][c % 2] for side in range(2)]
            pay_e[c, :, lanes] = mix(flip, left, right)
            pay_o[c, :, lanes] = mix(flip, right, left)

    times(TILES, column, 4)
    for send in sends:
        send.wait()


def along_y(smooth, detail, got_e, got_o, one_s, one_d, two, pay_e, pay_o, cells, thick):
    me = lax.axis_index("gy")
    first, last, flip = me == 0, me == lax.axis_size("gy") - 1, me % 2 == 1

    def column(t):
        lanes = tile_lanes(t)
        e = [got_e[c, :, lanes] for c in range(6)]
        o = [got_o[c, :, lanes] for c in range(6)]
        left = [mix(flip, e[c], o[c]) for c in range(6)]
        right = [mix(flip, o[c], e[c]) for c in range(6)]
        for k, (source, to) in enumerate(((detail, one_d), (smooth, one_s))):
            rows = [source[t, pl.ds(y, 8, stride=16), :] for y in range(16)]
            at = slice(0, 2) if k else slice(4, 6)
            low, high = lift(rows, left[at], right[at], first, last, mix)
            for y, v in enumerate(interleave(low, high)):
                to[t, pl.ds(y, 8, stride=16), :] = v
        to_right, to_left = edges(rows)
        left2, right2 = add_pairs(left[2:4], own_left(to_left)), add_pairs(right[2:4], own_right(to_right))
        low, high = lift(low, left2, right2, first, last, mix)
        for y, v in enumerate(interleave(low, high)):
            two[t, pl.ds(y, 8, stride=8), :] = v
        for r, v in enumerate(low):
            thick[pl.ds(4 * r, 4), lanes] = v[0:4]
            thick[pl.ds(16 + 4 * r, 4), lanes] = v[4:8]

    times(TILES, column, TILES)
    flip = lax.axis_index("gz") % 2 == 1

    def stack(t):
        lanes = tile_lanes(t)
        going_right, going_left = [], []

        def add(rows):
            to_right, to_left = edges(rows)
            going_right.append(pack_right(*to_right))
            going_left.append(pack_left(*to_left))
            return to_right, to_left

        for source in (one_s, one_d):
            for half in range(2):
                add([source[t, pl.ds(z * 16 + half * 8, 8), :] for z in range(8)])
        rows = [two[t, pl.ds(z * 8, 8), :] for z in range(8)]
        nothing = jnp.zeros_like(rows[0])
        left, right = beyond_halves((nothing, nothing), (nothing, nothing), *add(rows))
        add(lift(rows, left, right, False, False, lambda c, a, b: b)[0])
        for c in range(6):
            pay_e[c, :, lanes] = mix(flip, going_left[c], going_right[c])
            pay_o[c, :, lanes] = mix(flip, going_right[c], going_left[c])

    times(TILES, stack, TILES)
    for i in range(2):
        s, _ = lift_two(tiles_of(thick, pl.ds(8 * i, 8)), tiles_of(thick, pl.ds(16 + 8 * i, 8)), 2)
        put_tiles(cells, pl.ds(8 * i, 8), s)


def thin_z(w3, w4, cells, own, got, result, pay, beyond, held4, turned3, turned4, sem):
    me, count = lax.axis_index("gy"), got.shape[0]
    first, last = me == 0, me == count - 1
    near = lambda k: got[jnp.clip(me + k, 0, count - 1), :, 0:WIDE]
    beyond[0:8] = own[0:8] + (mix(me >= 1, near(-1), 0.0) + mix(me >= 2, near(-2), 0.0))
    beyond[8:16] = own[8:16] + (mix(me < count - 1, near(1), 0.0) + mix(me < count - 2, near(2), 0.0))
    four = got[0, :, WIDE:]
    for k in range(1, count):
        four = four + got[k, :, WIDE:]
    held4[:, 0 : WIDE // 2] = four[0:4]
    held4[:, WIDE // 2 :] = four[4:8]
    lane = lane_id((4, LANES))
    for t in range(TILES):
        at = lambda r: pl.ds(4 * r, 4)
        p, q, s, r = [beyond[at(c), tile(t)] for c in range(4)]
        rows = [cells[at(c), tile(t)] for c in range(4)]
        rows = interleave(*lift(rows, (p, q), (s, r), first, last, mix))
        for f in range(4):
            v = None
            for r in range(4):
                moved = pltpu.roll(rows[r], (r - f) % LANES, 1) if r != f else rows[r]
                v = jnp.where(lane % 4 == r, moved, v) if r else moved
            turned3[at(f), tile(t)] = v
        v = held4[:, tile(t)]
        for f in range(8):
            turned4[at(f), tile(t)] = pltpu.roll(v, LANES - f, 1) if f else v
    count = pay.shape[0]
    parts = [pl.ds(0, WIDE), pl.ds(WIDE, LANES)]
    sends = [pltpu.make_async_copy(pay.at[:, :, p], result.at[:, :, p], sem.at[k]) for k, p in enumerate(parts)]
    three = product(w3[...], turned3[...])
    four = product(w4[...], turned4[...])
    for to in range(count):
        pay[to, :, 0:WIDE] = three[to * 4 : to * 4 + 4]
    sends[0].start()
    lane = lane_id((count, LANES))
    for t in range(TILES // 2):
        v = four[0:count, tile(t)]
        for k in range(1, 8):
            w = four[k % 4 * count : (k % 4 + 1) * count, tile(t + k // 4 * (TILES // 2))]
            v = jnp.where(lane % 8 == k, pltpu.roll(w, k, 1), v)
        pay[:, t, WIDE:] = v
    sends[1].start()
    for send in sends:
        send.wait()


def along_z(one_s, one_d, two, got_e, got_o, result, fourth, out, fine, spread, sem):
    me = lax.axis_index("gz")
    flip, side = me % 2 == 1, lane_id((8, LANES)) % 2
    first = side == jnp.where(me == 0, 0, 2)
    last = side == jnp.where(me == lax.axis_size("gz") - 1, 1, 2)

    def stack(t):
        lanes = tile_lanes(t)
        e = [got_e[c, :, lanes] for c in range(6)]
        o = [got_o[c, :, lanes] for c in range(6)]
        left = [unpack_right(mix(flip, e[c], o[c])) for c in range(6)]
        right = [unpack_left(mix(flip, o[c], e[c])) for c in range(6)]
        for half in range(2):
            lifted = []
            for k, source in enumerate((one_s, one_d)):
                rows = [source[t, pl.ds(z * 16 + half * 8, 8), :] for z in range(8)]
                ends = beyond_halves(left[2 * k + half], right[2 * k + half], *edges(rows))
                lifted.append(interleave(*lift(rows, *ends, first, last, mix)))
            near, far = separate(*lifted, 1)
            for z in range(8):
                out[z, pl.ds(half * 8, 8), lanes] = near[z]
                out[z + 8, pl.ds(half * 8, 8), lanes] = far[z]
        rows = [two[t, pl.ds(z * 8, 8), :] for z in range(8)]
        to_right, to_left = edges(rows)
        rows, _ = lift(rows, *beyond_halves(left[4], right[4], to_right, to_left), first, last, mix)
        left2, right2 = add_pairs(left[5], own_left(to_left)), add_pairs(right[5], own_right(to_right))
        ends = beyond_halves(left2, right2, *edges(rows))
        for z, v in enumerate(interleave(*lift(rows, *ends, first, last, mix))):
            fine[pl.ds(z * 8, 8), lanes] = v

    times(TILES, stack, 2)
    sends = {z: pltpu.make_async_copy(out.at[z], result.at[z], sem.at[z]) for z in range(16) if z % 4}
    for z in range(1, 16, 2):
        sends[z].start()
    row = lax.broadcasted_iota(jnp.int32, (16, LANES), 0)
    here = (row % 2 == 0) & in_even((16, LANES))
    for i in (1, 3, 0, 2):
        v = lift_runs(tiles_of(fine, pl.ds(i * 8, 8)), 2)
        for z in (i, i + 4):
            for t in range(TILES):
                spread[t, pl.ds(z * 16, 8, stride=2), :] = v[t] if z == i else back(v[t])
                w = jnp.where(here, spread[t, pl.ds(z * 16, 16), :], out[2 * z, :, tile(t)])
                if z % 2:
                    out[2 * z, :, tile(t)] = w
                else:
                    fourth[z // 2, :, tile(t)] = w
            if z % 2:
                sends[2 * z].start()
    for send in sends.values():
        send.wait()


def join(got, fourth, base, result, planes, spread, sem):
    total = got[0]
    for k in range(1, got.shape[0]):
        total = total + got[k]
    three = lift_runs([total[:, tile(t)] for t in range(TILES)], 4)
    four = [total[t : t + 1, WIDE:] for t in range(TILES // 2)]
    four = lift_runs(four + [pltpu.roll(x, LANES - 4, 1) for x in four], 8)
    lane = lane_id((4, LANES))
    row = lax.broadcasted_iota(jnp.int32, (4, LANES), 0)
    for t in range(TILES):
        for r in range(4):
            v = pltpu.roll(three[t], LANES - r, 1) if r else three[t]
            for k in range(r // 2, 4, 2) if r % 2 == 0 else ():
                w = pltpu.roll(four[t], LANES - k, 1) if k else four[t]
                v = jnp.where((lane % 8 == 0) & (row == 2 * (k // 2)), jnp.broadcast_to(w, v.shape), v)
            spread[t, pl.ds(4 * r, 4, stride=16), :] = v
    row = lax.broadcasted_iota(jnp.int32, (16, LANES), 0)
    here = (row % 4 == 0) & (lane_id((16, LANES)) % 4 == 0)
    sends = [pltpu.make_async_copy(planes.at[i], result.at[4 * i], sem.at[i]) for i in range(4)]
    for i in range(4):
        for t in range(TILES):
            planes[i, :, tile(t)] = jnp.where(here, spread[t, pl.ds(i * 16, 16), :], fourth[i, :, tile(t)])
        sends[i].start()
    for send in sends:
        send.wait()


def deep_levels(n):
    fixed = lambda c, a, b: a if c else b
    level = lambda rows: lift(rows, (0.0, 0.0), (0.0, 0.0), True, True, fixed)
    cells = level(level(list(np.eye(n)))[0])[0]
    smooth, detail = level(cells)
    return cells, np.stack(interleave(smooth, detail)), np.stack(interleave(*level(smooth)))


def weights_y(devices):
    cells, _, four = deep_levels(16 * devices)
    w3 = np.zeros((devices, 48, 4, 16), np.float64)
    w4 = np.zeros((devices, devices, 2, 2, 2, 16), np.float64)
    for a in range(devices):
        mine = slice(16 * a, 16 * a + 16)
        for row, side, b in ((0, 0, -1), (8, 1, 1), (16, 0, 0), (24, 0, 1), (32, 1, 0), (40, 1, -1)):
            if 0 <= a + b < devices:
                pair = edges(cells[4 * (a + b) : 4 * (a + b) + 4])[side]
                for c in range(2):
                    for z in range(4):
                        w3[a, row + 4 * c + z, z] = pair[c][mine]
        for z in range(2):
            w4[a, :, :, z, z] = four[:, mine].reshape(devices, 2, 16)
    return (
        split_left(w3.reshape(devices, 48, 64).astype(np.float32)),
        split_left(w4.reshape(devices, 4 * devices, 32).astype(np.float32)),
    )


def weights_z(devices):
    _, three, four = deep_levels(16 * devices)
    w3 = np.zeros((devices, devices, 4, 4, 4), np.float64)
    w4 = np.zeros((devices, 2, 2, devices, 8, 2, 2), np.float64)
    for a in range(devices):
        for f in range(8):
            for zz in range(4):
                if f < 4:
                    z = 16 * a + zz + 4 * (f // 2) + 8 * (f % 2)
                    w3[a, :, :, f, zz] = three[:, z].reshape(devices, 4)
                if zz < 2:
                    z = 16 * a + zz + 2 * (f // 4) + 4 * (f // 2 % 2) + 8 * (f % 2)
                    for o in range(2):
                        w4[a, :, o, :, f, o, zz] = four[:, z].reshape(devices, 2).T
    return (
        split_left(w3.reshape(devices, 4 * devices, 16).astype(np.float32)),
        split_left(w4.reshape(devices, 4 * devices, 32).astype(np.float32)),
    )


def swap(values, axis, start):
    devices = lax.axis_size(axis)
    pairs = []
    for i in range(start, devices - 1, 2):
        pairs += [(i, i + 1), (i + 1, i)]
    return lax.ppermute(values, axis, pairs)


def f32(*shape):
    return jax.ShapeDtypeStruct(shape, jnp.float32)


def bf16(*shape):
    return jax.ShapeDtypeStruct(shape, jnp.bfloat16)


def call(body, out, scratch=(), cost=4 << 20, **more):
    return pl.pallas_call(
        body,
        out_shape=out,
        scratch_shapes=list(scratch),
        cost_estimate=pl.CostEstimate(flops=cost * 10, bytes_accessed=4 << 20, transcendentals=0),
        compiler_params=pltpu.CompilerParams(vmem_limit_bytes=24 * 1024 * 1024),
        **more,
    )


def per_device(density):
    planes, rows, cells = density.shape
    ny, nz = lax.axis_size("gy"), lax.axis_size("gz")
    vmem = lambda *shape: pltpu.VMEM(shape, jnp.float32)
    sems = lambda count: pltpu.SemaphoreType.DMA((count,))
    far, here = pl.BlockSpec(memory_space=pltpu.HBM), pl.BlockSpec(memory_space=pltpu.VMEM)
    stay = lambda v: pltpu.with_memory_space_constraint(jnp.asarray(v), pltpu.HBM)
    tiled = f32(TILES, planes * rows // 2, LANES)
    payload = f32(6, 8, cells)
    pay = (ny, 8, cells * 3 // 2)
    smooth, detail, pay_e, pay_o, own, pay, z3, z4 = call(
        along_x,
        [tiled, tiled, payload, payload, f32(16, cells), f32(*pay), bf16(4 * nz, 6 * 16), bf16(4 * nz, 6 * 32)],
        [
            vmem(planes * rows, cells),
            vmem(64, cells),
            vmem(32, cells),
            pltpu.VMEM((48, 6 * 64), jnp.bfloat16),
            pltpu.VMEM((4 * ny, 6 * 32), jnp.bfloat16),
            vmem(*pay),
            sems(4),
            sems(6),
        ],
        in_specs=[far] * 5,
        out_specs=[here] * 5 + [far, here, here],
    )(*[stay(w) for w in weights_y(ny) + weights_z(nz)], stay(density.reshape(planes * rows, cells)))
    got_e, got_o = swap(pay_e, "gy", 0), swap(pay_o, "gy", 1)
    got = lax.all_to_all(pay, "gy", 0, 0, tiled=True)

    one_s, one_d, two, pay_e, pay_o, third = call(
        along_y,
        [tiled, tiled, f32(TILES, planes * rows // 4, LANES), payload, payload, f32(16, cells)],
        [vmem(32, cells)],
        cost=400 << 20,
        input_output_aliases={0: 0, 1: 1},
    )(smooth, detail, got_e, got_o)
    got_e, got_o = swap(pay_e, "gz", 0), swap(pay_o, "gz", 1)
    pay = (nz, 4, cells + LANES)
    pay = call(
        thin_z,
        f32(*pay),
        [vmem(*pay), vmem(16, cells), vmem(4, cells), vmem(16, cells), vmem(32, cells), sems(2)],
        cost=40 << 20,
        out_specs=far,
    )(z3, z4, third, own, got)
    got = lax.all_to_all(pay, "gz", 0, 0, tiled=True)

    base, fourth = call(
        along_z,
        [f32(planes, rows, cells), f32(planes // 4, rows, cells)],
        [vmem(planes, rows, cells), vmem(32, cells), vmem(TILES, 128, LANES), sems(planes)],
        cost=400 << 20,
        out_specs=[far, here],
    )(one_s, one_d, two, got_e, got_o)
    return call(
        join,
        f32(planes, rows, cells),
        [vmem(planes // 4, rows, cells), vmem(TILES, 64, LANES), sems(4)],
        in_specs=[here, here, far],
        out_specs=far,
        input_output_aliases={2: 0},
    )(got, fourth, stay(base))


def solution(mesh):
    return jax.shard_map(
        per_device, mesh=mesh, in_specs=(P("gz", "gy", None),), out_specs=P("gz", "gy", None), check_vma=False
    )
```

```python
import functools

import jax
import jax.numpy as jnp
import ml_dtypes
import numpy as np
from jax import lax
from jax.experimental import pallas as pl
from jax.experimental.pallas import tpu as pltpu
from jax.sharding import PartitionSpec as P

A1 = -1.586134342059924
B1 = -0.052980118572961
A2 = 0.882911075530934
B2 = 0.443506852043971
GAIN = 1.230174104914001

WIDE = 1024
LANES = 128
TILES = WIDE // LANES


def lift(rows, left, right, first, last, choose):
    p, q = left
    s_next, r = right
    smooth, detail = rows[0::2], rows[1::2]
    m = len(smooth)
    s_next = choose(last, smooth[-1], s_next)
    d1 = [detail[i] + A1 * (smooth[i] + (smooth[i + 1] if i + 1 < m else s_next)) for i in range(m)]
    d1_before = choose(first, d1[0], p + A1 * smooth[0])
    s1 = [smooth[i] + B1 * ((d1[i - 1] if i else d1_before) + d1[i]) for i in range(m)]
    s1_after = choose(last, s1[-1], r + B1 * d1[-1])
    d2 = [d1[i] + A2 * (s1[i] + (s1[i + 1] if i + 1 < m else s1_after)) for i in range(m)]
    d2_before = choose(first, d2[0], d1_before + A2 * (q + B1 * d1_before + s1[0]))
    s2 = [s1[i] + B2 * ((d2[i - 1] if i else d2_before) + d2[i]) for i in range(m)]
    return [v * (1.0 / GAIN) for v in s2], [v * (GAIN / 2.0) for v in d2]


def lift_alone(rows):
    zero = jnp.zeros_like(rows[0])
    return lift(rows, (zero, zero), (zero, zero), False, False, lambda c, a, b: a if c else b)[0]


def edges(rows):
    s, d = rows[0::2], rows[1::2]
    to_right = (d[-1] + A1 * s[-1], s[-1] + B1 * (d[-2] + A1 * (s[-2] + s[-1])))
    to_left = (s[0], s[0] + B1 * (d[0] + A1 * (s[0] + s[1])))
    return to_right, to_left


def own_left(to_left):
    s, r = to_left
    c2 = (B2 * A2 * B1 * A1 / GAIN) * s
    c1 = ((B1 * A1 + B2 * A1 + 3 * B2 * A2 * B1 * A1) / GAIN) * s + (B2 * A2 / GAIN) * r
    return c1 + A1 * c2, (1 + B1 * A1) * c2


def own_right(to_right):
    p, q = to_right
    c0 = ((B1 + B2 + 3 * B2 * A2 * B1) / GAIN) * p + (B2 * A2 / GAIN) * q
    c1 = (B2 * A2 * B1 / GAIN) * p
    return c0, c0 + B1 * (c1 + A1 * c0)


def add_pairs(a, b):
    return a[0] + b[0], a[1] + b[1]


def mix(flag, a, b):
    return jnp.where(flag, a, b)


def interleave(smooth, detail):
    return [v for pair in zip(smooth, detail) for v in pair]


def filters():
    fixed = lambda c, a, b: a if c else b
    smooth, detail = lift(list(np.eye(32)), (0.0, 0.0), (0.0, 0.0), True, True, fixed)
    return [float(v) for v in smooth[8][16:21]], [float(v) for v in detail[8][17:21]]


def moved(tiles, step):
    if step == 0:
        return list(tiles)
    lane, count = lane_id(tiles[0].shape), len(tiles)
    r = [pltpu.roll(x, -step % LANES, 1) for x in tiles]
    if step > 0:
        return [jnp.where(lane < LANES - step, r[t], r[t + 1]) if t + 1 < count else r[t] for t in range(count)]
    return [jnp.where(lane >= -step, r[t], r[t - 1]) if t else r[t] for t in range(count)]


def lift_runs(v, stride):
    run = lane_id(v[0].shape) // stride
    ends = LANES // stride - 1
    at = {k: moved(v, k * stride) for k in range(-4, 5)}
    for k in range(1, 5):
        for j in range(k):
            at[-k][0] = jnp.where(run == j, at[k - 2 * j][0], at[-k][0])
    for k in range(1, 5):
        for j in range(k):
            at[k][-1] = jnp.where(run == ends - j, at[2 * j - k][-1], at[k][-1])
    smooth, detail = filters()
    weight = [jnp.where(run % 2 == 0, a, b) for a, b in zip(smooth, detail + [0.0])]
    out = [weight[0] * x for x in v]
    for k in range(1, 5):
        out = [x + weight[k] * (y + z) for x, y, z in zip(out, at[-k], at[k])]
    return out


def split_left(w):
    parts = []
    for _ in range(3):
        parts.append((w - sum(p.astype(np.float32) for p in parts)).astype(ml_dtypes.bfloat16))
    one, two, three = parts
    return np.concatenate([one, one, two, one, two, three], axis=-1)


def product(left, x):
    one = x.astype(jnp.bfloat16)
    rest = x - one.astype(jnp.float32)
    two = rest.astype(jnp.bfloat16)
    three = (rest - two.astype(jnp.float32)).astype(jnp.bfloat16)
    right = jnp.concatenate([one, two, one, three, two, one], axis=0)
    return jnp.dot(left, right, preferred_element_type=jnp.float32)


def lane_id(shape):
    return lax.broadcasted_iota(jnp.int32, shape, len(shape) - 1)


def in_even(shape):
    return lane_id(shape) % 2 == 0


def back(v):
    return pltpu.roll(v, LANES - 1, 1)


def on(v):
    return pltpu.roll(v, 1, 1)


def pack_right(p, q):
    return jnp.where(in_even(p.shape), back(q), p)


def unpack_right(v):
    return back(v), v


def pack_left(s, r):
    return jnp.where(in_even(s.shape), s, on(r))


def unpack_left(v):
    return on(v), v


def beyond_halves(left, right, to_right, to_left):
    even = in_even(to_right[0].shape)
    return (
        tuple(jnp.where(even, x, on(y)) for x, y in zip(left, to_right)),
        tuple(jnp.where(even, back(y), x) for x, y in zip(right, to_left)),
    )


def tile(t):
    return slice(t * LANES, (t + 1) * LANES)


def times(count, body, unroll=1):
    if unroll == count:
        for i in range(count):
            body(i)
        return

    def step(i, carry):
        body(i)
        return carry

    lax.fori_loop(0, count, step, 0, unroll=unroll)


def tile_lanes(t):
    return pl.ds(t * LANES if isinstance(t, int) else pl.multiple_of(t * LANES, LANES), LANES)


def lift_two(a, b, phase):
    lane = lane_id((a[0].shape[0], LANES))
    here = lane % (2 * phase) < phase
    count, reach = len(a), 2 * phase
    other = jnp.where(here, lane + phase, lane - phase)
    m = [jnp.take_along_axis(jnp.where(here, y, x), other, axis=1, mode="promise_in_bounds") for x, y in zip(a, b)]
    s = [jnp.where(here, x, y) for x, y in zip(a, m)]
    d = [jnp.where(here, y, x) for x, y in zip(b, m)]

    def ahead(x):
        r = [pltpu.roll(w, LANES - reach, 1) for w in x]
        return [jnp.where(lane < LANES - reach, r[t], r[t + 1] if t + 1 < count else x[t]) for t in range(count)]

    def behind(x):
        r = [pltpu.roll(w, reach, 1) for w in x]
        return [jnp.where(lane >= reach, r[t], r[t - 1] if t else x[t]) for t in range(count)]

    d = [x + A1 * (y + z) for x, y, z in zip(d, s, ahead(s))]
    s = [x + B1 * (y + z) for x, y, z in zip(s, d, behind(d))]
    d = [x + A2 * (y + z) for x, y, z in zip(d, s, ahead(s))]
    s = [(x + B2 * (y + z)) * (1.0 / GAIN) for x, y, z in zip(s, d, behind(d))]
    return s, [x * (GAIN / 2.0) for x in d]


def separate(s, d, phase):
    lane = lane_id(s[0].shape)
    here = lane % (2 * phase) < phase
    other = jnp.where(here, lane + phase, lane - phase)
    m = [jnp.take_along_axis(jnp.where(here, y, x), other, axis=1, mode="promise_in_bounds") for x, y in zip(s, d)]
    return [jnp.where(here, x, y) for x, y in zip(s, m)], [jnp.where(here, y, x) for x, y in zip(d, m)]


def tiles_of(ref, at):
    v = ref[at, :]
    return [v[:, tile(t)] for t in range(TILES)]


def put_tiles(ref, at, parts):
    for t, v in enumerate(parts):
        ref[at, tile(t)] = v


def along_x(
    y3, y4, z3, z4, density, smooth, detail, pay_e, pay_o, own, result, next3, next4, x, e2, e3, w3, w4, pay, load_sem, sem
):
    me, mz = lax.axis_index("gy"), lax.axis_index("gz")

    def load(k):
        at = pl.ds(pl.multiple_of(k * 32, 32), 32)
        return pltpu.make_async_copy(density.at[at], x.at[at], load_sem.at[k])

    for k in range(4):
        load(k).start()
        load(k + 4).start()
    hints = [
        pltpu.make_async_copy(y3.at[me], w3, sem.at[0]),
        pltpu.make_async_copy(y4.at[me], w4, sem.at[1]),
        pltpu.make_async_copy(z3.at[mz], next3, sem.at[2]),
        pltpu.make_async_copy(z4.at[mz], next4, sem.at[3]),
    ]
    for hint in hints:
        hint.start()

    def plane(i):
        z, y = i // 2, i % 2
        at = pl.multiple_of(z * 16 + y * 8, 8)
        far = pl.multiple_of(z * 16 + y * 8 + 128, 8)
        s, d = lift_two(tiles_of(x, pl.ds(at, 8)), tiles_of(x, pl.ds(far, 8)), 1)
        for t in range(TILES):
            smooth[t, pl.ds(at, 8), :] = s[t]
            detail[t, pl.ds(at, 8), :] = d[t]

    def group(k):
        for j in range(2):
            load(2 * k + j).wait()
            load(2 * k + j + 4).wait()
        for i in range(8):
            plane(8 * k + i)

    times(2, group)
    for hint in hints:
        hint.wait()

    def second(i):
        at = pl.multiple_of(i * 8, 8)
        near, far = [[smooth[t, pl.ds(at + k, 8), :] for t in range(TILES)] for k in (0, 64)]
        s, _ = lift_two(near, far, 2)
        put_tiles(e2, pl.ds(at, 8), s)

    times(8, second, 8)

    def third(i):
        at = pl.multiple_of(i * 8, 8)
        s, _ = lift_two(tiles_of(e2, pl.ds(at, 8)), tiles_of(e2, pl.ds(at + 32, 8)), 4)
        put_tiles(e3, pl.ds(at, 8), s)

    times(4, third, 4)
    three = product(w3[...], e2[...])
    four = product(w4[...], e3[...])
    own[...] = three[0:16]
    for to in range(pay.shape[0]):
        right = mix(to == me + 1, three[16:24], three[24:32])
        left = mix(to == me - 1, three[32:40], three[40:48])
        pay[to, :, 0:WIDE] = mix(to > me, right, left)
    parts = [pl.ds(0, WIDE), pl.ds(WIDE, WIDE // 2)]
    sends = [pltpu.make_async_copy(pay.at[:, :, p], result.at[:, :, p], sem.at[4 + k]) for k, p in enumerate(parts)]
    sends[0].start()
    for to in range(pay.shape[0]):
        pay[to, 0:4, WIDE:] = four[to * 4 : to * 4 + 4, : WIDE // 2]
        pay[to, 4:8, WIDE:] = four[to * 4 : to * 4 + 4, WIDE // 2 :]
    sends[1].start()
    flip = me % 2 == 1

    def column(t):
        lanes = tile_lanes(t)
        rows = [smooth[t, pl.ds(y, 8, stride=16), :] for y in range(16)]
        parts = [edges(rows), edges(lift_alone(rows))]
        parts.append(edges([detail[t, pl.ds(y, 8, stride=16), :] for y in range(16)]))
        for c in range(6):
            right, left = [parts[c // 2][side][c % 2] for side in range(2)]
            pay_e[c, :, lanes] = mix(flip, left, right)
            pay_o[c, :, lanes] = mix(flip, right, left)

    times(TILES, column, 4)
    for send in sends:
        send.wait()


def along_y(smooth, detail, got_e, got_o, one_s, one_d, two, pay_e, pay_o, cells, thick):
    me = lax.axis_index("gy")
    first, last, flip = me == 0, me == lax.axis_size("gy") - 1, me % 2 == 1

    def column(t):
        lanes = tile_lanes(t)
        e = [got_e[c, :, lanes] for c in range(6)]
        o = [got_o[c, :, lanes] for c in range(6)]
        left = [mix(flip, e[c], o[c]) for c in range(6)]
        right = [mix(flip, o[c], e[c]) for c in range(6)]
        for k, (source, to) in enumerate(((detail, one_d), (smooth, one_s))):
            rows = [source[t, pl.ds(y, 8, stride=16), :] for y in range(16)]
            at = slice(0, 2) if k else slice(4, 6)
            low, high = lift(rows, left[at], right[at], first, last, mix)
            for y, v in enumerate(interleave(low, high)):
                to[t, pl.ds(y, 8, stride=16), :] = v
        to_right, to_left = edges(rows)
        left2, right2 = add_pairs(left[2:4], own_left(to_left)), add_pairs(right[2:4], own_right(to_right))
        low, high = lift(low, left2, right2, first, last, mix)
        for y, v in enumerate(interleave(low, high)):
            two[t, pl.ds(y, 8, stride=8), :] = v
        for r, v in enumerate(low):
            thick[pl.ds(4 * r, 4), lanes] = v[0:4]
            thick[pl.ds(16 + 4 * r, 4), lanes] = v[4:8]

    times(TILES, column, TILES)
    flip = lax.axis_index("gz") % 2 == 1

    def stack(t):
        lanes = tile_lanes(t)
        going_right, going_left = [], []

        def add(rows):
            to_right, to_left = edges(rows)
            going_right.append(pack_right(*to_right))
            going_left.append(pack_left(*to_left))
            return to_right, to_left

        for source in (one_s, one_d):
            for half in range(2):
                add([source[t, pl.ds(z * 16 + half * 8, 8), :] for z in range(8)])
        rows = [two[t, pl.ds(z * 8, 8), :] for z in range(8)]
        nothing = jnp.zeros_like(rows[0])
        left, right = beyond_halves((nothing, nothing), (nothing, nothing), *add(rows))
        add(lift(rows, left, right, False, False, lambda c, a, b: b)[0])
        for c in range(6):
            pay_e[c, :, lanes] = mix(flip, going_left[c], going_right[c])
            pay_o[c, :, lanes] = mix(flip, going_right[c], going_left[c])

    times(TILES, stack, TILES)
    for i in range(2):
        s, _ = lift_two(tiles_of(thick, pl.ds(8 * i, 8)), tiles_of(thick, pl.ds(16 + 8 * i, 8)), 2)
        put_tiles(cells, pl.ds(8 * i, 8), s)


def thin_z(w3, w4, cells, own, got, result, pay, beyond, held4, turned3, turned4, sem):
    me, count = lax.axis_index("gy"), got.shape[0]
    first, last = me == 0, me == count - 1
    near = lambda k: got[jnp.clip(me + k, 0, count - 1), :, 0:WIDE]
    beyond[0:8] = own[0:8] + (mix(me >= 1, near(-1), 0.0) + mix(me >= 2, near(-2), 0.0))
    beyond[8:16] = own[8:16] + (mix(me < count - 1, near(1), 0.0) + mix(me < count - 2, near(2), 0.0))
    four = got[0, :, WIDE:]
    for k in range(1, count):
        four = four + got[k, :, WIDE:]
    held4[:, 0 : WIDE // 2] = four[0:4]
    held4[:, WIDE // 2 :] = four[4:8]
    lane = lane_id((4, LANES))
    for t in range(TILES):
        at = lambda r: pl.ds(4 * r, 4)
        p, q, s, r = [beyond[at(c), tile(t)] for c in range(4)]
        rows = [cells[at(c), tile(t)] for c in range(4)]
        rows = interleave(*lift(rows, (p, q), (s, r), first, last, mix))
        for f in range(4):
            v = None
            for r in range(4):
                moved = pltpu.roll(rows[r], (r - f) % LANES, 1) if r != f else rows[r]
                v = jnp.where(lane % 4 == r, moved, v) if r else moved
            turned3[at(f), tile(t)] = v
        v = held4[:, tile(t)]
        for f in range(8):
            turned4[at(f), tile(t)] = pltpu.roll(v, LANES - f, 1) if f else v
    count = pay.shape[0]
    parts = [pl.ds(0, WIDE), pl.ds(WIDE, LANES)]
    sends = [pltpu.make_async_copy(pay.at[:, :, p], result.at[:, :, p], sem.at[k]) for k, p in enumerate(parts)]
    three = product(w3[...], turned3[...])
    four = product(w4[...], turned4[...])
    for to in range(count):
        pay[to, :, 0:WIDE] = three[to * 4 : to * 4 + 4]
    sends[0].start()
    lane = lane_id((count, LANES))
    for t in range(TILES // 2):
        v = four[0:count, tile(t)]
        for k in range(1, 8):
            w = four[k % 4 * count : (k % 4 + 1) * count, tile(t + k // 4 * (TILES // 2))]
            v = jnp.where(lane % 8 == k, pltpu.roll(w, k, 1), v)
        pay[:, t, WIDE:] = v
    sends[1].start()
    for send in sends:
        send.wait()


def along_z(one_s, one_d, two, got_e, got_o, result, fourth, out, fine, spread, sem):
    me = lax.axis_index("gz")
    flip, side = me % 2 == 1, lane_id((8, LANES)) % 2
    first = side == jnp.where(me == 0, 0, 2)
    last = side == jnp.where(me == lax.axis_size("gz") - 1, 1, 2)

    def stack(t):
        lanes = tile_lanes(t)
        e = [got_e[c, :, lanes] for c in range(6)]
        o = [got_o[c, :, lanes] for c in range(6)]
        left = [unpack_right(mix(flip, e[c], o[c])) for c in range(6)]
        right = [unpack_left(mix(flip, o[c], e[c])) for c in range(6)]
        for half in range(2):
            lifted = []
            for k, source in enumerate((one_s, one_d)):
                rows = [source[t, pl.ds(z * 16 + half * 8, 8), :] for z in range(8)]
                ends = beyond_halves(left[2 * k + half], right[2 * k + half], *edges(rows))
                lifted.append(interleave(*lift(rows, *ends, first, last, mix)))
            near, far = separate(*lifted, 1)
            for z in range(8):
                out[z, pl.ds(half * 8, 8), lanes] = near[z]
                out[z + 8, pl.ds(half * 8, 8), lanes] = far[z]
        rows = [two[t, pl.ds(z * 8, 8), :] for z in range(8)]
        to_right, to_left = edges(rows)
        rows, _ = lift(rows, *beyond_halves(left[4], right[4], to_right, to_left), first, last, mix)
        left2, right2 = add_pairs(left[5], own_left(to_left)), add_pairs(right[5], own_right(to_right))
        ends = beyond_halves(left2, right2, *edges(rows))
        for z, v in enumerate(interleave(*lift(rows, *ends, first, last, mix))):
            fine[pl.ds(z * 8, 8), lanes] = v

    times(TILES, stack, TILES)
    sends = {z: pltpu.make_async_copy(out.at[z], result.at[z], sem.at[z]) for z in range(16) if z % 4}
    for z in range(1, 16, 2):
        sends[z].start()
    row = lax.broadcasted_iota(jnp.int32, (16, LANES), 0)
    here = (row % 2 == 0) & in_even((16, LANES))
    for i in (1, 3, 0, 2):
        v = lift_runs(tiles_of(fine, pl.ds(i * 8, 8)), 2)
        for z in (i, i + 4):
            for t in range(TILES):
                spread[t, pl.ds(z * 16, 8, stride=2), :] = v[t] if z == i else back(v[t])
                w = jnp.where(here, spread[t, pl.ds(z * 16, 16), :], out[2 * z, :, tile(t)])
                if z % 2:
                    out[2 * z, :, tile(t)] = w
                else:
                    fourth[z // 2, :, tile(t)] = w
            if z % 2:
                sends[2 * z].start()
    for send in sends.values():
        send.wait()


def join(got, fourth, base, result, planes, spread, sem):
    total = got[0]
    for k in range(1, got.shape[0]):
        total = total + got[k]
    three = lift_runs([total[:, tile(t)] for t in range(TILES)], 4)
    four = [total[t : t + 1, WIDE:] for t in range(TILES // 2)]
    four = lift_runs(four + [pltpu.roll(x, LANES - 4, 1) for x in four], 8)
    lane = lane_id((4, LANES))
    row = lax.broadcasted_iota(jnp.int32, (4, LANES), 0)
    for t in range(TILES):
        for r in range(4):
            v = pltpu.roll(three[t], LANES - r, 1) if r else three[t]
            for k in range(r // 2, 4, 2) if r % 2 == 0 else ():
                w = pltpu.roll(four[t], LANES - k, 1) if k else four[t]
                v = jnp.where((lane % 8 == 0) & (row == 2 * (k // 2)), jnp.broadcast_to(w, v.shape), v)
            spread[t, pl.ds(4 * r, 4, stride=16), :] = v
    row = lax.broadcasted_iota(jnp.int32, (16, LANES), 0)
    here = (row % 4 == 0) & (lane_id((16, LANES)) % 4 == 0)
    sends = [pltpu.make_async_copy(planes.at[i], result.at[4 * i], sem.at[i]) for i in range(4)]
    for i in (1, 3, 0, 2):
        for t in range(TILES):
            planes[i, :, tile(t)] = jnp.where(here, spread[t, pl.ds(i * 16, 16), :], fourth[i, :, tile(t)])
        sends[i].start()
    for send in sends:
        send.wait()


def deep_levels(n):
    fixed = lambda c, a, b: a if c else b
    level = lambda rows: lift(rows, (0.0, 0.0), (0.0, 0.0), True, True, fixed)
    cells = level(level(list(np.eye(n)))[0])[0]
    smooth, detail = level(cells)
    return cells, np.stack(interleave(smooth, detail)), np.stack(interleave(*level(smooth)))


def weights_y(devices):
    cells, _, four = deep_levels(16 * devices)
    w3 = np.zeros((devices, 48, 4, 16), np.float64)
    w4 = np.zeros((devices, devices, 2, 2, 2, 16), np.float64)
    for a in range(devices):
        mine = slice(16 * a, 16 * a + 16)
        for row, side, b in ((0, 0, -1), (8, 1, 1), (16, 0, 0), (24, 0, 1), (32, 1, 0), (40, 1, -1)):
            if 0 <= a + b < devices:
                pair = edges(cells[4 * (a + b) : 4 * (a + b) + 4])[side]
                for c in range(2):
                    for z in range(4):
                        w3[a, row + 4 * c + z, z] = pair[c][mine]
        for z in range(2):
            w4[a, :, :, z, z] = four[:, mine].reshape(devices, 2, 16)
    return (
        split_left(w3.reshape(devices, 48, 64).astype(np.float32)),
        split_left(w4.reshape(devices, 4 * devices, 32).astype(np.float32)),
    )


def weights_z(devices):
    _, three, four = deep_levels(16 * devices)
    w3 = np.zeros((devices, devices, 4, 4, 4), np.float64)
    w4 = np.zeros((devices, 2, 2, devices, 8, 2, 2), np.float64)
    for a in range(devices):
        for f in range(8):
            for zz in range(4):
                if f < 4:
                    z = 16 * a + zz + 4 * (f // 2) + 8 * (f % 2)
                    w3[a, :, :, f, zz] = three[:, z].reshape(devices, 4)
                if zz < 2:
                    z = 16 * a + zz + 2 * (f // 4) + 4 * (f // 2 % 2) + 8 * (f % 2)
                    for o in range(2):
                        w4[a, :, o, :, f, o, zz] = four[:, z].reshape(devices, 2).T
    return (
        split_left(w3.reshape(devices, 4 * devices, 16).astype(np.float32)),
        split_left(w4.reshape(devices, 4 * devices, 32).astype(np.float32)),
    )


def swap(values, axis, start):
    devices = lax.axis_size(axis)
    pairs = []
    for i in range(start, devices - 1, 2):
        pairs += [(i, i + 1), (i + 1, i)]
    return lax.ppermute(values, axis, pairs)


def f32(*shape):
    return jax.ShapeDtypeStruct(shape, jnp.float32)


def bf16(*shape):
    return jax.ShapeDtypeStruct(shape, jnp.bfloat16)


def call(body, out, scratch=(), cost=4 << 20, **more):
    return pl.pallas_call(
        body,
        out_shape=out,
        scratch_shapes=list(scratch),
        cost_estimate=pl.CostEstimate(flops=cost * 10, bytes_accessed=4 << 20, transcendentals=0),
        compiler_params=pltpu.CompilerParams(vmem_limit_bytes=24 * 1024 * 1024),
        **more,
    )


def per_device(density):
    planes, rows, cells = density.shape
    ny, nz = lax.axis_size("gy"), lax.axis_size("gz")
    vmem = lambda *shape: pltpu.VMEM(shape, jnp.float32)
    sems = lambda count: pltpu.SemaphoreType.DMA((count,))
    far, here = pl.BlockSpec(memory_space=pltpu.HBM), pl.BlockSpec(memory_space=pltpu.VMEM)
    stay = lambda v: pltpu.with_memory_space_constraint(jnp.asarray(v), pltpu.HBM)
    tiled = f32(TILES, planes * rows // 2, LANES)
    payload = f32(6, 8, cells)
    pay = (ny, 8, cells * 3 // 2)
    smooth, detail, pay_e, pay_o, own, pay, z3, z4 = call(
        along_x,
        [tiled, tiled, payload, payload, f32(16, cells), f32(*pay), bf16(4 * nz, 6 * 16), bf16(4 * nz, 6 * 32)],
        [
            vmem(planes * rows, cells),
            vmem(64, cells),
            vmem(32, cells),
            pltpu.VMEM((48, 6 * 64), jnp.bfloat16),
            pltpu.VMEM((4 * ny, 6 * 32), jnp.bfloat16),
            vmem(*pay),
            sems(8),
            sems(6),
        ],
        in_specs=[far] * 5,
        out_specs=[here] * 5 + [far, here, here],
    )(*[stay(w) for w in weights_y(ny) + weights_z(nz)], stay(density.reshape(planes * rows, cells)))
    got_e, got_o = swap(pay_e, "gy", 0), swap(pay_o, "gy", 1)
    got = lax.all_to_all(pay, "gy", 0, 0, tiled=True)

    one_s, one_d, two, pay_e, pay_o, third = call(
        along_y,
        [tiled, tiled, f32(TILES, planes * rows // 4, LANES), payload, payload, f32(16, cells)],
        [vmem(32, cells)],
        cost=400 << 20,
        input_output_aliases={0: 0, 1: 1},
    )(smooth, detail, got_e, got_o)
    got_e, got_o = swap(pay_e, "gz", 0), swap(pay_o, "gz", 1)
    pay = (nz, 4, cells + LANES)
    pay = call(
        thin_z,
        f32(*pay),
        [vmem(*pay), vmem(16, cells), vmem(4, cells), vmem(16, cells), vmem(32, cells), sems(2)],
        cost=40 << 20,
        out_specs=far,
    )(z3, z4, third, own, got)
    got = lax.all_to_all(pay, "gz", 0, 0, tiled=True)

    base, fourth = call(
        along_z,
        [f32(planes, rows, cells), f32(planes // 4, rows, cells)],
        [vmem(planes, rows, cells), vmem(32, cells), vmem(TILES, 128, LANES), sems(planes)],
        cost=400 << 20,
        out_specs=[far, here],
    )(one_s, one_d, two, got_e, got_o)
    return call(
        join,
        f32(planes, rows, cells),
        [vmem(planes // 4, rows, cells), vmem(TILES, 64, LANES), sems(4)],
        in_specs=[here, here, far],
        out_specs=far,
        input_output_aliases={2: 0},
    )(got, fourth, stay(base))


def solution(mesh):
    return jax.shard_map(
        per_device, mesh=mesh, in_specs=(P("gz", "gy", None),), out_specs=P("gz", "gy", None), check_vma=False
    )
```

```python
import functools

import jax
import jax.numpy as jnp
import ml_dtypes
import numpy as np
from jax import lax
from jax.experimental import pallas as pl
from jax.experimental.pallas import tpu as pltpu
from jax.sharding import PartitionSpec as P

A1 = -1.586134342059924
B1 = -0.052980118572961
A2 = 0.882911075530934
B2 = 0.443506852043971
GAIN = 1.230174104914001

WIDE = 1024
LANES = 128
TILES = WIDE // LANES


def lift(rows, left, right, first, last, choose):
    p, q = left
    s_next, r = right
    smooth, detail = rows[0::2], rows[1::2]
    m = len(smooth)
    s_next = choose(last, smooth[-1], s_next)
    d1 = [detail[i] + A1 * (smooth[i] + (smooth[i + 1] if i + 1 < m else s_next)) for i in range(m)]
    d1_before = choose(first, d1[0], p + A1 * smooth[0])
    s1 = [smooth[i] + B1 * ((d1[i - 1] if i else d1_before) + d1[i]) for i in range(m)]
    s1_after = choose(last, s1[-1], r + B1 * d1[-1])
    d2 = [d1[i] + A2 * (s1[i] + (s1[i + 1] if i + 1 < m else s1_after)) for i in range(m)]
    d2_before = choose(first, d2[0], d1_before + A2 * (q + B1 * d1_before + s1[0]))
    s2 = [s1[i] + B2 * ((d2[i - 1] if i else d2_before) + d2[i]) for i in range(m)]
    return [v * (1.0 / GAIN) for v in s2], [v * (GAIN / 2.0) for v in d2]


def lift_alone(rows):
    zero = jnp.zeros_like(rows[0])
    return lift(rows, (zero, zero), (zero, zero), False, False, lambda c, a, b: a if c else b)[0]


def edges(rows):
    s, d = rows[0::2], rows[1::2]
    to_right = (d[-1] + A1 * s[-1], s[-1] + B1 * (d[-2] + A1 * (s[-2] + s[-1])))
    to_left = (s[0], s[0] + B1 * (d[0] + A1 * (s[0] + s[1])))
    return to_right, to_left


def own_left(to_left):
    s, r = to_left
    c2 = (B2 * A2 * B1 * A1 / GAIN) * s
    c1 = ((B1 * A1 + B2 * A1 + 3 * B2 * A2 * B1 * A1) / GAIN) * s + (B2 * A2 / GAIN) * r
    return c1 + A1 * c2, (1 + B1 * A1) * c2


def own_right(to_right):
    p, q = to_right
    c0 = ((B1 + B2 + 3 * B2 * A2 * B1) / GAIN) * p + (B2 * A2 / GAIN) * q
    c1 = (B2 * A2 * B1 / GAIN) * p
    return c0, c0 + B1 * (c1 + A1 * c0)


def add_pairs(a, b):
    return a[0] + b[0], a[1] + b[1]


def mix(flag, a, b):
    return jnp.where(flag, a, b)


def interleave(smooth, detail):
    return [v for pair in zip(smooth, detail) for v in pair]


def filters():
    fixed = lambda c, a, b: a if c else b
    smooth, detail = lift(list(np.eye(32)), (0.0, 0.0), (0.0, 0.0), True, True, fixed)
    return [float(v) for v in smooth[8][16:21]], [float(v) for v in detail[8][17:21]]


def moved(tiles, step):
    if step == 0:
        return list(tiles)
    lane, count = lane_id(tiles[0].shape), len(tiles)
    r = [pltpu.roll(x, -step % LANES, 1) for x in tiles]
    if step > 0:
        return [jnp.where(lane < LANES - step, r[t], r[t + 1]) if t + 1 < count else r[t] for t in range(count)]
    return [jnp.where(lane >= -step, r[t], r[t - 1]) if t else r[t] for t in range(count)]


def lift_runs(v, stride):
    run = lane_id(v[0].shape) // stride
    ends = LANES // stride - 1
    at = {k: moved(v, k * stride) for k in range(-4, 5)}
    for k in range(1, 5):
        for j in range(k):
            at[-k][0] = jnp.where(run == j, at[k - 2 * j][0], at[-k][0])
    for k in range(1, 5):
        for j in range(k):
            at[k][-1] = jnp.where(run == ends - j, at[2 * j - k][-1], at[k][-1])
    smooth, detail = filters()
    weight = [jnp.where(run % 2 == 0, a, b) for a, b in zip(smooth, detail + [0.0])]
    out = [weight[0] * x for x in v]
    for k in range(1, 5):
        out = [x + weight[k] * (y + z) for x, y, z in zip(out, at[-k], at[k])]
    return out


def split_left(w):
    parts = []
    for _ in range(3):
        parts.append((w - sum(p.astype(np.float32) for p in parts)).astype(ml_dtypes.bfloat16))
    one, two, three = parts
    return np.concatenate([one, one, two, one, two, three], axis=-1)


def product(left, x):
    one = x.astype(jnp.bfloat16)
    rest = x - one.astype(jnp.float32)
    two = rest.astype(jnp.bfloat16)
    three = (rest - two.astype(jnp.float32)).astype(jnp.bfloat16)
    right = jnp.concatenate([one, two, one, three, two, one], axis=0)
    return jnp.dot(left, right, preferred_element_type=jnp.float32)


def lane_id(shape):
    return lax.broadcasted_iota(jnp.int32, shape, len(shape) - 1)


def in_even(shape):
    return lane_id(shape) % 2 == 0


def back(v):
    return pltpu.roll(v, LANES - 1, 1)


def on(v):
    return pltpu.roll(v, 1, 1)


def pack_right(p, q):
    return jnp.where(in_even(p.shape), back(q), p)


def unpack_right(v):
    return back(v), v


def pack_left(s, r):
    return jnp.where(in_even(s.shape), s, on(r))


def unpack_left(v):
    return on(v), v


def beyond_halves(left, right, to_right, to_left):
    even = in_even(to_right[0].shape)
    return (
        tuple(jnp.where(even, x, on(y)) for x, y in zip(left, to_right)),
        tuple(jnp.where(even, back(y), x) for x, y in zip(right, to_left)),
    )


def tile(t):
    return slice(t * LANES, (t + 1) * LANES)


def times(count, body, unroll=1):
    if unroll == count:
        for i in range(count):
            body(i)
        return

    def step(i, carry):
        body(i)
        return carry

    lax.fori_loop(0, count, step, 0, unroll=unroll)


def tile_lanes(t):
    return pl.ds(t * LANES if isinstance(t, int) else pl.multiple_of(t * LANES, LANES), LANES)


def lift_two(a, b, phase):
    lane = lane_id((a[0].shape[0], LANES))
    here = lane % (2 * phase) < phase
    count, reach = len(a), 2 * phase
    other = jnp.where(here, lane + phase, lane - phase)
    m = [jnp.take_along_axis(jnp.where(here, y, x), other, axis=1, mode="promise_in_bounds") for x, y in zip(a, b)]
    s = [jnp.where(here, x, y) for x, y in zip(a, m)]
    d = [jnp.where(here, y, x) for x, y in zip(b, m)]

    def ahead(x):
        r = [pltpu.roll(w, LANES - reach, 1) for w in x]
        return [jnp.where(lane < LANES - reach, r[t], r[t + 1] if t + 1 < count else x[t]) for t in range(count)]

    def behind(x):
        r = [pltpu.roll(w, reach, 1) for w in x]
        return [jnp.where(lane >= reach, r[t], r[t - 1] if t else x[t]) for t in range(count)]

    d = [x + A1 * (y + z) for x, y, z in zip(d, s, ahead(s))]
    s = [x + B1 * (y + z) for x, y, z in zip(s, d, behind(d))]
    d = [x + A2 * (y + z) for x, y, z in zip(d, s, ahead(s))]
    s = [(x + B2 * (y + z)) * (1.0 / GAIN) for x, y, z in zip(s, d, behind(d))]
    return s, [x * (GAIN / 2.0) for x in d]


def separate(s, d, phase):
    lane = lane_id(s[0].shape)
    here = lane % (2 * phase) < phase
    other = jnp.where(here, lane + phase, lane - phase)
    m = [jnp.take_along_axis(jnp.where(here, y, x), other, axis=1, mode="promise_in_bounds") for x, y in zip(s, d)]
    return [jnp.where(here, x, y) for x, y in zip(s, m)], [jnp.where(here, y, x) for x, y in zip(d, m)]


def tiles_of(ref, at):
    v = ref[at, :]
    return [v[:, tile(t)] for t in range(TILES)]


def put_tiles(ref, at, parts):
    for t, v in enumerate(parts):
        ref[at, tile(t)] = v


def along_x(
    y3, y4, z3, z4, density, smooth, detail, pay_e, pay_o, own, result, next3, next4, x, e2, e3, w3, w4, pay, load_sem, sem
):
    me, mz = lax.axis_index("gy"), lax.axis_index("gz")

    def load(k):
        at = pl.ds(pl.multiple_of(k * 64, 64), 64)
        return pltpu.make_async_copy(density.at[at], x.at[at], load_sem.at[k])

    for k in range(2):
        load(k).start()
        load(k + 2).start()
    hints = [
        pltpu.make_async_copy(y3.at[me], w3, sem.at[0]),
        pltpu.make_async_copy(y4.at[me], w4, sem.at[1]),
        pltpu.make_async_copy(z3.at[mz], next3, sem.at[2]),
        pltpu.make_async_copy(z4.at[mz], next4, sem.at[3]),
    ]
    for hint in hints:
        hint.start()

    def plane(i):
        z, y = i // 2, i % 2
        at = pl.multiple_of(z * 16 + y * 8, 8)
        far = pl.multiple_of(z * 16 + y * 8 + 128, 8)
        s, d = lift_two(tiles_of(x, pl.ds(at, 8)), tiles_of(x, pl.ds(far, 8)), 1)
        for t in range(TILES):
            smooth[t, pl.ds(at, 8), :] = s[t]
            detail[t, pl.ds(at, 8), :] = d[t]

    def group(k):
        load(k).wait()
        load(k + 2).wait()
        for i in range(8):
            plane(8 * k + i)

    times(2, group)
    for hint in hints:
        hint.wait()

    def second(i):
        at = pl.multiple_of(i * 8, 8)
        near, far = [[smooth[t, pl.ds(at + k, 8), :] for t in range(TILES)] for k in (0, 64)]
        s, _ = lift_two(near, far, 2)
        put_tiles(e2, pl.ds(at, 8), s)

    times(8, second, 8)

    def third(i):
        at = pl.multiple_of(i * 8, 8)
        s, _ = lift_two(tiles_of(e2, pl.ds(at, 8)), tiles_of(e2, pl.ds(at + 32, 8)), 4)
        put_tiles(e3, pl.ds(at, 8), s)

    times(4, third, 4)
    three = product(w3[...], e2[...])
    four = product(w4[...], e3[...])
    own[...] = three[0:16]
    for to in range(pay.shape[0]):
        right = mix(to == me + 1, three[16:24], three[24:32])
        left = mix(to == me - 1, three[32:40], three[40:48])
        pay[to, :, 0:WIDE] = mix(to > me, right, left)
    parts = [pl.ds(0, WIDE), pl.ds(WIDE, WIDE // 2)]
    sends = [pltpu.make_async_copy(pay.at[:, :, p], result.at[:, :, p], sem.at[4 + k]) for k, p in enumerate(parts)]
    sends[0].start(priority=1)
    for to in range(pay.shape[0]):
        pay[to, 0:4, WIDE:] = four[to * 4 : to * 4 + 4, : WIDE // 2]
        pay[to, 4:8, WIDE:] = four[to * 4 : to * 4 + 4, WIDE // 2 :]
    sends[1].start(priority=1)
    flip = me % 2 == 1

    def column(t):
        lanes = tile_lanes(t)
        rows = [smooth[t, pl.ds(y, 8, stride=16), :] for y in range(16)]
        parts = [edges(rows), edges(lift_alone(rows))]
        parts.append(edges([detail[t, pl.ds(y, 8, stride=16), :] for y in range(16)]))
        for c in range(6):
            right, left = [parts[c // 2][side][c % 2] for side in range(2)]
            pay_e[c, :, lanes] = mix(flip, left, right)
            pay_o[c, :, lanes] = mix(flip, right, left)

    times(TILES, column, 4)
    for send in sends:
        send.wait()


def along_y(smooth, detail, got_e, got_o, one_s, one_d, two, pay_e, pay_o, cells, thick):
    me = lax.axis_index("gy")
    first, last, flip = me == 0, me == lax.axis_size("gy") - 1, me % 2 == 1

    def column(t):
        lanes = tile_lanes(t)
        e = [got_e[c, :, lanes] for c in range(6)]
        o = [got_o[c, :, lanes] for c in range(6)]
        left = [mix(flip, e[c], o[c]) for c in range(6)]
        right = [mix(flip, o[c], e[c]) for c in range(6)]
        for k, (source, to) in enumerate(((detail, one_d), (smooth, one_s))):
            rows = [source[t, pl.ds(y, 8, stride=16), :] for y in range(16)]
            at = slice(0, 2) if k else slice(4, 6)
            low, high = lift(rows, left[at], right[at], first, last, mix)
            for y, v in enumerate(interleave(low, high)):
                to[t, pl.ds(y, 8, stride=16), :] = v
        to_right, to_left = edges(rows)
        left2, right2 = add_pairs(left[2:4], own_left(to_left)), add_pairs(right[2:4], own_right(to_right))
        low, high = lift(low, left2, right2, first, last, mix)
        for y, v in enumerate(interleave(low, high)):
            two[t, pl.ds(y, 8, stride=8), :] = v
        for r, v in enumerate(low):
            thick[pl.ds(4 * r, 4), lanes] = v[0:4]
            thick[pl.ds(16 + 4 * r, 4), lanes] = v[4:8]

    times(TILES, column, TILES)
    flip = lax.axis_index("gz") % 2 == 1

    def stack(t):
        lanes = tile_lanes(t)
        going_right, going_left = [], []

        def add(rows):
            to_right, to_left = edges(rows)
            going_right.append(pack_right(*to_right))
            going_left.append(pack_left(*to_left))
            return to_right, to_left

        for source in (one_s, one_d):
            for half in range(2):
                add([source[t, pl.ds(z * 16 + half * 8, 8), :] for z in range(8)])
        rows = [two[t, pl.ds(z * 8, 8), :] for z in range(8)]
        nothing = jnp.zeros_like(rows[0])
        left, right = beyond_halves((nothing, nothing), (nothing, nothing), *add(rows))
        add(lift(rows, left, right, False, False, lambda c, a, b: b)[0])
        for c in range(6):
            pay_e[c, :, lanes] = mix(flip, going_left[c], going_right[c])
            pay_o[c, :, lanes] = mix(flip, going_right[c], going_left[c])

    times(TILES, stack, TILES)
    for i in range(2):
        s, _ = lift_two(tiles_of(thick, pl.ds(8 * i, 8)), tiles_of(thick, pl.ds(16 + 8 * i, 8)), 2)
        put_tiles(cells, pl.ds(8 * i, 8), s)


def thin_z(w3, w4, cells, own, got, result, pay, beyond, held4, turned3, turned4, sem):
    me, count = lax.axis_index("gy"), got.shape[0]
    first, last = me == 0, me == count - 1
    near = lambda k: got[jnp.clip(me + k, 0, count - 1), :, 0:WIDE]
    beyond[0:8] = own[0:8] + (mix(me >= 1, near(-1), 0.0) + mix(me >= 2, near(-2), 0.0))
    beyond[8:16] = own[8:16] + (mix(me < count - 1, near(1), 0.0) + mix(me < count - 2, near(2), 0.0))
    four = got[0, :, WIDE:]
    for k in range(1, count):
        four = four + got[k, :, WIDE:]
    held4[:, 0 : WIDE // 2] = four[0:4]
    held4[:, WIDE // 2 :] = four[4:8]
    lane = lane_id((4, LANES))
    for t in range(TILES):
        at = lambda r: pl.ds(4 * r, 4)
        p, q, s, r = [beyond[at(c), tile(t)] for c in range(4)]
        rows = [cells[at(c), tile(t)] for c in range(4)]
        rows = interleave(*lift(rows, (p, q), (s, r), first, last, mix))
        for f in range(4):
            v = None
            for r in range(4):
                moved = pltpu.roll(rows[r], (r - f) % LANES, 1) if r != f else rows[r]
                v = jnp.where(lane % 4 == r, moved, v) if r else moved
            turned3[at(f), tile(t)] = v
        v = held4[:, tile(t)]
        for f in range(8):
            turned4[at(f), tile(t)] = pltpu.roll(v, LANES - f, 1) if f else v
    count = pay.shape[0]
    parts = [pl.ds(0, WIDE), pl.ds(WIDE, LANES)]
    sends = [pltpu.make_async_copy(pay.at[:, :, p], result.at[:, :, p], sem.at[k]) for k, p in enumerate(parts)]
    three = product(w3[...], turned3[...])
    four = product(w4[...], turned4[...])
    for to in range(count):
        pay[to, :, 0:WIDE] = three[to * 4 : to * 4 + 4]
    sends[0].start(priority=1)
    lane = lane_id((count, LANES))
    for t in range(TILES // 2):
        v = four[0:count, tile(t)]
        for k in range(1, 8):
            w = four[k % 4 * count : (k % 4 + 1) * count, tile(t + k // 4 * (TILES // 2))]
            v = jnp.where(lane % 8 == k, pltpu.roll(w, k, 1), v)
        pay[:, t, WIDE:] = v
    sends[1].start(priority=1)
    for send in sends:
        send.wait()


def along_z(one_s, one_d, two, got_e, got_o, result, fourth, out, fine, spread, sem):
    me = lax.axis_index("gz")
    flip, side = me % 2 == 1, lane_id((8, LANES)) % 2
    first = side == jnp.where(me == 0, 0, 2)
    last = side == jnp.where(me == lax.axis_size("gz") - 1, 1, 2)

    def stack(t):
        lanes = tile_lanes(t)
        e = [got_e[c, :, lanes] for c in range(6)]
        o = [got_o[c, :, lanes] for c in range(6)]
        left = [unpack_right(mix(flip, e[c], o[c])) for c in range(6)]
        right = [unpack_left(mix(flip, o[c], e[c])) for c in range(6)]
        for half in range(2):
            lifted = []
            for k, source in enumerate((one_s, one_d)):
                rows = [source[t, pl.ds(z * 16 + half * 8, 8), :] for z in range(8)]
                ends = beyond_halves(left[2 * k + half], right[2 * k + half], *edges(rows))
                lifted.append(interleave(*lift(rows, *ends, first, last, mix)))
            near, far = separate(*lifted, 1)
            for z in range(8):
                out[z, pl.ds(half * 8, 8), lanes] = near[z]
                out[z + 8, pl.ds(half * 8, 8), lanes] = far[z]
        rows = [two[t, pl.ds(z * 8, 8), :] for z in range(8)]
        to_right, to_left = edges(rows)
        rows, _ = lift(rows, *beyond_halves(left[4], right[4], to_right, to_left), first, last, mix)
        left2, right2 = add_pairs(left[5], own_left(to_left)), add_pairs(right[5], own_right(to_right))
        ends = beyond_halves(left2, right2, *edges(rows))
        for z, v in enumerate(interleave(*lift(rows, *ends, first, last, mix))):
            fine[pl.ds(z * 8, 8), lanes] = v

    times(TILES, stack, TILES)
    sends = {z: pltpu.make_async_copy(out.at[z], result.at[z], sem.at[z]) for z in range(16) if z % 4}
    for z in range(1, 16, 2):
        sends[z].start()
    row = lax.broadcasted_iota(jnp.int32, (16, LANES), 0)
    here = (row % 2 == 0) & in_even((16, LANES))
    for i in (1, 3, 0, 2):
        v = lift_runs(tiles_of(fine, pl.ds(i * 8, 8)), 2)
        for z in (i, i + 4):
            for t in range(TILES):
                spread[t, pl.ds(z * 16, 8, stride=2), :] = v[t] if z == i else back(v[t])
                w = jnp.where(here, spread[t, pl.ds(z * 16, 16), :], out[2 * z, :, tile(t)])
                if z % 2:
                    out[2 * z, :, tile(t)] = w
                else:
                    fourth[z // 2, :, tile(t)] = w
            if z % 2:
                sends[2 * z].start()
    for send in sends.values():
        send.wait()


def join(got, fourth, base, result, planes, spread, sem):
    total = got[0]
    for k in range(1, got.shape[0]):
        total = total + got[k]
    three = lift_runs([total[:, tile(t)] for t in range(TILES)], 4)
    four = [total[t : t + 1, WIDE:] for t in range(TILES // 2)]
    four = lift_runs(four + [pltpu.roll(x, LANES - 4, 1) for x in four], 8)
    lane = lane_id((4, LANES))
    row = lax.broadcasted_iota(jnp.int32, (4, LANES), 0)
    for t in range(TILES):
        for r in range(4):
            v = pltpu.roll(three[t], LANES - r, 1) if r else three[t]
            for k in range(r // 2, 4, 2) if r % 2 == 0 else ():
                w = pltpu.roll(four[t], LANES - k, 1) if k else four[t]
                v = jnp.where((lane % 8 == 0) & (row == 2 * (k // 2)), jnp.broadcast_to(w, v.shape), v)
            spread[t, pl.ds(4 * r, 4, stride=16), :] = v
    row = lax.broadcasted_iota(jnp.int32, (16, LANES), 0)
    here = (row % 4 == 0) & (lane_id((16, LANES)) % 4 == 0)
    sends = [pltpu.make_async_copy(planes.at[i], result.at[4 * i], sem.at[i]) for i in range(4)]
    for i in (1, 3, 0, 2):
        for t in range(TILES):
            planes[i, :, tile(t)] = jnp.where(here, spread[t, pl.ds(i * 16, 16), :], fourth[i, :, tile(t)])
        sends[i].start()
    for send in sends:
        send.wait()


def deep_levels(n):
    fixed = lambda c, a, b: a if c else b
    level = lambda rows: lift(rows, (0.0, 0.0), (0.0, 0.0), True, True, fixed)
    cells = level(level(list(np.eye(n)))[0])[0]
    smooth, detail = level(cells)
    return cells, np.stack(interleave(smooth, detail)), np.stack(interleave(*level(smooth)))


def weights_y(devices):
    cells, _, four = deep_levels(16 * devices)
    w3 = np.zeros((devices, 48, 4, 16), np.float64)
    w4 = np.zeros((devices, devices, 2, 2, 2, 16), np.float64)
    for a in range(devices):
        mine = slice(16 * a, 16 * a + 16)
        for row, side, b in ((0, 0, -1), (8, 1, 1), (16, 0, 0), (24, 0, 1), (32, 1, 0), (40, 1, -1)):
            if 0 <= a + b < devices:
                pair = edges(cells[4 * (a + b) : 4 * (a + b) + 4])[side]
                for c in range(2):
                    for z in range(4):
                        w3[a, row + 4 * c + z, z] = pair[c][mine]
        for z in range(2):
            w4[a, :, :, z, z] = four[:, mine].reshape(devices, 2, 16)
    return (
        split_left(w3.reshape(devices, 48, 64).astype(np.float32)),
        split_left(w4.reshape(devices, 4 * devices, 32).astype(np.float32)),
    )


def weights_z(devices):
    _, three, four = deep_levels(16 * devices)
    w3 = np.zeros((devices, devices, 4, 4, 4), np.float64)
    w4 = np.zeros((devices, 2, 2, devices, 8, 2, 2), np.float64)
    for a in range(devices):
        for f in range(8):
            for zz in range(4):
                if f < 4:
                    z = 16 * a + zz + 4 * (f // 2) + 8 * (f % 2)
                    w3[a, :, :, f, zz] = three[:, z].reshape(devices, 4)
                if zz < 2:
                    z = 16 * a + zz + 2 * (f // 4) + 4 * (f // 2 % 2) + 8 * (f % 2)
                    for o in range(2):
                        w4[a, :, o, :, f, o, zz] = four[:, z].reshape(devices, 2).T
    return (
        split_left(w3.reshape(devices, 4 * devices, 16).astype(np.float32)),
        split_left(w4.reshape(devices, 4 * devices, 32).astype(np.float32)),
    )


def swap(values, axis, start):
    devices = lax.axis_size(axis)
    pairs = []
    for i in range(start, devices - 1, 2):
        pairs += [(i, i + 1), (i + 1, i)]
    return lax.ppermute(values, axis, pairs)


def f32(*shape):
    return jax.ShapeDtypeStruct(shape, jnp.float32)


def bf16(*shape):
    return jax.ShapeDtypeStruct(shape, jnp.bfloat16)


def call(body, out, scratch=(), cost=4 << 20, **more):
    return pl.pallas_call(
        body,
        out_shape=out,
        scratch_shapes=list(scratch),
        cost_estimate=pl.CostEstimate(flops=cost * 10, bytes_accessed=4 << 20, transcendentals=0),
        compiler_params=pltpu.CompilerParams(vmem_limit_bytes=24 * 1024 * 1024),
        **more,
    )


def per_device(density):
    planes, rows, cells = density.shape
    ny, nz = lax.axis_size("gy"), lax.axis_size("gz")
    vmem = lambda *shape: pltpu.VMEM(shape, jnp.float32)
    sems = lambda count: pltpu.SemaphoreType.DMA((count,))
    far, here = pl.BlockSpec(memory_space=pltpu.HBM), pl.BlockSpec(memory_space=pltpu.VMEM)
    stay = lambda v: pltpu.with_memory_space_constraint(jnp.asarray(v), pltpu.HBM)
    tiled = f32(TILES, planes * rows // 2, LANES)
    payload = f32(6, 8, cells)
    pay = (ny, 8, cells * 3 // 2)
    smooth, detail, pay_e, pay_o, own, pay, z3, z4 = call(
        along_x,
        [tiled, tiled, payload, payload, f32(16, cells), f32(*pay), bf16(4 * nz, 6 * 16), bf16(4 * nz, 6 * 32)],
        [
            vmem(planes * rows, cells),
            vmem(64, cells),
            vmem(32, cells),
            pltpu.VMEM((48, 6 * 64), jnp.bfloat16),
            pltpu.VMEM((4 * ny, 6 * 32), jnp.bfloat16),
            vmem(*pay),
            sems(4),
            sems(6),
        ],
        in_specs=[far] * 5,
        out_specs=[here] * 5 + [far, here, here],
    )(*[stay(w) for w in weights_y(ny) + weights_z(nz)], stay(density.reshape(planes * rows, cells)))
    got_e, got_o = swap(pay_e, "gy", 0), swap(pay_o, "gy", 1)
    got = lax.all_to_all(pay, "gy", 0, 0, tiled=True)

    one_s, one_d, two, pay_e, pay_o, third = call(
        along_y,
        [tiled, tiled, f32(TILES, planes * rows // 4, LANES), payload, payload, f32(16, cells)],
        [vmem(32, cells)],
        cost=400 << 20,
        input_output_aliases={0: 0, 1: 1},
    )(smooth, detail, got_e, got_o)
    got_e, got_o = swap(pay_e, "gz", 0), swap(pay_o, "gz", 1)
    pay = (nz, 4, cells + LANES)
    pay = call(
        thin_z,
        f32(*pay),
        [vmem(*pay), vmem(16, cells), vmem(4, cells), vmem(16, cells), vmem(32, cells), sems(2)],
        cost=40 << 20,
        out_specs=far,
    )(z3, z4, third, own, got)
    got = lax.all_to_all(pay, "gz", 0, 0, tiled=True)

    base, fourth = call(
        along_z,
        [f32(planes, rows, cells), f32(planes // 4, rows, cells)],
        [vmem(planes, rows, cells), vmem(32, cells), vmem(TILES, 128, LANES), sems(planes)],
        cost=400 << 20,
        out_specs=[far, here],
    )(one_s, one_d, two, got_e, got_o)
    return call(
        join,
        f32(planes, rows, cells),
        [vmem(planes // 4, rows, cells), vmem(TILES, 64, LANES), sems(4)],
        in_specs=[here, here, far],
        out_specs=far,
        input_output_aliases={2: 0},
    )(got, fourth, stay(base))


def solution(mesh):
    return jax.shard_map(
        per_device, mesh=mesh, in_specs=(P("gz", "gy", None),), out_specs=P("gz", "gy", None), check_vma=False
    )
```
